32 devices in a mesh: groups: 2 (over x), seq: 16 (over z, y, core).
Axes of the slice: x: 2, y: 2, z: 4, core: 2. Of those that a mesh axis runs over, the one named last changes fastest.
Arguments:
- queries: bfloat16 [24576, 1024], P(('groups', 'seq')), parts along dimension 0, may hold values from -4 to 4
- resp_keys: bfloat16 [24576, 128], P(('groups', 'seq')), parts along dimension 0, may hold values from -6 to 6
- resp_values: bfloat16 [24576, 128], P(('groups', 'seq')), parts along dimension 0, may hold values from -6 to 6
- out_grad: bfloat16 [24576, 1024], P(('groups', 'seq')), parts along dimension 0, may hold values from -48 to 48
- prompt_keys: bfloat16 [1024, 128], P(('groups', 'seq')), parts along dimension 0, may hold values from -7.5 to 7.5
- prompt_values: bfloat16 [1024, 128], P(('groups', 'seq')), parts along dimension 0, may hold values from -6 to 6
- slot_prompt: int32 [64], P(('groups', 'seq')), parts along dimension 0, may hold values from 0 to 1, as said below
- slot_length: int32 [64], P(('groups', 'seq')), parts along dimension 0, may hold values from 76 to 384
- slot_begin: int32 [64], P(('groups', 'seq')), parts along dimension 0, may hold values from 0 to 308, as said below
- block_prompt: int32 [32], P('groups'), parts along dimension 0, may hold values from 0 to 15, as said below
Outputs:
- query_grad: float32 [24576, 1024], P(('groups', 'seq')), parts along dimension 0
- resp_key_grad: float32 [24576, 128], P(('groups', 'seq')), parts along dimension 0
- resp_value_grad: float32 [24576, 128], P(('groups', 'seq')), parts along dimension 0
- prompt_key_grad: float32 [1024, 128], P(('groups', 'seq')), parts along dimension 0
- prompt_value_grad: float32 [1024, 128], P(('groups', 'seq')), parts along dimension 0
The draws below stay inside these ranges and needn't reach their ends.
There are 2 independent parts, one for each index of `groups`. The reference program is written for one: setup_inputs(seed, part) draws one part's arguments, and reference() takes and returns one part's arrays. A program takes and returns all parts, laid end to end along the dimension named above; each array names one. Nothing has to cross between parts.
Inputs may be any that keep to these rules, and one draw needn't show every extreme that they name: `slot_prompt`: each prompt number is named by exactly 16 slots. slot_begin + slot_length <= 384 for every slot. `block_prompt`: a permutation: each value names one piece of one prompt.
All inputs are finite; a program needn't handle non-finite values.
Results may differ from the reference program's by a relative error of at most 0.012.
The reference program's roundings to bfloat16 on the way count: a program that leaves them out, or rounds other values in their place, can miss the bound.
Values may be sent and summed in bfloat16 or wider, within the bound.
No kernel may reach another device: no remote copies, remote signals or barrier semaphores. Data moves between devices by JAX's collectives and lax.ppermute only.
A program may use at most 128 MiB of HBM per device.

```python
import jax
import jax.numpy as jnp
from jax import lax

H = 8
DH = 128
OWNERS = 8
SLOT = 384
LMIN = 76
RESPONSES = 16
TOTAL_SLOTS = 32
ROWS = 12288
PROMPT_ROWS = 512
N_SEQ = 16


def length_plan(key):
    key_len, key_one, key_two = jax.random.split(jax.random.fold_in(key, 21), 3)
    lengths = jax.random.randint(key_len, (TOTAL_SLOTS,), LMIN, SLOT + 1)
    first = jax.random.randint(key_one, (), 0, TOTAL_SLOTS)
    second = (first + 1 + jax.random.randint(key_two, (), 0, TOTAL_SLOTS - 1)) % TOTAL_SLOTS
    lengths = lengths.at[first].set(SLOT).at[second].set(LMIN)
    return (lengths, first, second)


def draw_queries(key, part):
    key = jax.random.fold_in(key, 1)
    key_base = jax.random.fold_in(key, 0)
    base = jnp.clip(jax.random.normal(key_base, (ROWS, H * DH), jnp.float32), -4.0, 4.0)
    return base.astype(jnp.bfloat16)


def draw_prompt_keys(key, part):
    key = jax.random.fold_in(key, 2)
    key_base = jax.random.fold_in(key, 0)
    base = jnp.clip(jax.random.normal(key_base, (PROMPT_ROWS, DH), jnp.float32), -4.0, 4.0)
    return base.astype(jnp.bfloat16)


def draw_slot_prompt(key, part):
    key = jax.random.fold_in(key, 5)
    order = jax.random.permutation(key, TOTAL_SLOTS)
    return (order // RESPONSES).astype(jnp.int32)


def draw_slot_length(key, part):
    lengths, first, second = length_plan(key)
    return lengths.astype(jnp.int32)


def draw_slot_begin(key, part):
    lengths, first, second = length_plan(key)
    key = jax.random.fold_in(key, 4)
    begin = jax.random.randint(key, (TOTAL_SLOTS,), 0, SLOT - lengths + 1)
    begin = begin.at[first].set(0).at[second].set(SLOT - LMIN)
    return begin.astype(jnp.int32)


def draw_block_prompt(key, part):
    key = jax.random.fold_in(key, 9)
    return jax.random.permutation(key, N_SEQ).astype(jnp.int32)


def shard_levels(own_key, dims, cuts, smallest, largest):
    gain, own = 1.0, jax.random.fold_in(own_key, 6)
    for position, parts in cuts:
        heights = jnp.exp(jax.random.uniform(jax.random.fold_in(own, position), (parts,), jnp.float32, smallest / len(cuts), largest / len(cuts)))
        gain = gain * jnp.repeat(heights, dims[position] // parts).reshape([-1 if axis == position else 1 for axis in range(len(dims))])
    return gain


def centred(own_key, shape, scale, bound, cuts=(), kind=jnp.bfloat16):
    result = jax.random.normal(own_key, shape, jnp.float32) * scale
    if len(cuts) > 0:
        result = shard_levels(own_key, shape, cuts, -0.22, 0.18) * result
    return jnp.clip(result, min=-bound, max=bound).astype(kind)


def setup_inputs(seed: int = 0, part: int = 0) -> dict:
    arg_keys = jax.random.split(jax.random.key(seed), 11)
    part_splits = jax.random.split(jax.random.fold_in(arg_keys[10], part), 11)
    return {
        "queries": draw_queries(jax.random.fold_in(jax.random.fold_in(arg_keys[10], part), 71), part),
        "resp_keys": centred(part_splits[1], (ROWS, DH), 1.0, 6.0, ((0, 16),)),
        "resp_values": centred(part_splits[2], (ROWS, DH), 1.0, 6.0, ((0, 16),)),
        "out_grad": centred(part_splits[3], (ROWS, H * DH), 8.0, 48.0, ((0, 16),)),
        "prompt_keys": draw_prompt_keys(jax.random.fold_in(jax.random.fold_in(arg_keys[10], part), 71), part),
        "prompt_values": centred(part_splits[5], (PROMPT_ROWS, DH), 1.0, 6.0, ((0, 16),)),
        "slot_prompt": draw_slot_prompt(jax.random.fold_in(jax.random.fold_in(arg_keys[10], part), 71), part),
        "slot_length": draw_slot_length(jax.random.fold_in(jax.random.fold_in(arg_keys[10], part), 71), part),
        "slot_begin": draw_slot_begin(jax.random.fold_in(jax.random.fold_in(arg_keys[10], part), 71), part),
        "block_prompt": draw_block_prompt(jax.random.fold_in(jax.random.fold_in(arg_keys[10], part), 71), part),
    }


score_scale = 0.08838834764831845


def allowed_columns(slot_rows, prompt_len, length, begin):
    rows = jnp.arange(slot_rows, dtype=jnp.int32)
    live = (rows >= begin) & (rows < begin + length)
    local = live[None, :] & (rows[None, :] <= rows[:, None])
    prompt_part = jnp.ones((slot_rows, prompt_len), jnp.bool_)
    return jnp.concatenate([prompt_part, local], axis=1), live


def slot_gradients(slot_queries, slot_grad, keys, values, allowed, live):
    slot_rows = slot_queries.shape[0]
    width = keys.shape[1]
    heads = slot_queries.shape[1] // width
    grad_live = jnp.where(live[:, None], slot_grad, jnp.zeros_like(slot_grad))
    query_rows = slot_queries.reshape(slot_rows * heads, width)
    grad_rows = grad_live.reshape(slot_rows * heads, width)
    across = (((1,), (1,)), ((), ()))
    down = (((0,), (0,)), ((), ()))
    scores = lax.dot_general(query_rows, keys, across, preferred_element_type=jnp.float32) * score_scale
    scores = scores.reshape(slot_rows, heads, keys.shape[0])
    scores = jnp.where(allowed[:, None, :], scores, -jnp.inf)
    top = jnp.max(scores, axis=2, keepdims=True)
    lse = top + jnp.log(jnp.sum(jnp.exp(scores - top), axis=2, keepdims=True))
    prob = jnp.exp(scores - lse).reshape(slot_rows * heads, keys.shape[0])
    prob_rounded = prob.astype(jnp.bfloat16)
    attended = jnp.dot(prob_rounded, values, preferred_element_type=jnp.float32)
    delta = jnp.sum(grad_rows.astype(jnp.float32) * attended, axis=1, keepdims=True)
    dprob = lax.dot_general(grad_rows, values, across, preferred_element_type=jnp.float32)
    dscore = (prob * (dprob - delta)).astype(jnp.bfloat16)
    query_grad = jnp.dot(dscore, keys, preferred_element_type=jnp.float32) * score_scale
    query_grad = query_grad.reshape(slot_rows, heads * width)
    key_terms = lax.dot_general(dscore, query_rows, down, preferred_element_type=jnp.float32) * score_scale
    value_terms = lax.dot_general(prob_rounded, grad_rows, down, preferred_element_type=jnp.float32)
    return query_grad, key_terms, value_terms


def prompt_row_index(block_prompt, prompt, prow):
    blocks = block_prompt.shape[0]
    pieces = (prompt * OWNERS + jnp.arange(OWNERS, dtype=jnp.int32)).astype(jnp.int32)
    match = block_prompt[None, :] == pieces[:, None]
    holder = jnp.sum(jnp.where(match, jnp.arange(blocks, dtype=jnp.int32)[None, :], 0), axis=1).astype(jnp.int32)
    index = holder[:, None] * prow + jnp.arange(prow, dtype=jnp.int32)[None, :]
    return index.reshape(-1).astype(jnp.int32)


def reference(queries, resp_keys, resp_values, out_grad, prompt_keys, prompt_values, slot_prompt, slot_length, slot_begin, block_prompt):
    total = slot_prompt.shape[0]
    slot_rows = queries.shape[0] // total
    width = resp_keys.shape[1]
    prow = prompt_keys.shape[0] // block_prompt.shape[0]
    prompt_len = prow * OWNERS
    inputs = (queries.reshape(total, slot_rows, -1), out_grad.reshape(total, slot_rows, -1),
              resp_keys.reshape(total, slot_rows, width), resp_values.reshape(total, slot_rows, width),
              slot_prompt, slot_length, slot_begin)

    def advance(carry, item):
        slot_queries, slot_grad, own_keys, own_values, prompt, length, begin = item
        index = prompt_row_index(block_prompt, prompt, prow)
        keys = jnp.concatenate([prompt_keys[index], own_keys], axis=0)
        values = jnp.concatenate([prompt_values[index], own_values], axis=0)
        allowed, live = allowed_columns(slot_rows, prompt_len, length, begin)
        query_grad, key_terms, value_terms = slot_gradients(slot_queries, slot_grad, keys, values, allowed, live)
        key_total, value_total = carry
        key_total = key_total.at[index].add(key_terms[:prompt_len])
        value_total = value_total.at[index].add(value_terms[:prompt_len])
        return (key_total, value_total), (query_grad, key_terms[prompt_len:], value_terms[prompt_len:])

    start = (jnp.zeros(prompt_keys.shape, jnp.float32), jnp.zeros(prompt_keys.shape, jnp.float32))
    (prompt_key_grad, prompt_value_grad), (query_grad, key_rows, value_rows) = lax.scan(advance, start, inputs)
    return (query_grad.reshape(queries.shape[0], queries.shape[1]), key_rows.reshape(resp_keys.shape[0], width),
            value_rows.reshape(resp_keys.shape[0], width), prompt_key_grad, prompt_value_grad)
```

```python
import functools
import math

import jax
import jax.numpy as jnp
from jax import lax
from jax.experimental import pallas as pl
from jax.experimental.pallas import tpu as pltpu
from jax.sharding import PartitionSpec as P

OWNERS = 8
TILE = 128
score_scale = 0.08838834764831845
EXP2_SCALE = score_scale * math.log2(math.e)
MASKED = -1e30

ACROSS = (((1,), (1,)), ((), ()))


def same_core_groups(n):
    return [list(range(core, n, 2)) for core in range(2)]


def swap_cores(x, n):
    return lax.ppermute(x, "seq", [(i, i ^ 1) for i in range(n)])


def exchange(x, n):
    return lax.all_to_all(
        x, "seq", split_axis=0, concat_axis=0, axis_index_groups=same_core_groups(n), tiled=True
    )


def block_position(holder, me, n):
    return ((holder ^ me) & 1) * (n // 2) + (holder >> 1)


def grad_kernel(
    prompt_hbm,
    length_hbm,
    begin_hbm,
    holder_hbm,
    q_hbm,
    g_hbm,
    rk_hbm,
    rv_hbm,
    own_hbm,
    other_hbm,
    dq_hbm,
    drk_hbm,
    drv_hbm,
    own_term_hbm,
    other_term_hbm,
    prompt_ref,
    length_ref,
    begin_ref,
    holder_ref,
    place,
    q_all,
    g_all,
    rk_all,
    rv_all,
    dq_all,
    drk_all,
    drv_all,
    kv,
    term_ref,
    keys,
    values,
    keys_t,
    live_bias,
    scores,
    dprobs,
    prob16,
    dscore16,
    kt,
    vt,
    sem_scalar,
    sem_resp,
    sem_q,
    sem_g,
    sem_dq,
    sem_drk,
    sem_drv,
    sem_kv,
    sem_term,
):
    n = holder_ref.shape[0]
    slots = prompt_ref.shape[0]
    rows, width = rk_all.shape
    slot_rows = rows // slots
    tiles = slot_rows // TILE
    prow = term_ref.shape[0] // n
    prompt_len = prow * OWNERS
    heads = q_all.shape[1] // width
    me = lax.axis_index("seq")

    scalar_copies = [
        pltpu.make_async_copy(src, dst, sem_scalar.at[i])
        for i, (src, dst) in enumerate(
            [
                (prompt_hbm, prompt_ref),
                (length_hbm, length_ref),
                (begin_hbm, begin_ref),
                (holder_hbm, holder_ref),
            ]
        )
    ]
    resp_copies = [
        pltpu.make_async_copy(rk_hbm, rk_all, sem_resp.at[0]),
        pltpu.make_async_copy(rv_hbm, rv_all, sem_resp.at[1]),
    ]

    def tile_rows(chunk):
        return pl.ds(pl.multiple_of(chunk * TILE, TILE), TILE)

    def q_copy(chunk):
        part = tile_rows(chunk)
        return pltpu.make_async_copy(q_hbm.at[part], q_all.at[part], sem_q.at[chunk])

    def g_copy(chunk):
        part = tile_rows(chunk)
        return pltpu.make_async_copy(g_hbm.at[part], g_all.at[part], sem_g.at[chunk])

    def dq_copy(chunk):
        part = tile_rows(chunk)
        return pltpu.make_async_copy(dq_all.at[part], dq_hbm.at[part], sem_dq.at[chunk])

    def slot_part(s):
        return pl.ds(pl.multiple_of(s * slot_rows, slot_rows), slot_rows)

    def drk_copy(s):
        return pltpu.make_async_copy(
            drk_all.at[slot_part(s)], drk_hbm.at[slot_part(s)], sem_drk.at[s]
        )

    def drv_copy(s):
        return pltpu.make_async_copy(
            drv_all.at[slot_part(s)], drv_hbm.at[slot_part(s)], sem_drv.at[s]
        )

    half_rows = term_ref.shape[0] // 2
    kv_copies = [
        pltpu.make_async_copy(src, kv.at[pl.ds(i * half_rows, half_rows)], sem_kv.at[i])
        for i, src in enumerate([own_hbm, other_hbm])
    ]
    term_copies = [
        pltpu.make_async_copy(term_ref.at[pl.ds(i * half_rows, half_rows)], dst, sem_term.at[i])
        for i, dst in enumerate([own_term_hbm, other_term_hbm])
    ]
    for copy in scalar_copies + kv_copies + resp_copies:
        copy.start()
    for chunk in range(slots * tiles):
        q_copy(chunk).start()
        g_copy(chunk).start()

    term_ref[...] = jnp.zeros_like(term_ref)
    causal = jnp.where(
        lax.broadcasted_iota(jnp.int32, (TILE, TILE), 0)
        <= lax.broadcasted_iota(jnp.int32, (TILE, TILE), 1),
        0.0,
        MASKED,
    )
    for copy in scalar_copies + kv_copies + resp_copies:
        copy.wait()

    @pl.loop(0, n)
    def _(j):
        place[holder_ref[j]] = j

    half = heads // 2
    wide = 2 * TILE
    units = [(index, pair) for index in range(tiles) for pair in range(half)]

    def spans(columns):
        return [(c, min(wide, columns - c)) for c in range(0, columns, wide)]

    def columns_of(u):
        return prompt_len + (units[u][0] + 1) * TILE

    def stacked(ref, s, index, first, count):
        part = tile_rows(s * tiles + index)
        return jnp.concatenate(
            [ref[part, (first + h) * width : (first + h + 1) * width] for h in range(count)], axis=0
        )

    def fold(x, how):
        return how(x.reshape(x.shape[0] // 8, 8, x.shape[1]), axis=0)

    def head(s, u, out):
        index, pair = units[u]
        columns, buf = columns_of(u), u % 2
        if pair == 0:
            q_copy(s * tiles + index).wait()
            g_copy(s * tiles + index).wait()
        q2 = stacked(q_all, s, index, 2 * pair, 2)
        g2 = stacked(g_all, s, index, 2 * pair, 2)
        top = None
        for c, size in spans(columns):
            block = lax.dot_general(
                keys[c : c + size, :], q2, ACROSS, preferred_element_type=jnp.float32
            )
            if c >= prompt_len:
                bias = live_bias[c - prompt_len : c - prompt_len + size, :]
                if c + size == columns:
                    last = bias[size - TILE :] + causal
                    bias = last if size == TILE else jnp.concatenate([bias[: size - TILE], last], axis=0)
                block = block + jnp.concatenate([bias, bias], axis=1)
            scores[buf, c : c + size, :] = block
            high = fold(block, jnp.max)
            top = high if top is None else jnp.maximum(top, high)
            dprobs[buf, c : c + size, :] = lax.dot_general(
                values[c : c + size, :], g2, ACROSS, preferred_element_type=jnp.float32
            )
            yield
        out["top"] = jnp.max(top, axis=0, keepdims=True) * EXP2_SCALE

    def middle(s, u, top, out):
        index, _ = units[u]
        buf = u % 2
        total = jnp.zeros((8, wide), jnp.float32)
        weighted = jnp.zeros((8, wide), jnp.float32)
        for c, size in spans(columns_of(u)):
            e = jnp.exp2(scores[buf, c : c + size, :] * EXP2_SCALE - top)
            scores[buf, c : c + size, :] = e
            total = total + fold(e, jnp.sum)
            weighted = weighted + fold(e * dprobs[buf, c : c + size, :], jnp.sum)
            yield
        row = index * TILE + lax.broadcasted_iota(jnp.int32, (1, TILE), 1)
        live = (row >= begin_ref[s]) & (row < begin_ref[s] + length_ref[s])
        live = jnp.concatenate([live, live], axis=1)
        total = jnp.sum(total, axis=0, keepdims=True)
        out["inverse"] = jnp.where(live, 1.0 / total, 0.0)
        out["delta"] = jnp.sum(weighted, axis=0, keepdims=True) * out["inverse"]

    def tail(u, inverse, delta):
        buf, group = u % 2, (u // 2) % 2
        lanes = slice((u % 2) * wide, (u % 2 + 1) * wide)
        for c, size in spans(columns_of(u)):
            p = scores[buf, c : c + size, :] * inverse
            prob16[group, c : c + size, lanes] = p.astype(jnp.bfloat16)
            ds = p * (dprobs[buf, c : c + size, :] - delta)
            dscore16[group, c : c + size, lanes] = ds.astype(jnp.bfloat16)
            yield

    def flush_keys(s, u):
        index, pair = units[u]
        group = (u // 2) % 2
        q4 = stacked(q_all, s, index, 2 * (pair - 1), 4)
        for c, size in spans(columns_of(u)):
            kt[c : c + size, :] += jnp.dot(
                dscore16[group, c : c + size, :], q4, preferred_element_type=jnp.float32
            )
            yield

    def flush_values(s, u):
        index, pair = units[u]
        group = (u // 2) % 2
        g4 = stacked(g_all, s, index, 2 * (pair - 1), 4)
        for c, size in spans(columns_of(u)):
            vt[c : c + size, :] += jnp.dot(
                prob16[group, c : c + size, :], g4, preferred_element_type=jnp.float32
            )
            yield

    def flush_queries(s, u):
        index, pair = units[u]
        group = (u // 2) % 2
        columns = columns_of(u)
        part = tile_rows(s * tiles + index)
        for side in range(2):
            ds = dscore16[group, 0:columns, side * wide : (side + 1) * wide]
            dq = jnp.dot(keys_t[:, 0:columns], ds, preferred_element_type=jnp.float32).T * score_scale
            for h in range(2):
                first = (2 * (pair - 1 + side) + h) * width
                dq_all[part, first : first + width] = dq[h * TILE : (h + 1) * TILE]
            yield
        if pair == half - 1:
            dq_copy(s * tiles + index).start()

    def together(*steps):
        steps = list(steps)
        while steps:
            for step in list(steps):
                if next(step, steps) is steps:
                    steps.remove(step)

    def slot_units(s):
        ahead, now = {}, {}
        together(head(s, 0, ahead))
        for u in range(len(units)):
            top = ahead["top"]
            first, second = [], []
            if u >= 2 and u % 2 == 0:
                first, second = [flush_keys(s, u - 1)], [flush_queries(s, u - 1)]
            elif u >= 2:
                first = [flush_values(s, u - 2)]
            together(middle(s, u, top, now), *first)
            if u + 1 < len(units):
                second = [head(s, u + 1, ahead)] + second
            together(tail(u, now["inverse"], now["delta"]), *second)
        last = len(units) - 1
        together(flush_keys(s, last), flush_values(s, last), flush_queries(s, last))

    @pl.loop(0, slots)
    def _(s):
        first_block = prompt_ref[s] * OWNERS
        for o in range(OWNERS):
            start = block_position(place[first_block + o], me, n) * prow
            source = pl.ds(pl.multiple_of(start, prow), prow)
            keys[o * prow : (o + 1) * prow, :] = kv[source, 0:width]
            values[o * prow : (o + 1) * prow, :] = kv[source, width : 2 * width]
        keys[prompt_len:, :] = rk_all[slot_part(s), :]
        values[prompt_len:, :] = rv_all[slot_part(s), :]
        keys_t[...] = keys[...].astype(jnp.float32).T.astype(jnp.bfloat16)
        column = lax.broadcasted_iota(jnp.int32, (slot_rows, TILE), 0)
        live_bias[...] = jnp.where(column >= begin_ref[s], 0.0, MASKED)
        kt[...] = jnp.zeros_like(kt)
        vt[...] = jnp.zeros_like(vt)
        slot_units(s)
        drk_all[slot_part(s), :] = kt[prompt_len:, :] * score_scale
        drv_all[slot_part(s), :] = vt[prompt_len:, :]
        drk_copy(s).start()
        drv_copy(s).start()
        for o in range(OWNERS):
            start = block_position(place[first_block + o], me, n) * prow
            target = pl.ds(pl.multiple_of(start, prow), prow)
            block = slice(o * prow, (o + 1) * prow)
            term_ref[target, 0:width] += kt[block, :] * score_scale
            term_ref[target, width : 2 * width] += vt[block, :]

    for copy in term_copies:
        copy.start()
    for copy in term_copies:
        copy.wait()
    for chunk in range(slots * tiles):
        dq_copy(chunk).wait()
    for s in range(slots):
        drk_copy(s).wait()
        drv_copy(s).wait()


def slot_grads(queries, resp_keys, resp_values, out_grad, own_kv, other_kv, prompts, lengths, begins, holders):
    slots = prompts.shape[0]
    rows, columns = queries.shape
    slot_rows, width = rows // slots, resp_keys.shape[1]
    n = holders.shape[0]
    prow = 2 * own_kv.shape[0] // n
    total = prow * OWNERS + slot_rows
    tiles = slot_rows // TILE
    hbm = pl.BlockSpec(memory_space=pltpu.HBM)
    f32, bf16 = jnp.float32, jnp.bfloat16
    return pl.pallas_call(
        grad_kernel,
        in_specs=[hbm] * 10,
        out_specs=[hbm] * 5,
        out_shape=[
            jax.ShapeDtypeStruct((rows, columns), f32),
            jax.ShapeDtypeStruct((rows, width), f32),
            jax.ShapeDtypeStruct((rows, width), f32),
            jax.ShapeDtypeStruct((n * prow // 2, 2 * width), f32),
            jax.ShapeDtypeStruct((n * prow // 2, 2 * width), f32),
        ],
        scratch_shapes=[
            pltpu.SMEM((slots,), jnp.int32),
            pltpu.SMEM((slots,), jnp.int32),
            pltpu.SMEM((slots,), jnp.int32),
            pltpu.SMEM((n,), jnp.int32),
            pltpu.SMEM((n,), jnp.int32),
            pltpu.VMEM((rows, columns), bf16),
            pltpu.VMEM((rows, columns), bf16),
            pltpu.VMEM((rows, width), bf16),
            pltpu.VMEM((rows, width), bf16),
            pltpu.VMEM((rows, columns), f32),
            pltpu.VMEM((rows, width), f32),
            pltpu.VMEM((rows, width), f32),
            pltpu.VMEM((n * prow, 2 * width), bf16),
            pltpu.VMEM((n * prow, 2 * width), f32),
            pltpu.VMEM((total, width), bf16),
            pltpu.VMEM((total, width), bf16),
            pltpu.VMEM((width, total), bf16),
            pltpu.VMEM((slot_rows, TILE), f32),
            pltpu.VMEM((2, total, 2 * TILE), f32),
            pltpu.VMEM((2, total, 2 * TILE), f32),
            pltpu.VMEM((2, total, 4 * TILE), bf16),
            pltpu.VMEM((2, total, 4 * TILE), bf16),
            pltpu.VMEM((total, width), f32),
            pltpu.VMEM((total, width), f32),
            pltpu.SemaphoreType.DMA((4,)),
            pltpu.SemaphoreType.DMA((2,)),
            pltpu.SemaphoreType.DMA((slots * tiles,)),
            pltpu.SemaphoreType.DMA((slots * tiles,)),
            pltpu.SemaphoreType.DMA((slots * tiles,)),
            pltpu.SemaphoreType.DMA((slots,)),
            pltpu.SemaphoreType.DMA((slots,)),
            pltpu.SemaphoreType.DMA((2,)),
            pltpu.SemaphoreType.DMA((2,)),
        ],
        compiler_params=pltpu.CompilerParams(vmem_limit_bytes=60 * 1024 * 1024),
    )(prompts, lengths, begins, holders, queries, out_grad, resp_keys, resp_values, own_kv, other_kv)


def body(
    n,
    queries,
    resp_keys,
    resp_values,
    out_grad,
    prompt_keys,
    prompt_values,
    slot_prompt,
    slot_length,
    slot_begin,
    block_prompt,
):
    width = resp_keys.shape[1]
    prow = prompt_keys.shape[0]
    own = jnp.pad(prompt_keys, ((0, 0), (0, width))) + jnp.pad(prompt_values, ((0, 0), (width, 0)))
    own = jnp.broadcast_to(own[None], (n // 2, prow, 2 * width)).reshape(-1, 2 * width)
    own_kv = exchange(own, n)
    other_kv = swap_cores(own_kv, n)
    query_grad, key_grad, value_grad, own_term, other_term = slot_grads(
        queries, resp_keys, resp_values, out_grad, own_kv, other_kv,
        slot_prompt, slot_length, slot_begin, block_prompt,
    )
    chip = exchange(own_term + swap_cores(other_term, n), n)
    owned = jnp.sum(chip.reshape(n // 2, prow, 2 * width), axis=0)
    return query_grad, key_grad, value_grad, owned[:, :width], owned[:, width:]


def solution(mesh):
    n = mesh.shape["seq"]
    rows = P(("groups", "seq"), None)
    slots = P(("groups", "seq"))
    return jax.shard_map(
        functools.partial(body, n),
        mesh=mesh,
        in_specs=(rows,) * 6 + (slots,) * 3 + (P("groups"),),
        out_specs=(rows,) * 5,
        check_vma=False,
    )
```

```python
import functools
import math

import jax
import jax.numpy as jnp
from jax import lax
from jax.experimental import pallas as pl
from jax.experimental.pallas import tpu as pltpu
from jax.sharding import PartitionSpec as P

OWNERS = 8
TILE = 128
PIECE = 32
score_scale = 0.08838834764831845
EXP2_SCALE = score_scale * math.log2(math.e)
MASKED = -1e30

ACROSS = (((1,), (1,)), ((), ()))


def same_core_groups(n):
    return [list(range(core, n, 2)) for core in range(2)]


def swap_cores(x, n):
    return lax.ppermute(x, "seq", [(i, i ^ 1) for i in range(n)])


def exchange(x, n):
    return lax.all_to_all(
        x, "seq", split_axis=0, concat_axis=0, axis_index_groups=same_core_groups(n), tiled=True
    )


def block_position(holder, me, n):
    return ((holder ^ me) & 1) * (n // 2) + (holder >> 1)


def grad_kernel(
    prompt_hbm,
    length_hbm,
    begin_hbm,
    holder_hbm,
    q_hbm,
    g_hbm,
    rk_hbm,
    rv_hbm,
    own_hbm,
    other_hbm,
    dq_hbm,
    drk_hbm,
    drv_hbm,
    own_term_hbm,
    other_term_hbm,
    prompt_ref,
    length_ref,
    begin_ref,
    holder_ref,
    place,
    q_all,
    g_all,
    rk_all,
    rv_all,
    dq_all,
    drk_all,
    drv_all,
    kv,
    term_ref,
    keys,
    values,
    keys_t,
    live_bias,
    causal_bias,
    scores,
    dprobs,
    prob16,
    dscore16,
    kt,
    vt,
    sem_scalar,
    sem_resp,
    sem_q,
    sem_g,
    sem_dq,
    sem_drk,
    sem_drv,
    sem_kv,
    sem_term,
):
    n = holder_ref.shape[0]
    slots = prompt_ref.shape[0]
    rows, width = rk_all.shape
    slot_rows = rows // slots
    tiles = slot_rows // TILE
    prow = term_ref.shape[0] // n
    prompt_len = prow * OWNERS
    heads = q_all.shape[1] // width
    me = lax.axis_index("seq")

    scalar_copies = [
        pltpu.make_async_copy(src, dst, sem_scalar.at[i])
        for i, (src, dst) in enumerate(
            [
                (prompt_hbm, prompt_ref),
                (length_hbm, length_ref),
                (begin_hbm, begin_ref),
                (holder_hbm, holder_ref),
            ]
        )
    ]
    resp_copies = [
        pltpu.make_async_copy(rk_hbm, rk_all, sem_resp.at[0]),
        pltpu.make_async_copy(rv_hbm, rv_all, sem_resp.at[1]),
    ]

    def tile_rows(chunk):
        return pl.ds(pl.multiple_of(chunk * TILE, TILE), TILE)

    def q_copy(chunk):
        part = tile_rows(chunk)
        return pltpu.make_async_copy(q_hbm.at[part], q_all.at[part], sem_q.at[chunk])

    def g_copy(chunk):
        part = tile_rows(chunk)
        return pltpu.make_async_copy(g_hbm.at[part], g_all.at[part], sem_g.at[chunk])

    def dq_copy(chunk):
        part = tile_rows(chunk)
        return pltpu.make_async_copy(dq_all.at[part], dq_hbm.at[part], sem_dq.at[chunk])

    def slot_part(s):
        return pl.ds(pl.multiple_of(s * slot_rows, slot_rows), slot_rows)

    def drk_copy(s):
        return pltpu.make_async_copy(
            drk_all.at[slot_part(s)], drk_hbm.at[slot_part(s)], sem_drk.at[s]
        )

    def drv_copy(s):
        return pltpu.make_async_copy(
            drv_all.at[slot_part(s)], drv_hbm.at[slot_part(s)], sem_drv.at[s]
        )

    half_rows = term_ref.shape[0] // 2
    kv_copies = [
        pltpu.make_async_copy(src, kv.at[pl.ds(i * half_rows, half_rows)], sem_kv.at[i])
        for i, src in enumerate([own_hbm, other_hbm])
    ]
    term_copies = [
        pltpu.make_async_copy(term_ref.at[pl.ds(i * half_rows, half_rows)], dst, sem_term.at[i])
        for i, dst in enumerate([own_term_hbm, other_term_hbm])
    ]
    for copy in scalar_copies + kv_copies + resp_copies:
        copy.start()
    for chunk in range(slots * tiles):
        q_copy(chunk).start()
        g_copy(chunk).start()

    term_ref[...] = jnp.zeros_like(term_ref)
    causal_bias[...] = jnp.where(
        lax.broadcasted_iota(jnp.int32, (TILE, TILE), 0)
        <= lax.broadcasted_iota(jnp.int32, (TILE, TILE), 1),
        0.0,
        MASKED,
    )
    for copy in scalar_copies + kv_copies + resp_copies:
        copy.wait()

    @pl.loop(0, n)
    def _(j):
        place[holder_ref[j]] = j

    half = heads // 2
    wide = 2 * TILE
    units = [(index, pair) for index in range(tiles) for pair in range(half)]

    def spans(columns):
        return [(c, PIECE) for c in range(0, columns, PIECE)]

    def columns_of(u):
        return prompt_len + (units[u][0] + 1) * TILE

    def stacked(ref, s, index, first, count):
        part = tile_rows(s * tiles + index)
        return jnp.concatenate(
            [ref[part, (first + h) * width : (first + h + 1) * width] for h in range(count)], axis=0
        )

    def fold(x, how):
        return how(x.reshape(x.shape[0] // 8, 8, x.shape[1]), axis=0)

    def biased(buf, c, columns):
        block = scores[buf, c : c + PIECE, :]
        if c >= prompt_len:
            bias = live_bias[c - prompt_len : c - prompt_len + PIECE, :]
            if c >= columns - TILE:
                first = c - (columns - TILE)
                bias = bias + causal_bias[first : first + PIECE, :]
            block = block + jnp.concatenate([bias, bias], axis=1)
        return block

    def head(s, u, out):
        index, pair = units[u]
        columns, buf = columns_of(u), u % 2
        if pair == 0:
            q_copy(s * tiles + index).wait()
            g_copy(s * tiles + index).wait()
        q2 = stacked(q_all, s, index, 2 * pair, 2)
        scores[buf, 0:columns, :] = lax.dot_general(
            keys[0:columns, :], q2, ACROSS, preferred_element_type=jnp.float32
        )
        yield
        g2 = stacked(g_all, s, index, 2 * pair, 2)
        dprobs[buf, 0:columns, :] = lax.dot_general(
            values[0:columns, :], g2, ACROSS, preferred_element_type=jnp.float32
        )
        yield

    def middle(s, u, out):
        index, _ = units[u]
        buf, columns = u % 2, columns_of(u)
        top = None
        for c, size in spans(columns):
            high = fold(biased(buf, c, columns), jnp.max)
            top = high if top is None else jnp.maximum(top, high)
        top = jnp.max(top, axis=0, keepdims=True) * EXP2_SCALE
        yield
        total = jnp.zeros((8, wide), jnp.float32)
        weighted = jnp.zeros((8, wide), jnp.float32)
        for c, size in spans(columns):
            e = jnp.exp2(biased(buf, c, columns) * EXP2_SCALE - top)
            scores[buf, c : c + size, :] = e
            total = total + fold(e, jnp.sum)
            weighted = weighted + fold(e * dprobs[buf, c : c + size, :], jnp.sum)
            yield
        row = index * TILE + lax.broadcasted_iota(jnp.int32, (1, TILE), 1)
        live = (row >= begin_ref[s]) & (row < begin_ref[s] + length_ref[s])
        live = jnp.concatenate([live, live], axis=1)
        total = jnp.sum(total, axis=0, keepdims=True)
        out["inverse"] = jnp.where(live, 1.0 / total, 0.0)
        out["delta"] = jnp.sum(weighted, axis=0, keepdims=True) * out["inverse"]

    def tail(u, inverse, delta):
        buf, group = u % 2, (u // 2) % 2
        lanes = slice((u % 2) * wide, (u % 2 + 1) * wide)
        for c, size in spans(columns_of(u)):
            p = scores[buf, c : c + size, :] * inverse
            prob16[group, c : c + size, lanes] = p.astype(jnp.bfloat16)
            ds = p * (dprobs[buf, c : c + size, :] - delta)
            dscore16[group, c : c + size, lanes] = ds.astype(jnp.bfloat16)
            yield

    def flush_keys(s, u):
        index, pair = units[u]
        group, columns = (u // 2) % 2, columns_of(u)
        q4 = stacked(q_all, s, index, 2 * (pair - 1), 4)
        kt[0:columns, :] += jnp.dot(
            dscore16[group, 0:columns, :], q4, preferred_element_type=jnp.float32
        )
        yield

    def flush_values(s, u):
        index, pair = units[u]
        group, columns = (u // 2) % 2, columns_of(u)
        g4 = stacked(g_all, s, index, 2 * (pair - 1), 4)
        vt[0:columns, :] += jnp.dot(
            prob16[group, 0:columns, :], g4, preferred_element_type=jnp.float32
        )
        yield

    def flush_queries(s, u):
        index, pair = units[u]
        group = (u // 2) % 2
        columns = columns_of(u)
        part = tile_rows(s * tiles + index)
        for side in range(2):
            ds = dscore16[group, 0:columns, side * wide : (side + 1) * wide]
            dq = jnp.dot(keys_t[:, 0:columns], ds, preferred_element_type=jnp.float32).T * score_scale
            for h in range(2):
                first = (2 * (pair - 1 + side) + h) * width
                dq_all[part, first : first + width] = dq[h * TILE : (h + 1) * TILE]
            yield
        if pair == half - 1:
            dq_copy(s * tiles + index).start()

    def together(*steps):
        steps = list(steps)
        while steps:
            for step in list(steps):
                if next(step, steps) is steps:
                    steps.remove(step)

    def slot_units(s):
        now = {}
        together(head(s, 0, now))
        for u in range(len(units)):
            first, second = [], []
            if u >= 2 and u % 2 == 0:
                first, second = [flush_keys(s, u - 1)], [flush_queries(s, u - 1)]
            elif u >= 2:
                first = [flush_values(s, u - 2)]
            together(middle(s, u, now), *first)
            if u + 1 < len(units):
                second = [head(s, u + 1, now)] + second
            together(tail(u, now["inverse"], now["delta"]), *second)
        last = len(units) - 1
        together(flush_keys(s, last), flush_values(s, last), flush_queries(s, last))

    @pl.loop(0, slots)
    def _(s):
        first_block = prompt_ref[s] * OWNERS
        for o in range(OWNERS):
            start = block_position(place[first_block + o], me, n) * prow
            source = pl.ds(pl.multiple_of(start, prow), prow)
            keys[o * prow : (o + 1) * prow, :] = kv[source, 0:width]
            values[o * prow : (o + 1) * prow, :] = kv[source, width : 2 * width]
        keys[prompt_len:, :] = rk_all[slot_part(s), :]
        values[prompt_len:, :] = rv_all[slot_part(s), :]
        keys_t[...] = keys[...].astype(jnp.float32).T.astype(jnp.bfloat16)
        column = lax.broadcasted_iota(jnp.int32, (slot_rows, TILE), 0)
        live_bias[...] = jnp.where(column >= begin_ref[s], 0.0, MASKED)
        kt[...] = jnp.zeros_like(kt)
        vt[...] = jnp.zeros_like(vt)
        slot_units(s)
        drk_all[slot_part(s), :] = kt[prompt_len:, :] * score_scale
        drv_all[slot_part(s), :] = vt[prompt_len:, :]
        drk_copy(s).start()
        drv_copy(s).start()
        for o in range(OWNERS):
            start = block_position(place[first_block + o], me, n) * prow
            target = pl.ds(pl.multiple_of(start, prow), prow)
            block = slice(o * prow, (o + 1) * prow)
            term_ref[target, 0:width] += kt[block, :] * score_scale
            term_ref[target, width : 2 * width] += vt[block, :]

    for copy in term_copies:
        copy.start()
    for copy in term_copies:
        copy.wait()
    for chunk in range(slots * tiles):
        dq_copy(chunk).wait()
    for s in range(slots):
        drk_copy(s).wait()
        drv_copy(s).wait()


def slot_grads(queries, resp_keys, resp_values, out_grad, own_kv, other_kv, prompts, lengths, begins, holders):
    slots = prompts.shape[0]
    rows, columns = queries.shape
    slot_rows, width = rows // slots, resp_keys.shape[1]
    n = holders.shape[0]
    prow = 2 * own_kv.shape[0] // n
    total = prow * OWNERS + slot_rows
    tiles = slot_rows // TILE
    hbm = pl.BlockSpec(memory_space=pltpu.HBM)
    f32, bf16 = jnp.float32, jnp.bfloat16
    return pl.pallas_call(
        grad_kernel,
        in_specs=[hbm] * 10,
        out_specs=[hbm] * 5,
        out_shape=[
            jax.ShapeDtypeStruct((rows, columns), f32),
            jax.ShapeDtypeStruct((rows, width), f32),
            jax.ShapeDtypeStruct((rows, width), f32),
            jax.ShapeDtypeStruct((n * prow // 2, 2 * width), f32),
            jax.ShapeDtypeStruct((n * prow // 2, 2 * width), f32),
        ],
        scratch_shapes=[
            pltpu.SMEM((slots,), jnp.int32),
            pltpu.SMEM((slots,), jnp.int32),
            pltpu.SMEM((slots,), jnp.int32),
            pltpu.SMEM((n,), jnp.int32),
            pltpu.SMEM((n,), jnp.int32),
            pltpu.VMEM((rows, columns), bf16),
            pltpu.VMEM((rows, columns), bf16),
            pltpu.VMEM((rows, width), bf16),
            pltpu.VMEM((rows, width), bf16),
            pltpu.VMEM((rows, columns), f32),
            pltpu.VMEM((rows, width), f32),
            pltpu.VMEM((rows, width), f32),
            pltpu.VMEM((n * prow, 2 * width), bf16),
            pltpu.VMEM((n * prow, 2 * width), f32),
            pltpu.VMEM((total, width), bf16),
            pltpu.VMEM((total, width), bf16),
            pltpu.VMEM((width, total), bf16),
            pltpu.VMEM((slot_rows, TILE), f32),
            pltpu.VMEM((TILE, TILE), f32),
            pltpu.VMEM((2, total, 2 * TILE), f32),
            pltpu.VMEM((2, total, 2 * TILE), f32),
            pltpu.VMEM((2, total, 4 * TILE), bf16),
            pltpu.VMEM((2, total, 4 * TILE), bf16),
            pltpu.VMEM((total, width), f32),
            pltpu.VMEM((total, width), f32),
            pltpu.SemaphoreType.DMA((4,)),
            pltpu.SemaphoreType.DMA((2,)),
            pltpu.SemaphoreType.DMA((slots * tiles,)),
            pltpu.SemaphoreType.DMA((slots * tiles,)),
            pltpu.SemaphoreType.DMA((slots * tiles,)),
            pltpu.SemaphoreType.DMA((slots,)),
            pltpu.SemaphoreType.DMA((slots,)),
            pltpu.SemaphoreType.DMA((2,)),
            pltpu.SemaphoreType.DMA((2,)),
        ],
        compiler_params=pltpu.CompilerParams(vmem_limit_bytes=60 * 1024 * 1024),
    )(prompts, lengths, begins, holders, queries, out_grad, resp_keys, resp_values, own_kv, other_kv)


def body(
    n,
    queries,
    resp_keys,
    resp_values,
    out_grad,
    prompt_keys,
    prompt_values,
    slot_prompt,
    slot_length,
    slot_begin,
    block_prompt,
):
    width = resp_keys.shape[1]
    prow = prompt_keys.shape[0]
    own = jnp.pad(prompt_keys, ((0, 0), (0, width))) + jnp.pad(prompt_values, ((0, 0), (width, 0)))
    own = jnp.broadcast_to(own[None], (n // 2, prow, 2 * width)).reshape(-1, 2 * width)
    own_kv = exchange(own, n)
    other_kv = swap_cores(own_kv, n)
    query_grad, key_grad, value_grad, own_term, other_term = slot_grads(
        queries, resp_keys, resp_values, out_grad, own_kv, other_kv,
        slot_prompt, slot_length, slot_begin, block_prompt,
    )
    chip = (own_term + swap_cores(other_term, n)).astype(jnp.bfloat16)
    parts = exchange(chip, n).reshape(n // 2, prow, 2 * width)
    owned = jnp.sum(parts.astype(jnp.float32), axis=0)
    return query_grad, key_grad, value_grad, owned[:, :width], owned[:, width:]


def solution(mesh):
    n = mesh.shape["seq"]
    rows = P(("groups", "seq"), None)
    slots = P(("groups", "seq"))
    return jax.shard_map(
        functools.partial(body, n),
        mesh=mesh,
        in_specs=(rows,) * 6 + (slots,) * 3 + (P("groups"),),
        out_specs=(rows,) * 5,
        check_vma=False,
    )
```

```python
import functools
import math

import jax
import jax.numpy as jnp
from jax import lax
from jax.experimental import pallas as pl
from jax.experimental.pallas import tpu as pltpu
from jax.sharding import PartitionSpec as P

OWNERS = 8
TILE = 128
PIECE = 16
HEADS_AT_ONCE = 4
score_scale = 0.08838834764831845
EXP2_SCALE = score_scale * math.log2(math.e)
MASKED = -1e30

ACROSS = (((1,), (1,)), ((), ()))


def same_core_groups(n):
    return [list(range(core, n, 2)) for core in range(2)]


def swap_cores(x, n):
    return lax.ppermute(x, "seq", [(i, i ^ 1) for i in range(n)])


def exchange(x, n):
    return lax.all_to_all(
        x, "seq", split_axis=0, concat_axis=0, axis_index_groups=same_core_groups(n), tiled=True
    )


def block_position(holder, me, n):
    return ((holder ^ me) & 1) * (n // 2) + (holder >> 1)


def grad_kernel(
    prompt_hbm,
    length_hbm,
    begin_hbm,
    holder_hbm,
    q_hbm,
    g_hbm,
    rk_hbm,
    rv_hbm,
    own_hbm,
    other_hbm,
    dq_hbm,
    drk_hbm,
    drv_hbm,
    own_term_hbm,
    other_term_hbm,
    prompt_ref,
    length_ref,
    begin_ref,
    holder_ref,
    place,
    q_all,
    g_all,
    rk_all,
    rv_all,
    dq_all,
    drk_all,
    drv_all,
    kv,
    term_ref,
    keys,
    values,
    keys_t,
    live_bias,
    causal_bias,
    scores,
    dprobs,
    prob16,
    dscore16,
    kt,
    vt,
    sem_scalar,
    sem_resp,
    sem_q,
    sem_g,
    sem_dq,
    sem_drk,
    sem_drv,
    sem_kv,
    sem_term,
):
    n = holder_ref.shape[0]
    slots = prompt_ref.shape[0]
    rows, width = rk_all.shape
    slot_rows = rows // slots
    tiles = slot_rows // TILE
    prow = term_ref.shape[0] // n
    prompt_len = prow * OWNERS
    heads = q_all.shape[1] // width
    me = lax.axis_index("seq")

    scalar_copies = [
        pltpu.make_async_copy(src, dst, sem_scalar.at[i])
        for i, (src, dst) in enumerate(
            [
                (prompt_hbm, prompt_ref),
                (length_hbm, length_ref),
                (begin_hbm, begin_ref),
                (holder_hbm, holder_ref),
            ]
        )
    ]
    resp_copies = [
        pltpu.make_async_copy(rk_hbm, rk_all, sem_resp.at[0]),
        pltpu.make_async_copy(rv_hbm, rv_all, sem_resp.at[1]),
    ]

    def tile_rows(chunk):
        return pl.ds(pl.multiple_of(chunk * TILE, TILE), TILE)

    def q_copy(chunk):
        part = tile_rows(chunk)
        return pltpu.make_async_copy(q_hbm.at[part], q_all.at[part], sem_q.at[chunk])

    def g_copy(chunk):
        part = tile_rows(chunk)
        return pltpu.make_async_copy(g_hbm.at[part], g_all.at[part], sem_g.at[chunk])

    def dq_copy(chunk):
        part = tile_rows(chunk)
        return pltpu.make_async_copy(dq_all.at[part], dq_hbm.at[part], sem_dq.at[chunk])

    def slot_part(s):
        return pl.ds(pl.multiple_of(s * slot_rows, slot_rows), slot_rows)

    def drk_copy(s):
        return pltpu.make_async_copy(
            drk_all.at[slot_part(s)], drk_hbm.at[slot_part(s)], sem_drk.at[s]
        )

    def drv_copy(s):
        return pltpu.make_async_copy(
            drv_all.at[slot_part(s)], drv_hbm.at[slot_part(s)], sem_drv.at[s]
        )

    half_rows = term_ref.shape[0] // 2
    kv_copies = [
        pltpu.make_async_copy(src, kv.at[pl.ds(i * half_rows, half_rows)], sem_kv.at[i])
        for i, src in enumerate([own_hbm, other_hbm])
    ]
    term_copies = [
        pltpu.make_async_copy(term_ref.at[pl.ds(i * half_rows, half_rows)], dst, sem_term.at[i])
        for i, dst in enumerate([own_term_hbm, other_term_hbm])
    ]
    for copy in scalar_copies + kv_copies + resp_copies:
        copy.start()
    for chunk in range(slots * tiles):
        q_copy(chunk).start()
        g_copy(chunk).start()

    term_ref[...] = jnp.zeros_like(term_ref)
    causal_bias[...] = jnp.where(
        lax.broadcasted_iota(jnp.int32, (TILE, TILE), 0)
        <= lax.broadcasted_iota(jnp.int32, (TILE, TILE), 1),
        0.0,
        MASKED,
    )
    for copy in scalar_copies + kv_copies + resp_copies:
        copy.wait()

    @pl.loop(0, n)
    def _(j):
        place[holder_ref[j]] = j

    wide = HEADS_AT_ONCE * TILE
    groups = heads // HEADS_AT_ONCE
    units = [(index, group) for index in range(tiles) for group in range(groups)]

    def spans(columns):
        return [(c, PIECE) for c in range(0, columns, PIECE)]

    def columns_of(u):
        return prompt_len + (units[u][0] + 1) * TILE

    def stacked(ref, s, u):
        index, group = units[u]
        part = tile_rows(s * tiles + index)
        return jnp.concatenate(
            [
                ref[part, h * width : (h + 1) * width]
                for h in range(group * HEADS_AT_ONCE, (group + 1) * HEADS_AT_ONCE)
            ],
            axis=0,
        )

    def fold(x, how):
        return how(x.reshape(x.shape[0] // 8, 8, x.shape[1]), axis=0)

    def biased(buf, c, columns):
        block = scores[buf, c : c + PIECE, :]
        if c >= prompt_len:
            bias = live_bias[c - prompt_len : c - prompt_len + PIECE, :]
            if c >= columns - TILE:
                first = c - (columns - TILE)
                bias = bias + causal_bias[first : first + PIECE, :]
            block = block + jnp.concatenate([bias] * HEADS_AT_ONCE, axis=1)
        return block

    def head(s, u):
        index, group = units[u]
        columns, buf = columns_of(u), u % 2
        if group == 0:
            q_copy(s * tiles + index).wait()
            g_copy(s * tiles + index).wait()
        scores[buf, 0:columns, :] = lax.dot_general(
            keys[0:columns, :], stacked(q_all, s, u), ACROSS, preferred_element_type=jnp.float32
        )
        yield
        dprobs[buf, 0:columns, :] = lax.dot_general(
            values[0:columns, :], stacked(g_all, s, u), ACROSS, preferred_element_type=jnp.float32
        )
        yield

    def middle(s, u, out):
        index, _ = units[u]
        buf, columns = u % 2, columns_of(u)
        top = None
        for c, size in spans(columns):
            high = fold(biased(buf, c, columns), jnp.max)
            top = high if top is None else jnp.maximum(top, high)
        top = jnp.max(top, axis=0, keepdims=True) * EXP2_SCALE
        yield
        total = jnp.zeros((8, wide), jnp.float32)
        weighted = jnp.zeros((8, wide), jnp.float32)
        for c, size in spans(columns):
            e = jnp.exp2(biased(buf, c, columns) * EXP2_SCALE - top)
            scores[buf, c : c + size, :] = e
            total = total + fold(e, jnp.sum)
            weighted = weighted + fold(e * dprobs[buf, c : c + size, :], jnp.sum)
            yield
        row = index * TILE + lax.broadcasted_iota(jnp.int32, (1, TILE), 1)
        live = (row >= begin_ref[s]) & (row < begin_ref[s] + length_ref[s])
        live = jnp.concatenate([live] * HEADS_AT_ONCE, axis=1)
        total = jnp.sum(total, axis=0, keepdims=True)
        out["inverse"] = jnp.where(live, 1.0 / total, 0.0)
        out["delta"] = jnp.sum(weighted, axis=0, keepdims=True) * out["inverse"]

    def tail(u, inverse, delta):
        buf = u % 2
        for c, size in spans(columns_of(u)):
            p = scores[buf, c : c + size, :] * inverse
            prob16[buf, c : c + size, :] = p.astype(jnp.bfloat16)
            ds = p * (dprobs[buf, c : c + size, :] - delta)
            dscore16[buf, c : c + size, :] = ds.astype(jnp.bfloat16)
            yield

    def flush_keys(s, u):
        columns = columns_of(u)
        kt[0:columns, :] += jnp.dot(
            dscore16[u % 2, 0:columns, :], stacked(q_all, s, u), preferred_element_type=jnp.float32
        )
        yield

    def flush_values(s, u):
        columns = columns_of(u)
        vt[0:columns, :] += jnp.dot(
            prob16[u % 2, 0:columns, :], stacked(g_all, s, u), preferred_element_type=jnp.float32
        )
        yield

    def flush_queries(s, u):
        index, group = units[u]
        columns = columns_of(u)
        part = tile_rows(s * tiles + index)
        dqt = jnp.dot(
            keys_t[:, 0:columns], dscore16[u % 2, 0:columns, :], preferred_element_type=jnp.float32
        )
        yield
        for h in range(HEADS_AT_ONCE):
            first = (group * HEADS_AT_ONCE + h) * width
            dq = dqt[:, h * TILE : (h + 1) * TILE].T
            dq_all[part, first : first + width] = dq * score_scale
            yield
        if group == groups - 1:
            dq_copy(s * tiles + index).start()

    def together(*steps):
        steps = list(steps)
        while steps:
            for step in list(steps):
                if next(step, steps) is steps:
                    steps.remove(step)

    def slot_units(s):
        now = {}
        together(head(s, 0))
        for u in range(len(units)):
            first, second = [], []
            if u >= 1:
                first = [flush_keys(s, u - 1), flush_values(s, u - 1)]
                second = [flush_queries(s, u - 1)]
            together(middle(s, u, now), *first)
            if u + 1 < len(units):
                second = [head(s, u + 1)] + second
            together(tail(u, now["inverse"], now["delta"]), *second)
        last = len(units) - 1
        together(flush_keys(s, last), flush_values(s, last), flush_queries(s, last))

    @pl.loop(0, slots)
    def _(s):
        first_block = prompt_ref[s] * OWNERS
        for o in range(OWNERS):
            start = block_position(place[first_block + o], me, n) * prow
            source = pl.ds(pl.multiple_of(start, prow), prow)
            keys[o * prow : (o + 1) * prow, :] = kv[source, 0:width]
            values[o * prow : (o + 1) * prow, :] = kv[source, width : 2 * width]
        keys[prompt_len:, :] = rk_all[slot_part(s), :]
        values[prompt_len:, :] = rv_all[slot_part(s), :]
        keys_t[...] = keys[...].astype(jnp.float32).T.astype(jnp.bfloat16)
        column = lax.broadcasted_iota(jnp.int32, (slot_rows, TILE), 0)
        live_bias[...] = jnp.where(column >= begin_ref[s], 0.0, MASKED)
        kt[...] = jnp.zeros_like(kt)
        vt[...] = jnp.zeros_like(vt)
        slot_units(s)
        drk_all[slot_part(s), :] = kt[prompt_len:, :] * score_scale
        drv_all[slot_part(s), :] = vt[prompt_len:, :]
        drk_copy(s).start()
        drv_copy(s).start()
        for o in range(OWNERS):
            start = block_position(place[first_block + o], me, n) * prow
            target = pl.ds(pl.multiple_of(start, prow), prow)
            block = slice(o * prow, (o + 1) * prow)
            term_ref[target, 0:width] += kt[block, :] * score_scale
            term_ref[target, width : 2 * width] += vt[block, :]

    for copy in term_copies:
        copy.start()
    for copy in term_copies:
        copy.wait()
    for chunk in range(slots * tiles):
        dq_copy(chunk).wait()
    for s in range(slots):
        drk_copy(s).wait()
        drv_copy(s).wait()


def slot_grads(queries, resp_keys, resp_values, out_grad, own_kv, other_kv, prompts, lengths, begins, holders):
    slots = prompts.shape[0]
    rows, columns = queries.shape
    slot_rows, width = rows // slots, resp_keys.shape[1]
    n = holders.shape[0]
    prow = 2 * own_kv.shape[0] // n
    total = prow * OWNERS + slot_rows
    tiles = slot_rows // TILE
    hbm = pl.BlockSpec(memory_space=pltpu.HBM)
    f32, bf16 = jnp.float32, jnp.bfloat16
    return pl.pallas_call(
        grad_kernel,
        in_specs=[hbm] * 10,
        out_specs=[hbm] * 5,
        out_shape=[
            jax.ShapeDtypeStruct((rows, columns), f32),
            jax.ShapeDtypeStruct((rows, width), f32),
            jax.ShapeDtypeStruct((rows, width), f32),
            jax.ShapeDtypeStruct((n * prow // 2, 2 * width), f32),
            jax.ShapeDtypeStruct((n * prow // 2, 2 * width), f32),
        ],
        scratch_shapes=[
            pltpu.SMEM((slots,), jnp.int32),
            pltpu.SMEM((slots,), jnp.int32),
            pltpu.SMEM((slots,), jnp.int32),
            pltpu.SMEM((n,), jnp.int32),
            pltpu.SMEM((n,), jnp.int32),
            pltpu.VMEM((rows, columns), bf16),
            pltpu.VMEM((rows, columns), bf16),
            pltpu.VMEM((rows, width), bf16),
            pltpu.VMEM((rows, width), bf16),
            pltpu.VMEM((rows, columns), f32),
            pltpu.VMEM((rows, width), f32),
            pltpu.VMEM((rows, width), f32),
            pltpu.VMEM((n * prow, 2 * width), bf16),
            pltpu.VMEM((n * prow, 2 * width), f32),
            pltpu.VMEM((total, width), bf16),
            pltpu.VMEM((total, width), bf16),
            pltpu.VMEM((width, total), bf16),
            pltpu.VMEM((slot_rows, TILE), f32),
            pltpu.VMEM((TILE, TILE), f32),
            pltpu.VMEM((2, total, HEADS_AT_ONCE * TILE), f32),
            pltpu.VMEM((2, total, HEADS_AT_ONCE * TILE), f32),
            pltpu.VMEM((2, total, HEADS_AT_ONCE * TILE), bf16),
            pltpu.VMEM((2, total, HEADS_AT_ONCE * TILE), bf16),
            pltpu.VMEM((total, width), f32),
            pltpu.VMEM((total, width), f32),
            pltpu.SemaphoreType.DMA((4,)),
            pltpu.SemaphoreType.DMA((2,)),
            pltpu.SemaphoreType.DMA((slots * tiles,)),
            pltpu.SemaphoreType.DMA((slots * tiles,)),
            pltpu.SemaphoreType.DMA((slots * tiles,)),
            pltpu.SemaphoreType.DMA((slots,)),
            pltpu.SemaphoreType.DMA((slots,)),
            pltpu.SemaphoreType.DMA((2,)),
            pltpu.SemaphoreType.DMA((2,)),
        ],
        compiler_params=pltpu.CompilerParams(vmem_limit_bytes=60 * 1024 * 1024),
    )(prompts, lengths, begins, holders, queries, out_grad, resp_keys, resp_values, own_kv, other_kv)


def body(
    n,
    queries,
    resp_keys,
    resp_values,
    out_grad,
    prompt_keys,
    prompt_values,
    slot_prompt,
    slot_length,
    slot_begin,
    block_prompt,
):
    width = resp_keys.shape[1]
    prow = prompt_keys.shape[0]
    own = jnp.pad(prompt_keys, ((0, 0), (0, width))) + jnp.pad(prompt_values, ((0, 0), (width, 0)))
    own = jnp.broadcast_to(own[None], (n // 2, prow, 2 * width)).reshape(-1, 2 * width)
    own_kv = exchange(own, n)
    other_kv = swap_cores(own_kv, n)
    query_grad, key_grad, value_grad, own_term, other_term = slot_grads(
        queries, resp_keys, resp_values, out_grad, own_kv, other_kv,
        slot_prompt, slot_length, slot_begin, block_prompt,
    )
    parts = exchange(own_term + swap_cores(other_term, n), n)
    owned = jnp.sum(parts.reshape(n // 2, prow, 2 * width), axis=0)
    return query_grad, key_grad, value_grad, owned[:, :width], owned[:, width:]


def solution(mesh):
    n = mesh.shape["seq"]
    rows = P(("groups", "seq"), None)
    slots = P(("groups", "seq"))
    return jax.shard_map(
        functools.partial(body, n),
        mesh=mesh,
        in_specs=(rows,) * 6 + (slots,) * 3 + (P("groups"),),
        out_specs=(rows,) * 5,
        check_vma=False,
    )
```

```python
import functools
import math

import jax
import jax.numpy as jnp
from jax import lax
from jax.experimental import pallas as pl
from jax.experimental.pallas import tpu as pltpu
from jax.sharding import PartitionSpec as P

OWNERS = 8
TILE = 128
PIECE = 16
CHUNK = 128
HEADS_AT_ONCE = 4
score_scale = 0.08838834764831845
EXP2_SCALE = score_scale * math.log2(math.e)
MASKED = -1e30

ACROSS = (((1,), (1,)), ((), ()))


def same_core_groups(n):
    return [list(range(core, n, 2)) for core in range(2)]


def swap_cores(x, n):
    return lax.ppermute(x, "seq", [(i, i ^ 1) for i in range(n)])


def exchange(x, n):
    return lax.all_to_all(
        x, "seq", split_axis=0, concat_axis=0, axis_index_groups=same_core_groups(n), tiled=True
    )


def block_position(holder, me, n):
    return ((holder ^ me) & 1) * (n // 2) + (holder >> 1)


def grad_kernel(
    prompt_hbm,
    length_hbm,
    begin_hbm,
    holder_hbm,
    q_hbm,
    g_hbm,
    rk_hbm,
    rv_hbm,
    kv_hbm,
    dq_hbm,
    drk_hbm,
    drv_hbm,
    own_term_hbm,
    other_term_hbm,
    prompt_ref,
    length_ref,
    begin_ref,
    holder_ref,
    place,
    q_all,
    g_all,
    rk_all,
    rv_all,
    dq_all,
    drk_all,
    drv_all,
    kv,
    term_ref,
    keys,
    values,
    keys_t,
    live_bias,
    causal_bias,
    scores,
    dprobs,
    prob16,
    dscore16,
    kt,
    vt,
    sem_scalar,
    sem_resp,
    sem_q,
    sem_g,
    sem_dq,
    sem_drk,
    sem_drv,
    sem_kv,
    sem_term,
):
    n = holder_ref.shape[0]
    slots = prompt_ref.shape[0]
    rows, width = rk_all.shape
    slot_rows = rows // slots
    tiles = slot_rows // TILE
    prow = term_ref.shape[0] // n
    prompt_len = prow * OWNERS
    heads = q_all.shape[1] // width
    me = lax.axis_index("seq")

    scalar_copies = [
        pltpu.make_async_copy(src, dst, sem_scalar.at[i])
        for i, (src, dst) in enumerate(
            [
                (prompt_hbm, prompt_ref),
                (length_hbm, length_ref),
                (begin_hbm, begin_ref),
                (holder_hbm, holder_ref),
            ]
        )
    ]
    resp_copies = [
        pltpu.make_async_copy(rk_hbm, rk_all, sem_resp.at[0]),
        pltpu.make_async_copy(rv_hbm, rv_all, sem_resp.at[1]),
    ]

    def tile_rows(chunk):
        return pl.ds(pl.multiple_of(chunk * TILE, TILE), TILE)

    def q_copy(chunk):
        part = tile_rows(chunk)
        return pltpu.make_async_copy(q_hbm.at[part], q_all.at[part], sem_q.at[chunk])

    def g_copy(chunk):
        part = tile_rows(chunk)
        return pltpu.make_async_copy(g_hbm.at[part], g_all.at[part], sem_g.at[chunk])

    def dq_copy(chunk):
        part = tile_rows(chunk)
        return pltpu.make_async_copy(dq_all.at[part], dq_hbm.at[part], sem_dq.at[chunk])

    def slot_part(s):
        return pl.ds(pl.multiple_of(s * slot_rows, slot_rows), slot_rows)

    def drk_copy(s):
        return pltpu.make_async_copy(
            drk_all.at[slot_part(s)], drk_hbm.at[slot_part(s)], sem_drk.at[s]
        )

    def drv_copy(s):
        return pltpu.make_async_copy(
            drv_all.at[slot_part(s)], drv_hbm.at[slot_part(s)], sem_drv.at[s]
        )

    half_rows = term_ref.shape[0] // 2
    kv_copies = [pltpu.make_async_copy(kv_hbm, kv, sem_kv.at[0])]
    term_copies = [
        pltpu.make_async_copy(term_ref.at[pl.ds(i * half_rows, half_rows)], dst, sem_term.at[i])
        for i, dst in enumerate([own_term_hbm, other_term_hbm])
    ]
    for copy in scalar_copies + kv_copies + resp_copies:
        copy.start()
    for chunk in range(slots * tiles):
        q_copy(chunk).start()
        g_copy(chunk).start()

    term_ref[...] = jnp.zeros_like(term_ref)
    causal_bias[...] = jnp.where(
        lax.broadcasted_iota(jnp.int32, (TILE, TILE), 0)
        <= lax.broadcasted_iota(jnp.int32, (TILE, TILE), 1),
        0.0,
        MASKED,
    )
    for copy in scalar_copies + kv_copies + resp_copies:
        copy.wait()

    @pl.loop(0, n)
    def _(j):
        place[holder_ref[j]] = j

    wide = HEADS_AT_ONCE * TILE
    groups = heads // HEADS_AT_ONCE
    units = [(index, group) for index in range(tiles) for group in range(groups)]

    def spans(columns):
        return [(c, PIECE) for c in range(0, columns, PIECE)]

    def columns_of(u):
        return prompt_len + (units[u][0] + 1) * TILE

    def stacked(ref, s, u):
        index, group = units[u]
        part = tile_rows(s * tiles + index)
        return jnp.concatenate(
            [
                ref[part, h * width : (h + 1) * width]
                for h in range(group * HEADS_AT_ONCE, (group + 1) * HEADS_AT_ONCE)
            ],
            axis=0,
        )

    def fold(x, how):
        return how(x.reshape(x.shape[0] // 8, 8, x.shape[1]), axis=0)

    def biased(buf, c, columns):
        block = scores[buf, c : c + PIECE, :]
        if c >= prompt_len:
            bias = live_bias[c - prompt_len : c - prompt_len + PIECE, :]
            if c >= columns - TILE:
                first = c - (columns - TILE)
                bias = bias + causal_bias[first : first + PIECE, :]
            block = block + jnp.concatenate([bias] * HEADS_AT_ONCE, axis=1)
        return block

    def chunks(columns):
        return [slice(c, c + CHUNK) for c in range(0, columns, CHUNK)]

    def head(s, u, out):
        index, group = units[u]
        columns, buf = columns_of(u), u % 2
        if group == 0:
            q_copy(s * tiles + index).wait()
            g_copy(s * tiles + index).wait()
        q, g = stacked(q_all, s, u), stacked(g_all, s, u)
        top = None
        for rows_ in chunks(columns):
            scores[buf, rows_, :] = lax.dot_general(
                keys[rows_, :], q, ACROSS, preferred_element_type=jnp.float32
            )
            yield
            for c in range(rows_.start, rows_.stop, PIECE):
                high = fold(biased(buf, c, columns), jnp.max)
                top = high if top is None else jnp.maximum(top, high)
            dprobs[buf, rows_, :] = lax.dot_general(
                values[rows_, :], g, ACROSS, preferred_element_type=jnp.float32
            )
            yield
        out["top"] = jnp.max(top, axis=0, keepdims=True) * EXP2_SCALE

    def head_steps(u):
        return 2 * len(chunks(columns_of(u)))

    def middle(s, u, top, out):
        index, _ = units[u]
        buf, columns = u % 2, columns_of(u)
        total = jnp.zeros((8, wide), jnp.float32)
        weighted = jnp.zeros((8, wide), jnp.float32)
        for c, size in spans(columns):
            e = jnp.exp2(biased(buf, c, columns) * EXP2_SCALE - top)
            scores[buf, c : c + size, :] = e
            total = total + fold(e, jnp.sum)
            weighted = weighted + fold(e * dprobs[buf, c : c + size, :], jnp.sum)
            yield
        row = index * TILE + lax.broadcasted_iota(jnp.int32, (1, TILE), 1)
        live = (row >= begin_ref[s]) & (row < begin_ref[s] + length_ref[s])
        live = jnp.concatenate([live] * HEADS_AT_ONCE, axis=1)
        total = jnp.sum(total, axis=0, keepdims=True)
        out["inverse"] = jnp.where(live, 1.0 / total, 0.0)
        out["delta"] = jnp.sum(weighted, axis=0, keepdims=True) * out["inverse"]

    def tail(u, inverse, delta):
        buf = u % 2
        for c, size in spans(columns_of(u)):
            p = scores[buf, c : c + size, :] * inverse
            prob16[buf, c : c + size, :] = p.astype(jnp.bfloat16)
            ds = p * (dprobs[buf, c : c + size, :] - delta)
            dscore16[buf, c : c + size, :] = ds.astype(jnp.bfloat16)
            yield

    def pass_steps(u):
        return len(spans(columns_of(u)))

    def flush_columns(s, u):
        q, g = stacked(q_all, s, u), stacked(g_all, s, u)
        for rows_ in chunks(columns_of(u)):
            kt[rows_, :] += jnp.dot(dscore16[u % 2, rows_, :], q, preferred_element_type=jnp.float32)
            yield
            vt[rows_, :] += jnp.dot(prob16[u % 2, rows_, :], g, preferred_element_type=jnp.float32)
            yield

    def flush_queries(s, u):
        index, group = units[u]
        columns = columns_of(u)
        part = tile_rows(s * tiles + index)
        for h in range(0, HEADS_AT_ONCE, 2):
            lanes = slice(h * TILE, (h + 2) * TILE)
            dqt = jnp.dot(
                keys_t[:, 0:columns], dscore16[u % 2, 0:columns, lanes], preferred_element_type=jnp.float32
            )
            yield
            for side in range(2):
                first = (group * HEADS_AT_ONCE + h + side) * width
                dq = dqt[:, side * TILE : (side + 1) * TILE].T
                dq_all[part, first : first + width] = dq * score_scale
            yield
        if group == groups - 1:
            dq_copy(s * tiles + index).start()

    def together(*steps):
        steps = [[generator, count, 0] for generator, count in steps]
        while steps:
            step = min(steps, key=lambda step: step[2] / step[1])
            step[2] += 1
            if next(step[0], steps) is steps:
                steps.remove(step)

    def slot_units(s):
        now, ahead = {}, {}
        together((head(s, 0, ahead), head_steps(0)))
        for u in range(len(units)):
            first, second = [], []
            if u >= 1:
                first = [(flush_columns(s, u - 1), head_steps(u - 1))]
                second = [(flush_queries(s, u - 1), HEADS_AT_ONCE)]
            together((middle(s, u, ahead["top"], now), pass_steps(u)), *first)
            if u + 1 < len(units):
                second = [(head(s, u + 1, ahead), head_steps(u + 1))] + second
            together((tail(u, now["inverse"], now["delta"]), pass_steps(u)), *second)
        last = len(units) - 1
        together((flush_columns(s, last), head_steps(last)), (flush_queries(s, last), HEADS_AT_ONCE))

    @pl.loop(0, slots)
    def _(s):
        first_block = prompt_ref[s] * OWNERS
        for o in range(OWNERS):
            source = pl.ds(pl.multiple_of(place[first_block + o] * prow, prow), prow)
            keys[o * prow : (o + 1) * prow, :] = kv[source, 0:width]
            values[o * prow : (o + 1) * prow, :] = kv[source, width : 2 * width]
        keys[prompt_len:, :] = rk_all[slot_part(s), :]
        values[prompt_len:, :] = rv_all[slot_part(s), :]
        keys_t[...] = keys[...].astype(jnp.float32).T.astype(jnp.bfloat16)
        column = lax.broadcasted_iota(jnp.int32, (slot_rows, TILE), 0)
        live_bias[...] = jnp.where(column >= begin_ref[s], 0.0, MASKED)
        kt[...] = jnp.zeros_like(kt)
        vt[...] = jnp.zeros_like(vt)
        slot_units(s)
        drk_all[slot_part(s), :] = kt[prompt_len:, :] * score_scale
        drv_all[slot_part(s), :] = vt[prompt_len:, :]
        drk_copy(s).start()
        drv_copy(s).start()
        for o in range(OWNERS):
            start = block_position(place[first_block + o], me, n) * prow
            target = pl.ds(pl.multiple_of(start, prow), prow)
            block = slice(o * prow, (o + 1) * prow)
            term_ref[target, 0:width] += kt[block, :] * score_scale
            term_ref[target, width : 2 * width] += vt[block, :]

    for copy in term_copies:
        copy.start()
    for copy in term_copies:
        copy.wait()
    for chunk in range(slots * tiles):
        dq_copy(chunk).wait()
    for s in range(slots):
        drk_copy(s).wait()
        drv_copy(s).wait()


def slot_grads(queries, resp_keys, resp_values, out_grad, all_kv, prompts, lengths, begins, holders):
    slots = prompts.shape[0]
    rows, columns = queries.shape
    slot_rows, width = rows // slots, resp_keys.shape[1]
    n = holders.shape[0]
    prow = all_kv.shape[0] // n
    total = prow * OWNERS + slot_rows
    tiles = slot_rows // TILE
    hbm = pl.BlockSpec(memory_space=pltpu.HBM)
    f32, bf16 = jnp.float32, jnp.bfloat16
    return pl.pallas_call(
        grad_kernel,
        in_specs=[hbm] * 9,
        out_specs=[hbm] * 5,
        out_shape=[
            jax.ShapeDtypeStruct((rows, columns), f32),
            jax.ShapeDtypeStruct((rows, width), f32),
            jax.ShapeDtypeStruct((rows, width), f32),
            jax.ShapeDtypeStruct((n * prow // 2, 2 * width), f32),
            jax.ShapeDtypeStruct((n * prow // 2, 2 * width), f32),
        ],
        scratch_shapes=[
            pltpu.SMEM((slots,), jnp.int32),
            pltpu.SMEM((slots,), jnp.int32),
            pltpu.SMEM((slots,), jnp.int32),
            pltpu.SMEM((n,), jnp.int32),
            pltpu.SMEM((n,), jnp.int32),
            pltpu.VMEM((rows, columns), bf16),
            pltpu.VMEM((rows, columns), bf16),
            pltpu.VMEM((rows, width), bf16),
            pltpu.VMEM((rows, width), bf16),
            pltpu.VMEM((rows, columns), f32),
            pltpu.VMEM((rows, width), f32),
            pltpu.VMEM((rows, width), f32),
            pltpu.VMEM((n * prow, 2 * width), bf16),
            pltpu.VMEM((n * prow, 2 * width), f32),
            pltpu.VMEM((total, width), bf16),
            pltpu.VMEM((total, width), bf16),
            pltpu.VMEM((width, total), bf16),
            pltpu.VMEM((slot_rows, TILE), f32),
            pltpu.VMEM((TILE, TILE), f32),
            pltpu.VMEM((2, total, HEADS_AT_ONCE * TILE), f32),
            pltpu.VMEM((2, total, HEADS_AT_ONCE * TILE), f32),
            pltpu.VMEM((2, total, HEADS_AT_ONCE * TILE), bf16),
            pltpu.VMEM((2, total, HEADS_AT_ONCE * TILE), bf16),
            pltpu.VMEM((total, width), f32),
            pltpu.VMEM((total, width), f32),
            pltpu.SemaphoreType.DMA((4,)),
            pltpu.SemaphoreType.DMA((2,)),
            pltpu.SemaphoreType.DMA((slots * tiles,)),
            pltpu.SemaphoreType.DMA((slots * tiles,)),
            pltpu.SemaphoreType.DMA((slots * tiles,)),
            pltpu.SemaphoreType.DMA((slots,)),
            pltpu.SemaphoreType.DMA((slots,)),
            pltpu.SemaphoreType.DMA((1,)),
            pltpu.SemaphoreType.DMA((2,)),
        ],
        compiler_params=pltpu.CompilerParams(vmem_limit_bytes=60 * 1024 * 1024),
    )(prompts, lengths, begins, holders, queries, out_grad, resp_keys, resp_values, all_kv)


def body(
    n,
    queries,
    resp_keys,
    resp_values,
    out_grad,
    prompt_keys,
    prompt_values,
    slot_prompt,
    slot_length,
    slot_begin,
    block_prompt,
):
    width = resp_keys.shape[1]
    prow = prompt_keys.shape[0]
    own = jnp.pad(prompt_keys, ((0, 0), (0, width))) + jnp.pad(prompt_values, ((0, 0), (width, 0)))
    own = jnp.broadcast_to(own[None], (n, prow, 2 * width)).reshape(-1, 2 * width)
    all_kv = lax.all_to_all(own, "seq", split_axis=0, concat_axis=0, tiled=True)
    query_grad, key_grad, value_grad, own_term, other_term = slot_grads(
        queries, resp_keys, resp_values, out_grad, all_kv,
        slot_prompt, slot_length, slot_begin, block_prompt,
    )
    parts = exchange(own_term + swap_cores(other_term, n), n)
    owned = jnp.sum(parts.reshape(n // 2, prow, 2 * width), axis=0)
    return query_grad, key_grad, value_grad, owned[:, :width], owned[:, width:]


def solution(mesh):
    n = mesh.shape["seq"]
    rows = P(("groups", "seq"), None)
    slots = P(("groups", "seq"))
    return jax.shard_map(
        functools.partial(body, n),
        mesh=mesh,
        in_specs=(rows,) * 6 + (slots,) * 3 + (P("groups"),),
        out_specs=(rows,) * 5,
        check_vma=False,
    )
```

```python
import functools
import math

import jax
import jax.numpy as jnp
from jax import lax
from jax.experimental import pallas as pl
from jax.experimental.pallas import tpu as pltpu
from jax.sharding import PartitionSpec as P

OWNERS = 8
TILE = 128
PIECE = 16
score_scale = 0.08838834764831845
EXP2_SCALE = score_scale * math.log2(math.e)
MASKED = -1e30

ACROSS = (((1,), (1,)), ((), ()))


def same_core_groups(n):
    return [list(range(core, n, 2)) for core in range(2)]


def swap_cores(x, n):
    return lax.ppermute(x, "seq", [(i, i ^ 1) for i in range(n)])


def exchange(x, n):
    return lax.all_to_all(
        x, "seq", split_axis=0, concat_axis=0, axis_index_groups=same_core_groups(n), tiled=True
    )


def block_position(holder, me, n):
    return ((holder ^ me) & 1) * (n // 2) + (holder >> 1)


def grad_kernel(
    prompt_hbm,
    length_hbm,
    begin_hbm,
    holder_hbm,
    q_hbm,
    g_hbm,
    rk_hbm,
    rv_hbm,
    own_hbm,
    other_hbm,
    dq_hbm,
    drk_hbm,
    drv_hbm,
    own_term_hbm,
    other_term_hbm,
    prompt_ref,
    length_ref,
    begin_ref,
    holder_ref,
    place,
    q_all,
    g_all,
    rk_all,
    rv_all,
    dq_all,
    drk_all,
    drv_all,
    kv,
    term_ref,
    keys,
    values,
    keys_t,
    live_bias,
    causal_bias,
    exps,
    dprobs,
    prob16,
    dscore16,
    kt,
    vt,
    sem_scalar,
    sem_resp,
    sem_q,
    sem_g,
    sem_dq,
    sem_drk,
    sem_drv,
    sem_kv,
    sem_term,
):
    n = holder_ref.shape[0]
    slots = prompt_ref.shape[0]
    rows, width = rk_all.shape
    slot_rows = rows // slots
    tiles = slot_rows // TILE
    prow = term_ref.shape[0] // n
    prompt_len = prow * OWNERS
    heads = q_all.shape[1] // width
    me = lax.axis_index("seq")

    scalar_copies = [
        pltpu.make_async_copy(src, dst, sem_scalar.at[i])
        for i, (src, dst) in enumerate(
            [
                (prompt_hbm, prompt_ref),
                (length_hbm, length_ref),
                (begin_hbm, begin_ref),
                (holder_hbm, holder_ref),
            ]
        )
    ]
    resp_copies = [
        pltpu.make_async_copy(rk_hbm, rk_all, sem_resp.at[0]),
        pltpu.make_async_copy(rv_hbm, rv_all, sem_resp.at[1]),
    ]

    def tile_rows(chunk):
        return pl.ds(pl.multiple_of(chunk * TILE, TILE), TILE)

    def q_copy(chunk):
        part = tile_rows(chunk)
        return pltpu.make_async_copy(q_hbm.at[part], q_all.at[part], sem_q.at[chunk])

    def g_copy(chunk):
        part = tile_rows(chunk)
        return pltpu.make_async_copy(g_hbm.at[part], g_all.at[part], sem_g.at[chunk])

    def dq_copy(chunk):
        part = tile_rows(chunk)
        return pltpu.make_async_copy(dq_all.at[part], dq_hbm.at[part], sem_dq.at[chunk])

    def slot_part(s):
        return pl.ds(pl.multiple_of(s * slot_rows, slot_rows), slot_rows)

    def drk_copy(s):
        return pltpu.make_async_copy(
            drk_all.at[slot_part(s)], drk_hbm.at[slot_part(s)], sem_drk.at[s]
        )

    def drv_copy(s):
        return pltpu.make_async_copy(
            drv_all.at[slot_part(s)], drv_hbm.at[slot_part(s)], sem_drv.at[s]
        )

    half_rows = term_ref.shape[0] // 2
    kv_copies = [
        pltpu.make_async_copy(src, kv.at[pl.ds(i * half_rows, half_rows)], sem_kv.at[i])
        for i, src in enumerate([own_hbm, other_hbm])
    ]
    term_copies = [
        pltpu.make_async_copy(term_ref.at[pl.ds(i * half_rows, half_rows)], dst, sem_term.at[i])
        for i, dst in enumerate([own_term_hbm, other_term_hbm])
    ]
    for copy in scalar_copies + kv_copies + resp_copies:
        copy.start()
    for chunk in range(slots * tiles):
        q_copy(chunk).start()
        g_copy(chunk).start()

    term_ref[...] = jnp.zeros_like(term_ref)
    causal_bias[...] = jnp.where(
        lax.broadcasted_iota(jnp.int32, (TILE, TILE), 0)
        <= lax.broadcasted_iota(jnp.int32, (TILE, TILE), 1),
        0.0,
        MASKED,
    )
    for copy in scalar_copies + kv_copies + resp_copies:
        copy.wait()

    @pl.loop(0, n)
    def _(j):
        place[holder_ref[j]] = j

    half = heads // 2
    wide = 2 * TILE
    units = [(index, pair) for index in range(tiles) for pair in range(half)]

    def columns_of(u):
        return prompt_len + (units[u][0] + 1) * TILE

    def chunks(u):
        return range(0, columns_of(u), TILE)

    def stacked(ref, s, index, first, count):
        part = tile_rows(s * tiles + index)
        return jnp.concatenate(
            [ref[part, (first + h) * width : (first + h + 1) * width] for h in range(count)], axis=0
        )

    def fold(x, how):
        return how(how(x.reshape(x.shape[0] // 8, 8, x.shape[1]), axis=0), axis=0, keepdims=True)

    def head(s, u, out):
        index, pair = units[u]
        columns, buf = columns_of(u), u % 2
        if pair == 0:
            q_copy(s * tiles + index).wait()
            g_copy(s * tiles + index).wait()
        q2 = stacked(q_all, s, index, 2 * pair, 2)
        g2 = stacked(g_all, s, index, 2 * pair, 2)
        tops, totals, weights = [], [], []
        for c in chunks(u):
            part = slice(c, c + TILE)
            block = lax.dot_general(keys[part, :], q2, ACROSS, preferred_element_type=jnp.float32)
            if c >= prompt_len:
                bias = live_bias[c - prompt_len : c - prompt_len + TILE, :]
                if c + TILE == columns:
                    bias = bias + causal_bias[...]
                block = block + jnp.concatenate([bias, bias], axis=1)
            top = fold(block, jnp.max) * EXP2_SCALE
            e = jnp.exp2(block * EXP2_SCALE - top)
            exps[buf, part, :] = e
            yield
            d = lax.dot_general(values[part, :], g2, ACROSS, preferred_element_type=jnp.float32)
            dprobs[buf, part, :] = d
            tops.append(top)
            totals.append(fold(e, jnp.sum))
            weights.append(fold(e * d, jnp.sum))
            yield
        top = functools.reduce(jnp.maximum, tops)
        factors = [jnp.exp2(part - top) for part in tops]
        total = functools.reduce(jnp.add, [f * x for f, x in zip(factors, totals)])
        weighted = functools.reduce(jnp.add, [f * x for f, x in zip(factors, weights)])
        row = index * TILE + lax.broadcasted_iota(jnp.int32, (1, TILE), 1)
        live = (row >= begin_ref[s]) & (row < begin_ref[s] + length_ref[s])
        inverse = jnp.where(jnp.concatenate([live, live], axis=1), 1.0 / total, 0.0)
        out["delta"] = weighted * inverse
        out["factors"] = [f * inverse for f in factors]

    def tail(u, stats):
        buf, group = u % 2, (u // 2) % 2
        lanes = slice((u % 2) * wide, (u % 2 + 1) * wide)
        delta = stats["delta"]
        for c, factor in zip(chunks(u), stats["factors"]):
            for first in range(c, c + TILE, PIECE):
                part = slice(first, first + PIECE)
                p = exps[buf, part, :] * factor
                prob16[group, part, lanes] = p.astype(jnp.bfloat16)
                ds = p * (dprobs[buf, part, :] - delta)
                dscore16[group, part, lanes] = ds.astype(jnp.bfloat16)
            yield

    def flush_keys(s, u):
        index, pair = units[u]
        group, columns = (u // 2) % 2, columns_of(u)
        q4 = stacked(q_all, s, index, 2 * (pair - 1), 4)
        kt[0:columns, :] += jnp.dot(
            dscore16[group, 0:columns, :], q4, preferred_element_type=jnp.float32
        )
        yield

    def flush_values(s, u):
        index, pair = units[u]
        group, columns = (u // 2) % 2, columns_of(u)
        g4 = stacked(g_all, s, index, 2 * (pair - 1), 4)
        vt[0:columns, :] += jnp.dot(
            prob16[group, 0:columns, :], g4, preferred_element_type=jnp.float32
        )
        yield

    def flush_queries(s, u):
        index, pair = units[u]
        group, columns = (u // 2) % 2, columns_of(u)
        part = tile_rows(s * tiles + index)
        for side in range(2):
            ds = dscore16[group, 0:columns, side * wide : (side + 1) * wide]
            dqt = jnp.dot(keys_t[:, 0:columns], ds, preferred_element_type=jnp.float32)
            for h in range(2):
                first = (2 * (pair - 1 + side) + h) * width
                dq_all[part, first : first + width] = dqt[:, h * TILE : (h + 1) * TILE].T * score_scale
            yield
        if pair == half - 1:
            dq_copy(s * tiles + index).start()

    def together(*steps):
        steps = list(steps)
        while steps:
            for step in list(steps):
                if next(step, steps) is steps:
                    steps.remove(step)

    def slot_units(s):
        stats = {}
        together(head(s, 0, stats))
        for u in range(len(units)):
            now, stats = stats, {}
            steps = []
            if u + 1 < len(units):
                steps.append(head(s, u + 1, stats))
            steps.append(tail(u, now))
            if u >= 2 and u % 2 == 0:
                steps += [flush_keys(s, u - 1), flush_queries(s, u - 1)]
            elif u >= 2:
                steps.append(flush_values(s, u - 2))
            together(*steps)
        last = len(units) - 1
        together(flush_keys(s, last), flush_values(s, last), flush_queries(s, last))

    @pl.loop(0, slots)
    def _(s):
        first_block = prompt_ref[s] * OWNERS
        for o in range(OWNERS):
            start = block_position(place[first_block + o], me, n) * prow
            source = pl.ds(pl.multiple_of(start, prow), prow)
            keys[o * prow : (o + 1) * prow, :] = kv[source, 0:width]
            values[o * prow : (o + 1) * prow, :] = kv[source, width : 2 * width]
        keys[prompt_len:, :] = rk_all[slot_part(s), :]
        values[prompt_len:, :] = rv_all[slot_part(s), :]
        keys_t[...] = keys[...].astype(jnp.float32).T.astype(jnp.bfloat16)
        column = lax.broadcasted_iota(jnp.int32, (slot_rows, TILE), 0)
        live_bias[...] = jnp.where(column >= begin_ref[s], 0.0, MASKED)
        kt[...] = jnp.zeros_like(kt)
        vt[...] = jnp.zeros_like(vt)
        slot_units(s)
        drk_all[slot_part(s), :] = kt[prompt_len:, :] * score_scale
        drv_all[slot_part(s), :] = vt[prompt_len:, :]
        drk_copy(s).start()
        drv_copy(s).start()
        for o in range(OWNERS):
            start = block_position(place[first_block + o], me, n) * prow
            target = pl.ds(pl.multiple_of(start, prow), prow)
            block = slice(o * prow, (o + 1) * prow)
            term_ref[target, 0:width] += kt[block, :] * score_scale
            term_ref[target, width : 2 * width] += vt[block, :]

    for copy in term_copies:
        copy.start()
    for copy in term_copies:
        copy.wait()
    for chunk in range(slots * tiles):
        dq_copy(chunk).wait()
    for s in range(slots):
        drk_copy(s).wait()
        drv_copy(s).wait()


def slot_grads(queries, resp_keys, resp_values, out_grad, own_kv, other_kv, prompts, lengths, begins, holders):
    slots = prompts.shape[0]
    rows, columns = queries.shape
    slot_rows, width = rows // slots, resp_keys.shape[1]
    n = holders.shape[0]
    prow = 2 * own_kv.shape[0] // n
    total = prow * OWNERS + slot_rows
    tiles = slot_rows // TILE
    hbm = pl.BlockSpec(memory_space=pltpu.HBM)
    f32, bf16 = jnp.float32, jnp.bfloat16
    return pl.pallas_call(
        grad_kernel,
        in_specs=[hbm] * 10,
        out_specs=[hbm] * 5,
        out_shape=[
            jax.ShapeDtypeStruct((rows, columns), f32),
            jax.ShapeDtypeStruct((rows, width), f32),
            jax.ShapeDtypeStruct((rows, width), f32),
            jax.ShapeDtypeStruct((n * prow // 2, 2 * width), f32),
            jax.ShapeDtypeStruct((n * prow // 2, 2 * width), f32),
        ],
        scratch_shapes=[
            pltpu.SMEM((slots,), jnp.int32),
            pltpu.SMEM((slots,), jnp.int32),
            pltpu.SMEM((slots,), jnp.int32),
            pltpu.SMEM((n,), jnp.int32),
            pltpu.SMEM((n,), jnp.int32),
            pltpu.VMEM((rows, columns), bf16),
            pltpu.VMEM((rows, columns), bf16),
            pltpu.VMEM((rows, width), bf16),
            pltpu.VMEM((rows, width), bf16),
            pltpu.VMEM((rows, columns), f32),
            pltpu.VMEM((rows, width), f32),
            pltpu.VMEM((rows, width), f32),
            pltpu.VMEM((n * prow, 2 * width), bf16),
            pltpu.VMEM((n * prow, 2 * width), f32),
            pltpu.VMEM((total, width), bf16),
            pltpu.VMEM((total, width), bf16),
            pltpu.VMEM((width, total), bf16),
            pltpu.VMEM((slot_rows, TILE), f32),
            pltpu.VMEM((TILE, TILE), f32),
            pltpu.VMEM((2, total, 2 * TILE), f32),
            pltpu.VMEM((2, total, 2 * TILE), f32),
            pltpu.VMEM((2, total, 4 * TILE), bf16),
            pltpu.VMEM((2, total, 4 * TILE), bf16),
            pltpu.VMEM((total, width), f32),
            pltpu.VMEM((total, width), f32),
            pltpu.SemaphoreType.DMA((4,)),
            pltpu.SemaphoreType.DMA((2,)),
            pltpu.SemaphoreType.DMA((slots * tiles,)),
            pltpu.SemaphoreType.DMA((slots * tiles,)),
            pltpu.SemaphoreType.DMA((slots * tiles,)),
            pltpu.SemaphoreType.DMA((slots,)),
            pltpu.SemaphoreType.DMA((slots,)),
            pltpu.SemaphoreType.DMA((2,)),
            pltpu.SemaphoreType.DMA((2,)),
        ],
        compiler_params=pltpu.CompilerParams(vmem_limit_bytes=60 * 1024 * 1024),
    )(prompts, lengths, begins, holders, queries, out_grad, resp_keys, resp_values, own_kv, other_kv)


def body(
    n,
    queries,
    resp_keys,
    resp_values,
    out_grad,
    prompt_keys,
    prompt_values,
    slot_prompt,
    slot_length,
    slot_begin,
    block_prompt,
):
    width = resp_keys.shape[1]
    prow = prompt_keys.shape[0]
    own = jnp.pad(prompt_keys, ((0, 0), (0, width))) + jnp.pad(prompt_values, ((0, 0), (width, 0)))
    own = jnp.broadcast_to(own[None], (n // 2, prow, 2 * width)).reshape(-1, 2 * width)
    own_kv = exchange(own, n)
    other_kv = swap_cores(own_kv, n)
    query_grad, key_grad, value_grad, own_term, other_term = slot_grads(
        queries, resp_keys, resp_values, out_grad, own_kv, other_kv,
        slot_prompt, slot_length, slot_begin, block_prompt,
    )
    parts = exchange(own_term + swap_cores(other_term, n), n)
    owned = jnp.sum(parts.reshape(n // 2, prow, 2 * width), axis=0)
    return query_grad, key_grad, value_grad, owned[:, :width], owned[:, width:]


def solution(mesh):
    n = mesh.shape["seq"]
    rows = P(("groups", "seq"), None)
    slots = P(("groups", "seq"))
    return jax.shard_map(
        functools.partial(body, n),
        mesh=mesh,
        in_specs=(rows,) * 6 + (slots,) * 3 + (P("groups"),),
        out_specs=(rows,) * 5,
        check_vma=False,
    )
```

```python
import functools
import math

import jax
import jax.numpy as jnp
from jax import lax
from jax.experimental import pallas as pl
from jax.experimental.pallas import tpu as pltpu
from jax.sharding import PartitionSpec as P

OWNERS = 8
TILE = 128
PIECE = 16
score_scale = 0.08838834764831845
EXP2_SCALE = score_scale * math.log2(math.e)
MASKED = -1e30


def same_core_groups(n):
    return [list(range(core, n, 2)) for core in range(2)]


def swap_cores(x, n):
    return lax.ppermute(x, "seq", [(i, i ^ 1) for i in range(n)])


def exchange(x, n):
    return lax.all_to_all(
        x, "seq", split_axis=0, concat_axis=0, axis_index_groups=same_core_groups(n), tiled=True
    )


def block_position(holder, me, n):
    return ((holder ^ me) & 1) * (n // 2) + (holder >> 1)


def grad_kernel(
    prompt_hbm,
    length_hbm,
    begin_hbm,
    holder_hbm,
    q_hbm,
    g_hbm,
    rk_hbm,
    rv_hbm,
    own_hbm,
    other_hbm,
    dq_hbm,
    drk_hbm,
    drv_hbm,
    own_term_hbm,
    other_term_hbm,
    prompt_ref,
    length_ref,
    begin_ref,
    holder_ref,
    place,
    q_all,
    g_all,
    rk_all,
    rv_all,
    dq_all,
    drk_all,
    drv_all,
    kv,
    term_ref,
    keys,
    values,
    keys_t,
    live_bias,
    causal_bias,
    turned,
    exps,
    dprobs,
    prob16,
    dscore16,
    kt,
    vt,
    sem_scalar,
    sem_resp,
    sem_q,
    sem_g,
    sem_dq,
    sem_drk,
    sem_drv,
    sem_kv,
    sem_term,
):
    n = holder_ref.shape[0]
    slots = prompt_ref.shape[0]
    rows, width = rk_all.shape
    slot_rows = rows // slots
    tiles = slot_rows // TILE
    prow = term_ref.shape[0] // n
    prompt_len = prow * OWNERS
    heads = q_all.shape[1] // width
    me = lax.axis_index("seq")

    scalar_copies = [
        pltpu.make_async_copy(src, dst, sem_scalar.at[i])
        for i, (src, dst) in enumerate(
            [
                (prompt_hbm, prompt_ref),
                (length_hbm, length_ref),
                (begin_hbm, begin_ref),
                (holder_hbm, holder_ref),
            ]
        )
    ]
    resp_copies = [
        pltpu.make_async_copy(rk_hbm, rk_all, sem_resp.at[0]),
        pltpu.make_async_copy(rv_hbm, rv_all, sem_resp.at[1]),
    ]

    def tile_rows(chunk):
        return pl.ds(pl.multiple_of(chunk * TILE, TILE), TILE)

    def q_copy(chunk):
        part = tile_rows(chunk)
        return pltpu.make_async_copy(q_hbm.at[part], q_all.at[part], sem_q.at[chunk])

    def g_copy(chunk):
        part = tile_rows(chunk)
        return pltpu.make_async_copy(g_hbm.at[part], g_all.at[part], sem_g.at[chunk])

    def dq_copy(chunk):
        part = tile_rows(chunk)
        return pltpu.make_async_copy(dq_all.at[part], dq_hbm.at[part], sem_dq.at[chunk])

    def slot_part(s):
        return pl.ds(pl.multiple_of(s * slot_rows, slot_rows), slot_rows)

    def drk_copy(s):
        return pltpu.make_async_copy(
            drk_all.at[slot_part(s)], drk_hbm.at[slot_part(s)], sem_drk.at[s]
        )

    def drv_copy(s):
        return pltpu.make_async_copy(
            drv_all.at[slot_part(s)], drv_hbm.at[slot_part(s)], sem_drv.at[s]
        )

    half_rows = term_ref.shape[0] // 2
    kv_copies = [
        pltpu.make_async_copy(src, kv.at[pl.ds(i * half_rows, half_rows)], sem_kv.at[i])
        for i, src in enumerate([own_hbm, other_hbm])
    ]
    term_copies = [
        pltpu.make_async_copy(term_ref.at[pl.ds(i * half_rows, half_rows)], dst, sem_term.at[i])
        for i, dst in enumerate([own_term_hbm, other_term_hbm])
    ]
    for copy in scalar_copies + kv_copies + resp_copies:
        copy.start()
    for chunk in range(slots * tiles):
        q_copy(chunk).start()
        g_copy(chunk).start()

    term_ref[...] = jnp.zeros_like(term_ref)
    causal_bias[...] = jnp.where(
        lax.broadcasted_iota(jnp.int32, (TILE, TILE), 0)
        <= lax.broadcasted_iota(jnp.int32, (TILE, TILE), 1),
        0.0,
        MASKED,
    )
    for copy in scalar_copies + kv_copies + resp_copies:
        copy.wait()

    @pl.loop(0, n)
    def _(j):
        place[holder_ref[j]] = j

    half = heads // 2
    wide = 2 * TILE
    units = [(index, pair) for index in range(tiles) for pair in range(half)]

    def columns_of(u):
        return prompt_len + (units[u][0] + 1) * TILE

    def chunks(u):
        return range(0, columns_of(u), TILE)

    def stacked(ref, s, index, first, count):
        part = tile_rows(s * tiles + index)
        return jnp.concatenate(
            [ref[part, (first + h) * width : (first + h + 1) * width] for h in range(count)], axis=0
        )

    def fold(x, how):
        return how(how(x.reshape(x.shape[0] // 8, 8, x.shape[1]), axis=0), axis=0, keepdims=True)

    def head(s, u, out):
        index, pair = units[u]
        columns, buf = columns_of(u), u % 2
        if pair == 0:
            q_copy(s * tiles + index).wait()
            g_copy(s * tiles + index).wait()
        q2t, g2t = turned.at[buf, 0], turned.at[buf, 1]
        q2t[...] = stacked(q_all, s, index, 2 * pair, 2).T
        g2t[...] = stacked(g_all, s, index, 2 * pair, 2).T
        tops, totals, weights = [], [], []
        for c in chunks(u):
            part = slice(c, c + TILE)
            block = jnp.dot(keys[part, :], q2t[...], preferred_element_type=jnp.float32)
            if c >= prompt_len:
                bias = live_bias[c - prompt_len : c - prompt_len + TILE, :]
                if c + TILE == columns:
                    bias = bias + causal_bias[...]
                block = block + jnp.concatenate([bias, bias], axis=1)
            top = fold(block, jnp.max) * EXP2_SCALE
            e = jnp.exp2(block * EXP2_SCALE - top)
            exps[buf, part, :] = e
            yield
            d = jnp.dot(values[part, :], g2t[...], preferred_element_type=jnp.float32)
            dprobs[buf, part, :] = d
            tops.append(top)
            totals.append(fold(e, jnp.sum))
            weights.append(fold(e * d, jnp.sum))
            yield
        top = functools.reduce(jnp.maximum, tops)
        factors = [jnp.exp2(part - top) for part in tops]
        total = functools.reduce(jnp.add, [f * x for f, x in zip(factors, totals)])
        weighted = functools.reduce(jnp.add, [f * x for f, x in zip(factors, weights)])
        row = index * TILE + lax.broadcasted_iota(jnp.int32, (1, TILE), 1)
        live = (row >= begin_ref[s]) & (row < begin_ref[s] + length_ref[s])
        inverse = jnp.where(jnp.concatenate([live, live], axis=1), 1.0 / total, 0.0)
        out["delta"] = weighted * inverse
        out["factors"] = [f * inverse for f in factors]

    def tail(u, stats):
        buf, group = u % 2, (u // 2) % 2
        lanes = slice((u % 2) * wide, (u % 2 + 1) * wide)
        delta = stats["delta"]
        for c, factor in zip(chunks(u), stats["factors"]):
            for first in range(c, c + TILE, PIECE):
                part = slice(first, first + PIECE)
                p = exps[buf, part, :] * factor
                prob16[group, part, lanes] = p.astype(jnp.bfloat16)
                ds = p * (dprobs[buf, part, :] - delta)
                dscore16[group, part, lanes] = ds.astype(jnp.bfloat16)
            yield

    def flush_keys(s, u):
        index, pair = units[u]
        group, columns = (u // 2) % 2, columns_of(u)
        q4 = stacked(q_all, s, index, 2 * (pair - 1), 4)
        kt[0:columns, :] += jnp.dot(
            dscore16[group, 0:columns, :], q4, preferred_element_type=jnp.float32
        )
        yield

    def flush_values(s, u):
        index, pair = units[u]
        group, columns = (u // 2) % 2, columns_of(u)
        g4 = stacked(g_all, s, index, 2 * (pair - 1), 4)
        vt[0:columns, :] += jnp.dot(
            prob16[group, 0:columns, :], g4, preferred_element_type=jnp.float32
        )
        yield

    def flush_queries(s, u):
        index, pair = units[u]
        group, columns = (u // 2) % 2, columns_of(u)
        part = tile_rows(s * tiles + index)
        for side in range(2):
            ds = dscore16[group, 0:columns, side * wide : (side + 1) * wide]
            dqt = jnp.dot(keys_t[:, 0:columns], ds, preferred_element_type=jnp.float32)
            for h in range(2):
                first = (2 * (pair - 1 + side) + h) * width
                dq_all[part, first : first + width] = dqt[:, h * TILE : (h + 1) * TILE].T * score_scale
            yield
        if pair == half - 1:
            dq_copy(s * tiles + index).start()

    def together(*steps):
        steps = list(steps)
        while steps:
            for step in list(steps):
                if next(step, steps) is steps:
                    steps.remove(step)

    def slot_units(s):
        stats = {}
        together(head(s, 0, stats))
        for u in range(len(units)):
            now, stats = stats, {}
            steps = []
            if u + 1 < len(units):
                steps.append(head(s, u + 1, stats))
            steps.append(tail(u, now))
            if u >= 2 and u % 2 == 0:
                steps += [flush_keys(s, u - 1), flush_queries(s, u - 1)]
            elif u >= 2:
                steps.append(flush_values(s, u - 2))
            together(*steps)
        last = len(units) - 1
        together(flush_keys(s, last), flush_values(s, last), flush_queries(s, last))

    @pl.loop(0, slots)
    def _(s):
        first_block = prompt_ref[s] * OWNERS
        for o in range(OWNERS):
            start = block_position(place[first_block + o], me, n) * prow
            source = pl.ds(pl.multiple_of(start, prow), prow)
            keys[o * prow : (o + 1) * prow, :] = kv[source, 0:width]
            values[o * prow : (o + 1) * prow, :] = kv[source, width : 2 * width]
        keys[prompt_len:, :] = rk_all[slot_part(s), :]
        values[prompt_len:, :] = rv_all[slot_part(s), :]
        keys_t[...] = keys[...].astype(jnp.float32).T.astype(jnp.bfloat16)
        column = lax.broadcasted_iota(jnp.int32, (slot_rows, TILE), 0)
        live_bias[...] = jnp.where(column >= begin_ref[s], 0.0, MASKED)
        kt[...] = jnp.zeros_like(kt)
        vt[...] = jnp.zeros_like(vt)
        slot_units(s)
        drk_all[slot_part(s), :] = kt[prompt_len:, :] * score_scale
        drv_all[slot_part(s), :] = vt[prompt_len:, :]
        drk_copy(s).start()
        drv_copy(s).start()
        for o in range(OWNERS):
            start = block_position(place[first_block + o], me, n) * prow
            target = pl.ds(pl.multiple_of(start, prow), prow)
            block = slice(o * prow, (o + 1) * prow)
            term_ref[target, 0:width] += kt[block, :] * score_scale
            term_ref[target, width : 2 * width] += vt[block, :]

    for copy in term_copies:
        copy.start()
    for copy in term_copies:
        copy.wait()
    for chunk in range(slots * tiles):
        dq_copy(chunk).wait()
    for s in range(slots):
        drk_copy(s).wait()
        drv_copy(s).wait()


def slot_grads(queries, resp_keys, resp_values, out_grad, own_kv, other_kv, prompts, lengths, begins, holders):
    slots = prompts.shape[0]
    rows, columns = queries.shape
    slot_rows, width = rows // slots, resp_keys.shape[1]
    n = holders.shape[0]
    prow = 2 * own_kv.shape[0] // n
    total = prow * OWNERS + slot_rows
    tiles = slot_rows // TILE
    hbm = pl.BlockSpec(memory_space=pltpu.HBM)
    f32, bf16 = jnp.float32, jnp.bfloat16
    return pl.pallas_call(
        grad_kernel,
        in_specs=[hbm] * 10,
        out_specs=[hbm] * 5,
        out_shape=[
            jax.ShapeDtypeStruct((rows, columns), f32),
            jax.ShapeDtypeStruct((rows, width), f32),
            jax.ShapeDtypeStruct((rows, width), f32),
            jax.ShapeDtypeStruct((n * prow // 2, 2 * width), f32),
            jax.ShapeDtypeStruct((n * prow // 2, 2 * width), f32),
        ],
        scratch_shapes=[
            pltpu.SMEM((slots,), jnp.int32),
            pltpu.SMEM((slots,), jnp.int32),
            pltpu.SMEM((slots,), jnp.int32),
            pltpu.SMEM((n,), jnp.int32),
            pltpu.SMEM((n,), jnp.int32),
            pltpu.VMEM((rows, columns), bf16),
            pltpu.VMEM((rows, columns), bf16),
            pltpu.VMEM((rows, width), bf16),
            pltpu.VMEM((rows, width), bf16),
            pltpu.VMEM((rows, columns), f32),
            pltpu.VMEM((rows, width), f32),
            pltpu.VMEM((rows, width), f32),
            pltpu.VMEM((n * prow, 2 * width), bf16),
            pltpu.VMEM((n * prow, 2 * width), f32),
            pltpu.VMEM((total, width), bf16),
            pltpu.VMEM((total, width), bf16),
            pltpu.VMEM((width, total), bf16),
            pltpu.VMEM((slot_rows, TILE), f32),
            pltpu.VMEM((TILE, TILE), f32),
            pltpu.VMEM((2, 2, width, 2 * TILE), bf16),
            pltpu.VMEM((2, total, 2 * TILE), f32),
            pltpu.VMEM((2, total, 2 * TILE), f32),
            pltpu.VMEM((2, total, 4 * TILE), bf16),
            pltpu.VMEM((2, total, 4 * TILE), bf16),
            pltpu.VMEM((total, width), f32),
            pltpu.VMEM((total, width), f32),
            pltpu.SemaphoreType.DMA((4,)),
            pltpu.SemaphoreType.DMA((2,)),
            pltpu.SemaphoreType.DMA((slots * tiles,)),
            pltpu.SemaphoreType.DMA((slots * tiles,)),
            pltpu.SemaphoreType.DMA((slots * tiles,)),
            pltpu.SemaphoreType.DMA((slots,)),
            pltpu.SemaphoreType.DMA((slots,)),
            pltpu.SemaphoreType.DMA((2,)),
            pltpu.SemaphoreType.DMA((2,)),
        ],
        compiler_params=pltpu.CompilerParams(vmem_limit_bytes=60 * 1024 * 1024),
    )(prompts, lengths, begins, holders, queries, out_grad, resp_keys, resp_values, own_kv, other_kv)


def body(
    n,
    queries,
    resp_keys,
    resp_values,
    out_grad,
    prompt_keys,
    prompt_values,
    slot_prompt,
    slot_length,
    slot_begin,
    block_prompt,
):
    width = resp_keys.shape[1]
    prow = prompt_keys.shape[0]
    own = jnp.pad(prompt_keys, ((0, 0), (0, width))) + jnp.pad(prompt_values, ((0, 0), (width, 0)))
    own = jnp.broadcast_to(own[None], (n // 2, prow, 2 * width)).reshape(-1, 2 * width)
    own_kv = exchange(own, n)
    other_kv = swap_cores(own_kv, n)
    query_grad, key_grad, value_grad, own_term, other_term = slot_grads(
        queries, resp_keys, resp_values, out_grad, own_kv, other_kv,
        slot_prompt, slot_length, slot_begin, block_prompt,
    )
    parts = exchange(own_term + swap_cores(other_term, n), n)
    owned = jnp.sum(parts.reshape(n // 2, prow, 2 * width), axis=0)
    return query_grad, key_grad, value_grad, owned[:, :width], owned[:, width:]


def solution(mesh):
    n = mesh.shape["seq"]
    rows = P(("groups", "seq"), None)
    slots = P(("groups", "seq"))
    return jax.shard_map(
        functools.partial(body, n),
        mesh=mesh,
        in_specs=(rows,) * 6 + (slots,) * 3 + (P("groups"),),
        out_specs=(rows,) * 5,
        check_vma=False,
    )
```

```python
import functools
import math

import jax
import jax.numpy as jnp
from jax import lax
from jax.experimental import pallas as pl
from jax.experimental.pallas import tpu as pltpu
from jax.sharding import PartitionSpec as P

OWNERS = 8
TILE = 128
PIECE = 16
score_scale = 0.08838834764831845
EXP2_SCALE = score_scale * math.log2(math.e)
MASKED = -1e30

ACROSS = (((1,), (1,)), ((), ()))


def same_core_groups(n):
    return [list(range(core, n, 2)) for core in range(2)]


def swap_cores(x, n):
    return lax.ppermute(x, "seq", [(i, i ^ 1) for i in range(n)])


def exchange(x, n):
    return lax.all_to_all(
        x, "seq", split_axis=0, concat_axis=0, axis_index_groups=same_core_groups(n), tiled=True
    )


def block_position(holder, me, n):
    return ((holder ^ me) & 1) * (n // 2) + (holder >> 1)


def grad_kernel(
    prompt_hbm,
    length_hbm,
    begin_hbm,
    holder_hbm,
    q_hbm,
    g_hbm,
    rk_hbm,
    rv_hbm,
    own_hbm,
    other_hbm,
    dq_hbm,
    drk_hbm,
    drv_hbm,
    own_term_hbm,
    other_term_hbm,
    prompt_ref,
    length_ref,
    begin_ref,
    holder_ref,
    place,
    q_all,
    g_all,
    rk_all,
    rv_all,
    dq_all,
    drk_all,
    drv_all,
    kv,
    term_ref,
    keys,
    values,
    keys_t,
    live_bias,
    causal_bias,
    turned,
    exps,
    dprobs,
    prob16,
    dscore16,
    kt,
    vt,
    sem_scalar,
    sem_resp,
    sem_q,
    sem_g,
    sem_dq,
    sem_drk,
    sem_drv,
    sem_kv,
    sem_term,
):
    n = holder_ref.shape[0]
    slots = prompt_ref.shape[0]
    rows, width = rk_all.shape
    slot_rows = rows // slots
    tiles = slot_rows // TILE
    prow = term_ref.shape[0] // n
    prompt_len = prow * OWNERS
    heads = q_all.shape[1] // width
    me = lax.axis_index("seq")

    scalar_copies = [
        pltpu.make_async_copy(src, dst, sem_scalar.at[i])
        for i, (src, dst) in enumerate(
            [
                (prompt_hbm, prompt_ref),
                (length_hbm, length_ref),
                (begin_hbm, begin_ref),
                (holder_hbm, holder_ref),
            ]
        )
    ]
    resp_copies = [
        pltpu.make_async_copy(rk_hbm, rk_all, sem_resp.at[0]),
        pltpu.make_async_copy(rv_hbm, rv_all, sem_resp.at[1]),
    ]

    def tile_rows(chunk):
        return pl.ds(pl.multiple_of(chunk * TILE, TILE), TILE)

    def q_copy(chunk):
        part = tile_rows(chunk)
        return pltpu.make_async_copy(q_hbm.at[part], q_all.at[part], sem_q.at[chunk])

    def g_copy(chunk):
        part = tile_rows(chunk)
        return pltpu.make_async_copy(g_hbm.at[part], g_all.at[part], sem_g.at[chunk])

    def dq_copy(chunk):
        part = tile_rows(chunk)
        return pltpu.make_async_copy(dq_all.at[part], dq_hbm.at[part], sem_dq.at[chunk])

    def slot_part(s):
        return pl.ds(pl.multiple_of(s * slot_rows, slot_rows), slot_rows)

    def drk_copy(s):
        return pltpu.make_async_copy(
            drk_all.at[slot_part(s)], drk_hbm.at[slot_part(s)], sem_drk.at[s]
        )

    def drv_copy(s):
        return pltpu.make_async_copy(
            drv_all.at[slot_part(s)], drv_hbm.at[slot_part(s)], sem_drv.at[s]
        )

    half_rows = term_ref.shape[0] // 2
    kv_copies = [
        pltpu.make_async_copy(src, kv.at[pl.ds(i * half_rows, half_rows)], sem_kv.at[i])
        for i, src in enumerate([own_hbm, other_hbm])
    ]
    term_copies = [
        pltpu.make_async_copy(term_ref.at[pl.ds(i * half_rows, half_rows)], dst, sem_term.at[i])
        for i, dst in enumerate([own_term_hbm, other_term_hbm])
    ]
    for copy in scalar_copies + kv_copies + resp_copies:
        copy.start()
    for chunk in range(slots * tiles):
        q_copy(chunk).start()
        g_copy(chunk).start()

    term_ref[...] = jnp.zeros_like(term_ref)
    causal_bias[...] = jnp.where(
        lax.broadcasted_iota(jnp.int32, (TILE, TILE), 0)
        <= lax.broadcasted_iota(jnp.int32, (TILE, TILE), 1),
        0.0,
        MASKED,
    )
    for copy in scalar_copies + kv_copies + resp_copies:
        copy.wait()

    @pl.loop(0, n)
    def _(j):
        place[holder_ref[j]] = j

    half = heads // 2
    wide = 2 * TILE
    units = [(index, pair) for index in range(tiles) for pair in range(half)]

    def columns_of(u):
        return prompt_len + (units[u][0] + 1) * TILE

    def chunks(u):
        return range(0, columns_of(u), TILE)

    def stacked(ref, s, index, first, count):
        part = tile_rows(s * tiles + index)
        return jnp.concatenate(
            [ref[part, (first + h) * width : (first + h + 1) * width] for h in range(count)], axis=0
        )

    def fold(x, how):
        return how(how(x.reshape(x.shape[0] // 8, 8, x.shape[1]), axis=0), axis=0, keepdims=True)

    def head(s, u, out):
        index, pair = units[u]
        columns, buf = columns_of(u), u % 2
        if pair == 0:
            q_copy(s * tiles + index).wait()
            g_copy(s * tiles + index).wait()
        lanes = slice((u % 2) * wide, (u % 2 + 1) * wide)
        q2t, g2t = turned.at[(u // 2) % 3, 0, :, lanes], turned.at[(u // 2) % 3, 1, :, lanes]
        q2t[...] = stacked(q_all, s, index, 2 * pair, 2).T
        g2t[...] = stacked(g_all, s, index, 2 * pair, 2).T
        tops, totals, weights = [], [], []
        for c in chunks(u):
            part = slice(c, c + TILE)
            block = jnp.dot(keys[part, :], q2t[...], preferred_element_type=jnp.float32)
            if c >= prompt_len:
                bias = live_bias[c - prompt_len : c - prompt_len + TILE, :]
                if c + TILE == columns:
                    bias = bias + causal_bias[...]
                block = block + jnp.concatenate([bias, bias], axis=1)
            top = fold(block, jnp.max) * EXP2_SCALE
            e = jnp.exp2(block * EXP2_SCALE - top)
            exps[buf, part, :] = e
            yield
            d = jnp.dot(values[part, :], g2t[...], preferred_element_type=jnp.float32)
            dprobs[buf, part, :] = d
            tops.append(top)
            totals.append(fold(e, jnp.sum))
            weights.append(fold(e * d, jnp.sum))
            yield
        top = functools.reduce(jnp.maximum, tops)
        factors = [jnp.exp2(part - top) for part in tops]
        total = functools.reduce(jnp.add, [f * x for f, x in zip(factors, totals)])
        weighted = functools.reduce(jnp.add, [f * x for f, x in zip(factors, weights)])
        row = index * TILE + lax.broadcasted_iota(jnp.int32, (1, TILE), 1)
        live = (row >= begin_ref[s]) & (row < begin_ref[s] + length_ref[s])
        inverse = jnp.where(jnp.concatenate([live, live], axis=1), 1.0 / total, 0.0)
        out["delta"] = weighted * inverse
        out["factors"] = [f * inverse for f in factors]

    def tail(u, stats):
        buf, group = u % 2, (u // 2) % 2
        lanes = slice((u % 2) * wide, (u % 2 + 1) * wide)
        delta = stats["delta"]
        for c, factor in zip(chunks(u), stats["factors"]):
            for first in range(c, c + TILE, PIECE):
                part = slice(first, first + PIECE)
                p = exps[buf, part, :] * factor
                prob16[group, part, lanes] = p.astype(jnp.bfloat16)
                ds = p * (dprobs[buf, part, :] - delta)
                dscore16[group, part, lanes] = ds.astype(jnp.bfloat16)
            yield

    def flush_keys(s, u):
        group, columns = (u // 2) % 2, columns_of(u)
        kt[:, 0:columns] += lax.dot_general(
            turned[(u // 2) % 3, 0], dscore16[group, 0:columns, :], ACROSS, preferred_element_type=jnp.float32
        )
        yield

    def flush_values(s, u):
        group, columns = (u // 2) % 2, columns_of(u)
        vt[:, 0:columns] += lax.dot_general(
            turned[(u // 2) % 3, 1], prob16[group, 0:columns, :], ACROSS, preferred_element_type=jnp.float32
        )
        yield

    def flush_queries(s, u):
        index, pair = units[u]
        group, columns = (u // 2) % 2, columns_of(u)
        part = tile_rows(s * tiles + index)
        for side in range(2):
            ds = dscore16[group, 0:columns, side * wide : (side + 1) * wide]
            dqt = jnp.dot(keys_t[:, 0:columns], ds, preferred_element_type=jnp.float32)
            for h in range(2):
                first = (2 * (pair - 1 + side) + h) * width
                dq_all[part, first : first + width] = dqt[:, h * TILE : (h + 1) * TILE].T * score_scale
            yield
        if pair == half - 1:
            dq_copy(s * tiles + index).start()

    def together(*steps):
        steps = list(steps)
        while steps:
            for step in list(steps):
                if next(step, steps) is steps:
                    steps.remove(step)

    def slot_units(s):
        stats = {}
        together(head(s, 0, stats))
        for u in range(len(units)):
            now, stats = stats, {}
            steps = []
            if u + 1 < len(units):
                steps.append(head(s, u + 1, stats))
            steps.append(tail(u, now))
            if u >= 2 and u % 2 == 0:
                steps += [flush_keys(s, u - 1), flush_queries(s, u - 1)]
            elif u >= 2:
                steps.append(flush_values(s, u - 2))
            together(*steps)
        last = len(units) - 1
        together(flush_keys(s, last), flush_values(s, last), flush_queries(s, last))

    @pl.loop(0, slots)
    def _(s):
        first_block = prompt_ref[s] * OWNERS
        for o in range(OWNERS):
            start = block_position(place[first_block + o], me, n) * prow
            source = pl.ds(pl.multiple_of(start, prow), prow)
            keys[o * prow : (o + 1) * prow, :] = kv[source, 0:width]
            values[o * prow : (o + 1) * prow, :] = kv[source, width : 2 * width]
        keys[prompt_len:, :] = rk_all[slot_part(s), :]
        values[prompt_len:, :] = rv_all[slot_part(s), :]
        keys_t[...] = keys[...].astype(jnp.float32).T.astype(jnp.bfloat16)
        column = lax.broadcasted_iota(jnp.int32, (slot_rows, TILE), 0)
        live_bias[...] = jnp.where(column >= begin_ref[s], 0.0, MASKED)
        kt[...] = jnp.zeros_like(kt)
        vt[...] = jnp.zeros_like(vt)
        slot_units(s)
        drk_all[slot_part(s), :] = kt[:, prompt_len:].T * score_scale
        drv_all[slot_part(s), :] = vt[:, prompt_len:].T
        prompt_kt = kt[:, 0:prompt_len].T * score_scale
        prompt_vt = vt[:, 0:prompt_len].T
        drk_copy(s).start()
        drv_copy(s).start()
        for o in range(OWNERS):
            start = block_position(place[first_block + o], me, n) * prow
            target = pl.ds(pl.multiple_of(start, prow), prow)
            block = slice(o * prow, (o + 1) * prow)
            term_ref[target, 0:width] += prompt_kt[block]
            term_ref[target, width : 2 * width] += prompt_vt[block]

    for copy in term_copies:
        copy.start()
    for copy in term_copies:
        copy.wait()
    for chunk in range(slots * tiles):
        dq_copy(chunk).wait()
    for s in range(slots):
        drk_copy(s).wait()
        drv_copy(s).wait()


def slot_grads(queries, resp_keys, resp_values, out_grad, own_kv, other_kv, prompts, lengths, begins, holders):
    slots = prompts.shape[0]
    rows, columns = queries.shape
    slot_rows, width = rows // slots, resp_keys.shape[1]
    n = holders.shape[0]
    prow = 2 * own_kv.shape[0] // n
    total = prow * OWNERS + slot_rows
    tiles = slot_rows // TILE
    hbm = pl.BlockSpec(memory_space=pltpu.HBM)
    f32, bf16 = jnp.float32, jnp.bfloat16
    return pl.pallas_call(
        grad_kernel,
        in_specs=[hbm] * 10,
        out_specs=[hbm] * 5,
        out_shape=[
            jax.ShapeDtypeStruct((rows, columns), f32),
            jax.ShapeDtypeStruct((rows, width), f32),
            jax.ShapeDtypeStruct((rows, width), f32),
            jax.ShapeDtypeStruct((n * prow // 2, 2 * width), f32),
            jax.ShapeDtypeStruct((n * prow // 2, 2 * width), f32),
        ],
        scratch_shapes=[
            pltpu.SMEM((slots,), jnp.int32),
            pltpu.SMEM((slots,), jnp.int32),
            pltpu.SMEM((slots,), jnp.int32),
            pltpu.SMEM((n,), jnp.int32),
            pltpu.SMEM((n,), jnp.int32),
            pltpu.VMEM((rows, columns), bf16),
            pltpu.VMEM((rows, columns), bf16),
            pltpu.VMEM((rows, width), bf16),
            pltpu.VMEM((rows, width), bf16),
            pltpu.VMEM((rows, columns), f32),
            pltpu.VMEM((rows, width), f32),
            pltpu.VMEM((rows, width), f32),
            pltpu.VMEM((n * prow, 2 * width), bf16),
            pltpu.VMEM((n * prow, 2 * width), f32),
            pltpu.VMEM((total, width), bf16),
            pltpu.VMEM((total, width), bf16),
            pltpu.VMEM((width, total), bf16),
            pltpu.VMEM((slot_rows, TILE), f32),
            pltpu.VMEM((TILE, TILE), f32),
            pltpu.VMEM((3, 2, width, 4 * TILE), bf16),
            pltpu.VMEM((2, total, 2 * TILE), f32),
            pltpu.VMEM((2, total, 2 * TILE), f32),
            pltpu.VMEM((2, total, 4 * TILE), bf16),
            pltpu.VMEM((2, total, 4 * TILE), bf16),
            pltpu.VMEM((width, total), f32),
            pltpu.VMEM((width, total), f32),
            pltpu.SemaphoreType.DMA((4,)),
            pltpu.SemaphoreType.DMA((2,)),
            pltpu.SemaphoreType.DMA((slots * tiles,)),
            pltpu.SemaphoreType.DMA((slots * tiles,)),
            pltpu.SemaphoreType.DMA((slots * tiles,)),
            pltpu.SemaphoreType.DMA((slots,)),
            pltpu.SemaphoreType.DMA((slots,)),
            pltpu.SemaphoreType.DMA((2,)),
            pltpu.SemaphoreType.DMA((2,)),
        ],
        compiler_params=pltpu.CompilerParams(vmem_limit_bytes=60 * 1024 * 1024),
    )(prompts, lengths, begins, holders, queries, out_grad, resp_keys, resp_values, own_kv, other_kv)


def body(
    n,
    queries,
    resp_keys,
    resp_values,
    out_grad,
    prompt_keys,
    prompt_values,
    slot_prompt,
    slot_length,
    slot_begin,
    block_prompt,
):
    width = resp_keys.shape[1]
    prow = prompt_keys.shape[0]
    own = jnp.pad(prompt_keys, ((0, 0), (0, width))) + jnp.pad(prompt_values, ((0, 0), (width, 0)))
    own = jnp.broadcast_to(own[None], (n // 2, prow, 2 * width)).reshape(-1, 2 * width)
    own_kv = exchange(own, n)
    other_kv = swap_cores(own_kv, n)
    query_grad, key_grad, value_grad, own_term, other_term = slot_grads(
        queries, resp_keys, resp_values, out_grad, own_kv, other_kv,
        slot_prompt, slot_length, slot_begin, block_prompt,
    )
    parts = exchange(own_term + swap_cores(other_term, n), n)
    owned = jnp.sum(parts.reshape(n // 2, prow, 2 * width), axis=0)
    return query_grad, key_grad, value_grad, owned[:, :width], owned[:, width:]


def solution(mesh):
    n = mesh.shape["seq"]
    rows = P(("groups", "seq"), None)
    slots = P(("groups", "seq"))
    return jax.shard_map(
        functools.partial(body, n),
        mesh=mesh,
        in_specs=(rows,) * 6 + (slots,) * 3 + (P("groups"),),
        out_specs=(rows,) * 5,
        check_vma=False,
    )
```

```python
import functools
import math

import jax
import jax.numpy as jnp
from jax import lax
from jax.experimental import pallas as pl
from jax.experimental.pallas import tpu as pltpu
from jax.sharding import PartitionSpec as P

OWNERS = 8
TILE = 128
PIECE = 16
score_scale = 0.08838834764831845
EXP2_SCALE = score_scale * math.log2(math.e)
MASKED = -1e30

ACROSS = (((1,), (1,)), ((), ()))


def same_core_groups(n):
    return [list(range(core, n, 2)) for core in range(2)]


def swap_cores(x, n):
    return lax.ppermute(x, "seq", [(i, i ^ 1) for i in range(n)])


def exchange(x, n):
    return lax.all_to_all(
        x, "seq", split_axis=0, concat_axis=0, axis_index_groups=same_core_groups(n), tiled=True
    )


def block_position(holder, me, n):
    return ((holder ^ me) & 1) * (n // 2) + (holder >> 1)


def grad_kernel(
    prompt_hbm,
    length_hbm,
    begin_hbm,
    holder_hbm,
    q_hbm,
    g_hbm,
    rk_hbm,
    rv_hbm,
    own_hbm,
    other_hbm,
    dq_hbm,
    drk_hbm,
    drv_hbm,
    own_term_hbm,
    other_term_hbm,
    prompt_ref,
    length_ref,
    begin_ref,
    holder_ref,
    place,
    q_all,
    g_all,
    rk_all,
    rv_all,
    dq_all,
    drk_all,
    drv_all,
    kv,
    term_ref,
    keys,
    values,
    keys_t,
    live_bias,
    causal_bias,
    turned,
    exps,
    dprobs,
    prob16,
    dscore16,
    kt,
    vt,
    sem_scalar,
    sem_resp,
    sem_q,
    sem_g,
    sem_dq,
    sem_drk,
    sem_drv,
    sem_kv,
    sem_term,
):
    n = holder_ref.shape[0]
    slots = prompt_ref.shape[0]
    rows, width = rk_all.shape
    slot_rows = rows // slots
    tiles = slot_rows // TILE
    prow = term_ref.shape[0] // n
    prompt_len = prow * OWNERS
    heads = q_all.shape[1] // width
    me = lax.axis_index("seq")

    scalar_copies = [
        pltpu.make_async_copy(src, dst, sem_scalar.at[i])
        for i, (src, dst) in enumerate(
            [
                (prompt_hbm, prompt_ref),
                (length_hbm, length_ref),
                (begin_hbm, begin_ref),
                (holder_hbm, holder_ref),
            ]
        )
    ]
    resp_copies = [
        pltpu.make_async_copy(rk_hbm, rk_all, sem_resp.at[0]),
        pltpu.make_async_copy(rv_hbm, rv_all, sem_resp.at[1]),
    ]

    def tile_rows(chunk):
        return pl.ds(pl.multiple_of(chunk * TILE, TILE), TILE)

    def q_copy(chunk):
        part = tile_rows(chunk)
        return pltpu.make_async_copy(q_hbm.at[part], q_all.at[part], sem_q.at[chunk])

    def g_copy(chunk):
        part = tile_rows(chunk)
        return pltpu.make_async_copy(g_hbm.at[part], g_all.at[part], sem_g.at[chunk])

    def dq_copy(chunk):
        part = tile_rows(chunk)
        return pltpu.make_async_copy(dq_all.at[part], dq_hbm.at[part], sem_dq.at[chunk])

    def slot_part(s):
        return pl.ds(pl.multiple_of(s * slot_rows, slot_rows), slot_rows)

    def drk_copy(s):
        return pltpu.make_async_copy(
            drk_all.at[slot_part(s)], drk_hbm.at[slot_part(s)], sem_drk.at[s]
        )

    def drv_copy(s):
        return pltpu.make_async_copy(
            drv_all.at[slot_part(s)], drv_hbm.at[slot_part(s)], sem_drv.at[s]
        )

    half_rows = term_ref.shape[0] // 2
    kv_copies = [
        pltpu.make_async_copy(src, kv.at[pl.ds(i * half_rows, half_rows)], sem_kv.at[i])
        for i, src in enumerate([own_hbm, other_hbm])
    ]
    term_copies = [
        pltpu.make_async_copy(term_ref.at[pl.ds(i * half_rows, half_rows)], dst, sem_term.at[i])
        for i, dst in enumerate([own_term_hbm, other_term_hbm])
    ]
    for copy in scalar_copies + kv_copies + resp_copies:
        copy.start()
    for chunk in range(slots * tiles):
        q_copy(chunk).start()
        g_copy(chunk).start()

    term_ref[...] = jnp.zeros_like(term_ref)
    causal_bias[...] = jnp.where(
        lax.broadcasted_iota(jnp.int32, (TILE, TILE), 0)
        <= lax.broadcasted_iota(jnp.int32, (TILE, TILE), 1),
        0.0,
        MASKED,
    )
    for copy in scalar_copies + kv_copies + resp_copies:
        copy.wait()

    @pl.loop(0, n)
    def _(j):
        place[holder_ref[j]] = j

    wide = 2 * TILE
    at_once = 4

    def head_lanes(h):
        return pl.ds(pl.multiple_of(h * width, width), width)

    def stacked(ref, part, first, count):
        return jnp.concatenate([ref[part, head_lanes(first + h)] for h in range(count)], axis=0)

    def fold(x, how):
        return how(how(x.reshape(x.shape[0] // 8, 8, x.shape[1]), axis=0), axis=0, keepdims=True)

    def chunks(columns):
        return range(0, columns, TILE)

    def head(s, index, columns, first, side, out):
        part = tile_rows(s * tiles + index)
        lanes = slice(side * wide, (side + 1) * wide)
        q2t, g2t = turned.at[0, :, lanes], turned.at[1, :, lanes]
        q2t[...] = stacked(q_all, part, first + 2 * side, 2).T
        g2t[...] = stacked(g_all, part, first + 2 * side, 2).T
        tops, totals, weights = [], [], []
        for c in chunks(columns):
            span = slice(c, c + TILE)
            block = jnp.dot(keys[span, :], q2t[...], preferred_element_type=jnp.float32)
            if c >= prompt_len:
                bias = live_bias[c - prompt_len : c - prompt_len + TILE, :]
                if c + TILE == columns:
                    bias = bias + causal_bias[...]
                block = block + jnp.concatenate([bias, bias], axis=1)
            top = fold(block, jnp.max) * EXP2_SCALE
            e = jnp.exp2(block * EXP2_SCALE - top)
            exps[side, span, :] = e
            yield
            d = jnp.dot(values[span, :], g2t[...], preferred_element_type=jnp.float32)
            dprobs[side, span, :] = d
            tops.append(top)
            totals.append(fold(e, jnp.sum))
            weights.append(fold(e * d, jnp.sum))
            yield
        top = functools.reduce(jnp.maximum, tops)
        factors = [jnp.exp2(x - top) for x in tops]
        total = functools.reduce(jnp.add, [f * x for f, x in zip(factors, totals)])
        weighted = functools.reduce(jnp.add, [f * x for f, x in zip(factors, weights)])
        row = index * TILE + lax.broadcasted_iota(jnp.int32, (1, TILE), 1)
        live = (row >= begin_ref[s]) & (row < begin_ref[s] + length_ref[s])
        inverse = jnp.where(jnp.concatenate([live, live], axis=1), 1.0 / total, 0.0)
        out["delta"] = weighted * inverse
        out["factors"] = [f * inverse for f in factors]

    def tail(columns, side, stats):
        lanes = slice(side * wide, (side + 1) * wide)
        delta = stats["delta"]
        for c, factor in zip(chunks(columns), stats["factors"]):
            for start in range(c, c + TILE, PIECE):
                span = slice(start, start + PIECE)
                p = exps[side, span, :] * factor
                prob16[span, lanes] = p.astype(jnp.bfloat16)
                ds = p * (dprobs[side, span, :] - delta)
                dscore16[span, lanes] = ds.astype(jnp.bfloat16)
            yield

    def flush_queries(part, columns, first, side):
        lanes = slice(side * wide, (side + 1) * wide)
        dqt = jnp.dot(
            keys_t[:, 0:columns], dscore16[0:columns, lanes], preferred_element_type=jnp.float32
        )
        for h in range(2):
            dq = dqt[:, h * TILE : (h + 1) * TILE].T * score_scale
            dq_all[part, head_lanes(first + 2 * side + h)] = dq
        yield

    def together(*steps):
        steps = list(steps)
        while steps:
            for step in list(steps):
                if next(step, steps) is steps:
                    steps.remove(step)

    def slot_units(s):
        for index in range(tiles):
            chunk = s * tiles + index
            columns = prompt_len + (index + 1) * TILE
            part = tile_rows(chunk)
            q_copy(chunk).wait()
            g_copy(chunk).wait()

            @pl.loop(0, heads // at_once)
            def _(group):
                first = group * at_once
                left, right = {}, {}
                together(head(s, index, columns, first, 0, left))
                together(head(s, index, columns, first, 1, right), tail(columns, 0, left))
                together(tail(columns, 1, right), flush_queries(part, columns, first, 0))
                kt[:, 0:columns] += lax.dot_general(
                    turned[0], dscore16[0:columns, :], ACROSS, preferred_element_type=jnp.float32
                )
                vt[:, 0:columns] += lax.dot_general(
                    turned[1], prob16[0:columns, :], ACROSS, preferred_element_type=jnp.float32
                )
                together(flush_queries(part, columns, first, 1))

            dq_copy(chunk).start()

    @pl.loop(0, slots)
    def _(s):
        first_block = prompt_ref[s] * OWNERS
        for o in range(OWNERS):
            start = block_position(place[first_block + o], me, n) * prow
            source = pl.ds(pl.multiple_of(start, prow), prow)
            keys[o * prow : (o + 1) * prow, :] = kv[source, 0:width]
            values[o * prow : (o + 1) * prow, :] = kv[source, width : 2 * width]
        keys[prompt_len:, :] = rk_all[slot_part(s), :]
        values[prompt_len:, :] = rv_all[slot_part(s), :]
        keys_t[...] = keys[...].astype(jnp.float32).T.astype(jnp.bfloat16)
        column = lax.broadcasted_iota(jnp.int32, (slot_rows, TILE), 0)
        live_bias[...] = jnp.where(column >= begin_ref[s], 0.0, MASKED)
        kt[...] = jnp.zeros_like(kt)
        vt[...] = jnp.zeros_like(vt)
        slot_units(s)
        drk_all[slot_part(s), :] = kt[:, prompt_len:].T * score_scale
        drv_all[slot_part(s), :] = vt[:, prompt_len:].T
        prompt_kt = kt[:, 0:prompt_len].T * score_scale
        prompt_vt = vt[:, 0:prompt_len].T
        drk_copy(s).start()
        drv_copy(s).start()
        for o in range(OWNERS):
            start = block_position(place[first_block + o], me, n) * prow
            target = pl.ds(pl.multiple_of(start, prow), prow)
            block = slice(o * prow, (o + 1) * prow)
            term_ref[target, 0:width] += prompt_kt[block]
            term_ref[target, width : 2 * width] += prompt_vt[block]

    for copy in term_copies:
        copy.start()
    for copy in term_copies:
        copy.wait()
    for chunk in range(slots * tiles):
        dq_copy(chunk).wait()
    for s in range(slots):
        drk_copy(s).wait()
        drv_copy(s).wait()


def slot_grads(queries, resp_keys, resp_values, out_grad, own_kv, other_kv, prompts, lengths, begins, holders):
    slots = prompts.shape[0]
    rows, columns = queries.shape
    slot_rows, width = rows // slots, resp_keys.shape[1]
    n = holders.shape[0]
    prow = 2 * own_kv.shape[0] // n
    total = prow * OWNERS + slot_rows
    tiles = slot_rows // TILE
    hbm = pl.BlockSpec(memory_space=pltpu.HBM)
    f32, bf16 = jnp.float32, jnp.bfloat16
    return pl.pallas_call(
        grad_kernel,
        in_specs=[hbm] * 10,
        out_specs=[hbm] * 5,
        out_shape=[
            jax.ShapeDtypeStruct((rows, columns), f32),
            jax.ShapeDtypeStruct((rows, width), f32),
            jax.ShapeDtypeStruct((rows, width), f32),
            jax.ShapeDtypeStruct((n * prow // 2, 2 * width), f32),
            jax.ShapeDtypeStruct((n * prow // 2, 2 * width), f32),
        ],
        scratch_shapes=[
            pltpu.SMEM((slots,), jnp.int32),
            pltpu.SMEM((slots,), jnp.int32),
            pltpu.SMEM((slots,), jnp.int32),
            pltpu.SMEM((n,), jnp.int32),
            pltpu.SMEM((n,), jnp.int32),
            pltpu.VMEM((rows, columns), bf16),
            pltpu.VMEM((rows, columns), bf16),
            pltpu.VMEM((rows, width), bf16),
            pltpu.VMEM((rows, width), bf16),
            pltpu.VMEM((rows, columns), f32),
            pltpu.VMEM((rows, width), f32),
            pltpu.VMEM((rows, width), f32),
            pltpu.VMEM((n * prow, 2 * width), bf16),
            pltpu.VMEM((n * prow, 2 * width), f32),
            pltpu.VMEM((total, width), bf16),
            pltpu.VMEM((total, width), bf16),
            pltpu.VMEM((width, total), bf16),
            pltpu.VMEM((slot_rows, TILE), f32),
            pltpu.VMEM((TILE, TILE), f32),
            pltpu.VMEM((2, width, 4 * TILE), bf16),
            pltpu.VMEM((2, total, 2 * TILE), f32),
            pltpu.VMEM((2, total, 2 * TILE), f32),
            pltpu.VMEM((total, 4 * TILE), bf16),
            pltpu.VMEM((total, 4 * TILE), bf16),
            pltpu.VMEM((width, total), f32),
            pltpu.VMEM((width, total), f32),
            pltpu.SemaphoreType.DMA((4,)),
            pltpu.SemaphoreType.DMA((2,)),
            pltpu.SemaphoreType.DMA((slots * tiles,)),
            pltpu.SemaphoreType.DMA((slots * tiles,)),
            pltpu.SemaphoreType.DMA((slots * tiles,)),
            pltpu.SemaphoreType.DMA((slots,)),
            pltpu.SemaphoreType.DMA((slots,)),
            pltpu.SemaphoreType.DMA((2,)),
            pltpu.SemaphoreType.DMA((2,)),
        ],
        compiler_params=pltpu.CompilerParams(vmem_limit_bytes=60 * 1024 * 1024),
    )(prompts, lengths, begins, holders, queries, out_grad, resp_keys, resp_values, own_kv, other_kv)


def body(
    n,
    queries,
    resp_keys,
    resp_values,
    out_grad,
    prompt_keys,
    prompt_values,
    slot_prompt,
    slot_length,
    slot_begin,
    block_prompt,
):
    width = resp_keys.shape[1]
    prow = prompt_keys.shape[0]
    own = jnp.pad(prompt_keys, ((0, 0), (0, width))) + jnp.pad(prompt_values, ((0, 0), (width, 0)))
    own = jnp.broadcast_to(own[None], (n // 2, prow, 2 * width)).reshape(-1, 2 * width)
    own_kv = exchange(own, n)
    other_kv = swap_cores(own_kv, n)
    query_grad, key_grad, value_grad, own_term, other_term = slot_grads(
        queries, resp_keys, resp_values, out_grad, own_kv, other_kv,
        slot_prompt, slot_length, slot_begin, block_prompt,
    )
    parts = exchange(own_term + swap_cores(other_term, n), n)
    owned = jnp.sum(parts.reshape(n // 2, prow, 2 * width), axis=0)
    return query_grad, key_grad, value_grad, owned[:, :width], owned[:, width:]


def solution(mesh):
    n = mesh.shape["seq"]
    rows = P(("groups", "seq"), None)
    slots = P(("groups", "seq"))
    return jax.shard_map(
        functools.partial(body, n),
        mesh=mesh,
        in_specs=(rows,) * 6 + (slots,) * 3 + (P("groups"),),
        out_specs=(rows,) * 5,
        check_vma=False,
    )
```

```python
import functools
import math

import jax
import jax.numpy as jnp
from jax import lax
from jax.experimental import pallas as pl
from jax.experimental.pallas import tpu as pltpu
from jax.sharding import PartitionSpec as P

OWNERS = 8
TILE = 128
PIECE = 16
score_scale = 0.08838834764831845
EXP2_SCALE = score_scale * math.log2(math.e)
MASKED = -1e30

ACROSS = (((1,), (1,)), ((), ()))


def same_core_groups(n):
    return [list(range(core, n, 2)) for core in range(2)]


def swap_cores(x, n):
    return lax.ppermute(x, "seq", [(i, i ^ 1) for i in range(n)])


def exchange(x, n):
    return lax.all_to_all(
        x, "seq", split_axis=0, concat_axis=0, axis_index_groups=same_core_groups(n), tiled=True
    )


def block_position(holder, me, n):
    return ((holder ^ me) & 1) * (n // 2) + (holder >> 1)


def grad_kernel(
    prompt_hbm,
    length_hbm,
    begin_hbm,
    holder_hbm,
    q_hbm,
    g_hbm,
    rk_hbm,
    rv_hbm,
    own_hbm,
    other_hbm,
    dq_hbm,
    drk_hbm,
    drv_hbm,
    own_term_hbm,
    other_term_hbm,
    prompt_ref,
    length_ref,
    begin_ref,
    holder_ref,
    place,
    q_all,
    g_all,
    rk_all,
    rv_all,
    dq_all,
    drk_all,
    drv_all,
    kv,
    term_ref,
    keys,
    values,
    keys_t,
    live_bias,
    causal_bias,
    turned,
    exps,
    dprobs,
    prob16,
    dscore16,
    kt,
    vt,
    sem_scalar,
    sem_resp,
    sem_q,
    sem_g,
    sem_dq,
    sem_drk,
    sem_drv,
    sem_kv,
    sem_term,
):
    n = holder_ref.shape[0]
    slots = prompt_ref.shape[0]
    rows, width = rk_all.shape
    slot_rows = rows // slots
    tiles = slot_rows // TILE
    prow = term_ref.shape[0] // n
    prompt_len = prow * OWNERS
    heads = q_all.shape[1] // width
    me = lax.axis_index("seq")

    scalar_copies = [
        pltpu.make_async_copy(src, dst, sem_scalar.at[i])
        for i, (src, dst) in enumerate(
            [
                (prompt_hbm, prompt_ref),
                (length_hbm, length_ref),
                (begin_hbm, begin_ref),
                (holder_hbm, holder_ref),
            ]
        )
    ]
    resp_copies = [
        pltpu.make_async_copy(rk_hbm, rk_all, sem_resp.at[0]),
        pltpu.make_async_copy(rv_hbm, rv_all, sem_resp.at[1]),
    ]

    def tile_rows(chunk):
        return pl.ds(pl.multiple_of(chunk * TILE, TILE), TILE)

    def q_copy(chunk):
        part = tile_rows(chunk)
        return pltpu.make_async_copy(q_hbm.at[part], q_all.at[part], sem_q.at[chunk])

    def g_copy(chunk):
        part = tile_rows(chunk)
        return pltpu.make_async_copy(g_hbm.at[part], g_all.at[part], sem_g.at[chunk])

    def dq_copy(chunk):
        part = tile_rows(chunk)
        return pltpu.make_async_copy(dq_all.at[part], dq_hbm.at[part], sem_dq.at[chunk])

    def slot_part(s):
        return pl.ds(pl.multiple_of(s * slot_rows, slot_rows), slot_rows)

    def drk_copy(s):
        return pltpu.make_async_copy(
            drk_all.at[slot_part(s)], drk_hbm.at[slot_part(s)], sem_drk.at[s]
        )

    def drv_copy(s):
        return pltpu.make_async_copy(
            drv_all.at[slot_part(s)], drv_hbm.at[slot_part(s)], sem_drv.at[s]
        )

    half_rows = term_ref.shape[0] // 2
    kv_copies = [
        pltpu.make_async_copy(src, kv.at[pl.ds(i * half_rows, half_rows)], sem_kv.at[i])
        for i, src in enumerate([own_hbm, other_hbm])
    ]
    term_copies = [
        pltpu.make_async_copy(term_ref.at[pl.ds(i * half_rows, half_rows)], dst, sem_term.at[i])
        for i, dst in enumerate([own_term_hbm, other_term_hbm])
    ]
    for copy in scalar_copies + kv_copies + resp_copies:
        copy.start()
    for chunk in range(slots * tiles):
        q_copy(chunk).start()
        g_copy(chunk).start()

    term_ref[...] = jnp.zeros_like(term_ref)
    causal_bias[...] = jnp.where(
        lax.broadcasted_iota(jnp.int32, (TILE, TILE), 0)
        <= lax.broadcasted_iota(jnp.int32, (TILE, TILE), 1),
        0.0,
        MASKED,
    )
    for copy in scalar_copies + kv_copies + resp_copies:
        copy.wait()

    @pl.loop(0, n)
    def _(j):
        place[holder_ref[j]] = j

    wide = 2 * TILE
    at_once = 4
    groups = heads // at_once
    units = [(s, index, g) for s in range(slots) for index in range(tiles) for g in range(groups)]

    def columns_of(u):
        return prompt_len + (units[u][1] + 1) * TILE

    def rows_of(u):
        s, index, _ = units[u]
        first = (s * tiles + index) * TILE
        return slice(first, first + TILE)

    def first_head(u, side):
        return units[u][2] * at_once + 2 * side

    def chunks(u):
        return range(0, columns_of(u), TILE)

    def lanes_of(side):
        return slice(side * wide, (side + 1) * wide)

    def stacked(ref, u, side):
        first = first_head(u, side)
        return jnp.concatenate(
            [ref[rows_of(u), (first + h) * width : (first + h + 1) * width] for h in range(2)], axis=0
        )

    def fold(x, how):
        return how(how(x.reshape(x.shape[0] // 8, 8, x.shape[1]), axis=0), axis=0, keepdims=True)

    def prepare(s):
        first_block = prompt_ref[s] * OWNERS
        for o in range(OWNERS):
            start = block_position(place[first_block + o], me, n) * prow
            source = pl.ds(pl.multiple_of(start, prow), prow)
            keys[s, o * prow : (o + 1) * prow, :] = kv[source, 0:width]
            values[s, o * prow : (o + 1) * prow, :] = kv[source, width : 2 * width]
        own = slice(s * slot_rows, (s + 1) * slot_rows)
        keys[s, prompt_len:, :] = rk_all[own, :]
        values[s, prompt_len:, :] = rv_all[own, :]
        yield
        keys_t[s] = keys[s].astype(jnp.float32).T.astype(jnp.bfloat16)
        yield
        column = lax.broadcasted_iota(jnp.int32, (slot_rows, TILE), 0)
        live_bias[s] = jnp.where(column >= begin_ref[s], 0.0, MASKED)
        kt[s] = jnp.zeros_like(kt[s])
        vt[s] = jnp.zeros_like(vt[s])
        yield

    def finish(s):
        own = slice(s * slot_rows, (s + 1) * slot_rows)
        prompt_kt = kt[s, :, 0:prompt_len].T * score_scale
        prompt_vt = vt[s, :, 0:prompt_len].T
        yield
        drk_all[own, :] = kt[s, :, prompt_len:].T * score_scale
        drv_all[own, :] = vt[s, :, prompt_len:].T
        yield
        first_block = prompt_ref[s] * OWNERS
        for o in range(OWNERS):
            start = block_position(place[first_block + o], me, n) * prow
            target = pl.ds(pl.multiple_of(start, prow), prow)
            block = slice(o * prow, (o + 1) * prow)
            term_ref[target, 0:width] += prompt_kt[block]
            term_ref[target, width : 2 * width] += prompt_vt[block]
        yield

    def head(u, side, out):
        s, index, _ = units[u]
        columns, buf = columns_of(u), u % 2
        q2t, g2t = turned.at[u % 3, 0, :, lanes_of(side)], turned.at[u % 3, 1, :, lanes_of(side)]
        q2t[...] = stacked(q_all, u, side).T
        g2t[...] = stacked(g_all, u, side).T
        tops, totals, weights = [], [], []
        for c in chunks(u):
            part = slice(c, c + TILE)
            block = jnp.dot(keys[s, part, :], q2t[...], preferred_element_type=jnp.float32)
            if c >= prompt_len:
                bias = live_bias[s, c - prompt_len : c - prompt_len + TILE, :]
                if c + TILE == columns:
                    bias = bias + causal_bias[...]
                block = block + jnp.concatenate([bias, bias], axis=1)
            top = fold(block, jnp.max) * EXP2_SCALE
            e = jnp.exp2(block * EXP2_SCALE - top)
            exps[buf, side, part, :] = e
            yield
            d = jnp.dot(values[s, part, :], g2t[...], preferred_element_type=jnp.float32)
            dprobs[buf, side, part, :] = d
            tops.append(top)
            totals.append(fold(e, jnp.sum))
            weights.append(fold(e * d, jnp.sum))
            yield
        top = functools.reduce(jnp.maximum, tops)
        factors = [jnp.exp2(part - top) for part in tops]
        total = functools.reduce(jnp.add, [f * x for f, x in zip(factors, totals)])
        weighted = functools.reduce(jnp.add, [f * x for f, x in zip(factors, weights)])
        row = index * TILE + lax.broadcasted_iota(jnp.int32, (1, TILE), 1)
        live = (row >= begin_ref[s]) & (row < begin_ref[s] + length_ref[s])
        inverse = jnp.where(jnp.concatenate([live, live], axis=1), 1.0 / total, 0.0)
        out["delta"] = weighted * inverse
        out["factors"] = [f * inverse for f in factors]

    def tail(u, side, stats):
        buf, lanes = u % 2, lanes_of(side)
        delta = stats["delta"]
        for c, factor in zip(chunks(u), stats["factors"]):
            for first in range(c, c + TILE, PIECE):
                part = slice(first, first + PIECE)
                p = exps[buf, side, part, :] * factor
                prob16[buf, part, lanes] = p.astype(jnp.bfloat16)
                ds = p * (dprobs[buf, side, part, :] - delta)
                dscore16[buf, part, lanes] = ds.astype(jnp.bfloat16)
            yield

    def flush_keys(u):
        s, columns = units[u][0], columns_of(u)
        kt[s, :, 0:columns] += lax.dot_general(
            turned[u % 3, 0], dscore16[u % 2, 0:columns, :], ACROSS, preferred_element_type=jnp.float32
        )
        yield

    def flush_values(u):
        s, columns = units[u][0], columns_of(u)
        vt[s, :, 0:columns] += lax.dot_general(
            turned[u % 3, 1], prob16[u % 2, 0:columns, :], ACROSS, preferred_element_type=jnp.float32
        )
        yield

    def flush_queries(u):
        s, columns = units[u][0], columns_of(u)
        for side in range(2):
            ds = dscore16[u % 2, 0:columns, lanes_of(side)]
            dqt = jnp.dot(keys_t[s, :, 0:columns], ds, preferred_element_type=jnp.float32)
            for h in range(2):
                first = (first_head(u, side) + h) * width
                dq = dqt[:, h * TILE : (h + 1) * TILE].T * score_scale
                dq_all[rows_of(u), first : first + width] = dq
            yield

    def together(*steps):
        steps = list(steps)
        while steps:
            for step in list(steps):
                if next(step, steps) is steps:
                    steps.remove(step)

    def wait_rows(u):
        s, index, g = units[u]
        if g == 0:
            q_copy(s * tiles + index).wait()
            g_copy(s * tiles + index).wait()

    count = len(units)
    per_slot = tiles * groups
    stats = [({}, {}) for _ in units]
    together(prepare(0))
    wait_rows(0)
    together(head(0, 0, stats[0][0]))
    for u in range(count):
        s = units[u][0]
        steps = [head(u, 1, stats[u][1]), tail(u, 0, stats[u][0])]
        if u >= 1:
            steps += [flush_keys(u - 1), flush_queries(u - 1)]
        if u % per_slot == 2 and s + 1 < slots:
            steps.append(prepare(s + 1))
        if u % per_slot == 1 and s >= 1:
            steps.append(finish(s - 1))
        together(*steps)
        if u >= 1 and units[u - 1][2] == groups - 1:
            dq_copy(units[u - 1][0] * tiles + units[u - 1][1]).start()
        if u % per_slot == 1 and s >= 1:
            drk_copy(s - 1).start()
            drv_copy(s - 1).start()
        steps = []
        if u + 1 < count:
            wait_rows(u + 1)
            steps.append(head(u + 1, 0, stats[u + 1][0]))
        steps.append(tail(u, 1, stats[u][1]))
        if u >= 1:
            steps.append(flush_values(u - 1))
        together(*steps)
    together(flush_keys(count - 1), flush_values(count - 1), flush_queries(count - 1))
    dq_copy(slots * tiles - 1).start()
    together(finish(slots - 1))
    drk_copy(slots - 1).start()
    drv_copy(slots - 1).start()

    for copy in term_copies:
        copy.start()
    for copy in term_copies:
        copy.wait()
    for chunk in range(slots * tiles):
        dq_copy(chunk).wait()
    for s in range(slots):
        drk_copy(s).wait()
        drv_copy(s).wait()


def slot_grads(queries, resp_keys, resp_values, out_grad, own_kv, other_kv, prompts, lengths, begins, holders):
    slots = prompts.shape[0]
    rows, columns = queries.shape
    slot_rows, width = rows // slots, resp_keys.shape[1]
    n = holders.shape[0]
    prow = 2 * own_kv.shape[0] // n
    total = prow * OWNERS + slot_rows
    tiles = slot_rows // TILE
    hbm = pl.BlockSpec(memory_space=pltpu.HBM)
    f32, bf16 = jnp.float32, jnp.bfloat16
    return pl.pallas_call(
        grad_kernel,
        in_specs=[hbm] * 10,
        out_specs=[hbm] * 5,
        out_shape=[
            jax.ShapeDtypeStruct((rows, columns), f32),
            jax.ShapeDtypeStruct((rows, width), f32),
            jax.ShapeDtypeStruct((rows, width), f32),
            jax.ShapeDtypeStruct((n * prow // 2, 2 * width), f32),
            jax.ShapeDtypeStruct((n * prow // 2, 2 * width), f32),
        ],
        scratch_shapes=[
            pltpu.SMEM((slots,), jnp.int32),
            pltpu.SMEM((slots,), jnp.int32),
            pltpu.SMEM((slots,), jnp.int32),
            pltpu.SMEM((n,), jnp.int32),
            pltpu.SMEM((n,), jnp.int32),
            pltpu.VMEM((rows, columns), bf16),
            pltpu.VMEM((rows, columns), bf16),
            pltpu.VMEM((rows, width), bf16),
            pltpu.VMEM((rows, width), bf16),
            pltpu.VMEM((rows, columns), f32),
            pltpu.VMEM((rows, width), f32),
            pltpu.VMEM((rows, width), f32),
            pltpu.VMEM((n * prow, 2 * width), bf16),
            pltpu.VMEM((n * prow, 2 * width), f32),
            pltpu.VMEM((slots, total, width), bf16),
            pltpu.VMEM((slots, total, width), bf16),
            pltpu.VMEM((slots, width, total), bf16),
            pltpu.VMEM((slots, slot_rows, TILE), f32),
            pltpu.VMEM((TILE, TILE), f32),
            pltpu.VMEM((3, 2, width, 4 * TILE), bf16),
            pltpu.VMEM((2, 2, total, 2 * TILE), f32),
            pltpu.VMEM((2, 2, total, 2 * TILE), f32),
            pltpu.VMEM((2, total, 4 * TILE), bf16),
            pltpu.VMEM((2, total, 4 * TILE), bf16),
            pltpu.VMEM((slots, width, total), f32),
            pltpu.VMEM((slots, width, total), f32),
            pltpu.SemaphoreType.DMA((4,)),
            pltpu.SemaphoreType.DMA((2,)),
            pltpu.SemaphoreType.DMA((slots * tiles,)),
            pltpu.SemaphoreType.DMA((slots * tiles,)),
            pltpu.SemaphoreType.DMA((slots * tiles,)),
            pltpu.SemaphoreType.DMA((slots,)),
            pltpu.SemaphoreType.DMA((slots,)),
            pltpu.SemaphoreType.DMA((2,)),
            pltpu.SemaphoreType.DMA((2,)),
        ],
        compiler_params=pltpu.CompilerParams(vmem_limit_bytes=60 * 1024 * 1024),
    )(prompts, lengths, begins, holders, queries, out_grad, resp_keys, resp_values, own_kv, other_kv)


def body(
    n,
    queries,
    resp_keys,
    resp_values,
    out_grad,
    prompt_keys,
    prompt_values,
    slot_prompt,
    slot_length,
    slot_begin,
    block_prompt,
):
    width = resp_keys.shape[1]
    prow = prompt_keys.shape[0]
    own = jnp.pad(prompt_keys, ((0, 0), (0, width))) + jnp.pad(prompt_values, ((0, 0), (width, 0)))
    own = jnp.broadcast_to(own[None], (n // 2, prow, 2 * width)).reshape(-1, 2 * width)
    own_kv = exchange(own, n)
    other_kv = swap_cores(own_kv, n)
    query_grad, key_grad, value_grad, own_term, other_term = slot_grads(
        queries, resp_keys, resp_values, out_grad, own_kv, other_kv,
        slot_prompt, slot_length, slot_begin, block_prompt,
    )
    parts = exchange(own_term + swap_cores(other_term, n), n)
    owned = jnp.sum(parts.reshape(n // 2, prow, 2 * width), axis=0)
    return query_grad, key_grad, value_grad, owned[:, :width], owned[:, width:]


def solution(mesh):
    n = mesh.shape["seq"]
    rows = P(("groups", "seq"), None)
    slots = P(("groups", "seq"))
    return jax.shard_map(
        functools.partial(body, n),
        mesh=mesh,
        in_specs=(rows,) * 6 + (slots,) * 3 + (P("groups"),),
        out_specs=(rows,) * 5,
        check_vma=False,
    )
```

```python
import functools
import math

import jax
import jax.numpy as jnp
from jax import lax
from jax.experimental import pallas as pl
from jax.experimental.pallas import tpu as pltpu
from jax.sharding import PartitionSpec as P

OWNERS = 8
TILE = 128
PIECE = 16
score_scale = 0.08838834764831845
EXP2_SCALE = score_scale * math.log2(math.e)
MASKED = -1e30

ACROSS = (((1,), (1,)), ((), ()))


def same_core_groups(n):
    return [list(range(core, n, 2)) for core in range(2)]


def swap_cores(x, n):
    return lax.ppermute(x, "seq", [(i, i ^ 1) for i in range(n)])


def exchange(x, n):
    return lax.all_to_all(
        x, "seq", split_axis=0, concat_axis=0, axis_index_groups=same_core_groups(n), tiled=True
    )


def block_position(holder, me, n):
    return ((holder ^ me) & 1) * (n // 2) + (holder >> 1)


def grad_kernel(
    prompt_hbm,
    length_hbm,
    begin_hbm,
    holder_hbm,
    q_hbm,
    g_hbm,
    rk_hbm,
    rv_hbm,
    own_hbm,
    other_hbm,
    dq_hbm,
    drk_hbm,
    drv_hbm,
    own_term_hbm,
    other_term_hbm,
    prompt_ref,
    length_ref,
    begin_ref,
    holder_ref,
    place,
    q_all,
    g_all,
    rk_all,
    rv_all,
    dq_all,
    drk_all,
    drv_all,
    kv,
    term_ref,
    keys,
    values,
    keys_t,
    live_bias,
    causal_bias,
    turned,
    exps,
    dprobs,
    prob16,
    dscore16,
    kt,
    vt,
    sem_scalar,
    sem_resp,
    sem_q,
    sem_g,
    sem_dq,
    sem_drk,
    sem_drv,
    sem_kv,
    sem_term,
):
    n = holder_ref.shape[0]
    slots = prompt_ref.shape[0]
    rows, width = rk_all.shape
    slot_rows = rows // slots
    tiles = slot_rows // TILE
    prow = term_ref.shape[0] // n
    prompt_len = prow * OWNERS
    heads = q_all.shape[1] // width
    me = lax.axis_index("seq")

    scalar_copies = [
        pltpu.make_async_copy(src, dst, sem_scalar.at[i])
        for i, (src, dst) in enumerate(
            [
                (prompt_hbm, prompt_ref),
                (length_hbm, length_ref),
                (begin_hbm, begin_ref),
                (holder_hbm, holder_ref),
            ]
        )
    ]
    resp_copies = [
        pltpu.make_async_copy(rk_hbm, rk_all, sem_resp.at[0]),
        pltpu.make_async_copy(rv_hbm, rv_all, sem_resp.at[1]),
    ]

    def tile_rows(chunk):
        return pl.ds(pl.multiple_of(chunk * TILE, TILE), TILE)

    def q_copy(chunk):
        part = tile_rows(chunk)
        return pltpu.make_async_copy(q_hbm.at[part], q_all.at[part], sem_q.at[chunk])

    def g_copy(chunk):
        part = tile_rows(chunk)
        return pltpu.make_async_copy(g_hbm.at[part], g_all.at[part], sem_g.at[chunk])

    def dq_copy(chunk):
        part = tile_rows(chunk)
        return pltpu.make_async_copy(dq_all.at[part], dq_hbm.at[part], sem_dq.at[chunk])

    def slot_part(s):
        return pl.ds(pl.multiple_of(s * slot_rows, slot_rows), slot_rows)

    def drk_copy(s):
        return pltpu.make_async_copy(
            drk_all.at[slot_part(s)], drk_hbm.at[slot_part(s)], sem_drk.at[s]
        )

    def drv_copy(s):
        return pltpu.make_async_copy(
            drv_all.at[slot_part(s)], drv_hbm.at[slot_part(s)], sem_drv.at[s]
        )

    half_rows = term_ref.shape[0] // 2
    kv_copies = [
        pltpu.make_async_copy(src, kv.at[pl.ds(i * half_rows, half_rows)], sem_kv.at[i])
        for i, src in enumerate([own_hbm, other_hbm])
    ]
    term_copies = [
        pltpu.make_async_copy(term_ref.at[pl.ds(i * half_rows, half_rows)], dst, sem_term.at[i])
        for i, dst in enumerate([own_term_hbm, other_term_hbm])
    ]
    for copy in scalar_copies + kv_copies + resp_copies:
        copy.start()
    for chunk in range(slots * tiles):
        q_copy(chunk).start()
        g_copy(chunk).start()

    term_ref[...] = jnp.zeros_like(term_ref)
    causal_bias[...] = jnp.where(
        lax.broadcasted_iota(jnp.int32, (TILE, TILE), 0)
        <= lax.broadcasted_iota(jnp.int32, (TILE, TILE), 1),
        0.0,
        MASKED,
    )
    for copy in scalar_copies + kv_copies + resp_copies:
        copy.wait()

    @pl.loop(0, n)
    def _(j):
        place[holder_ref[j]] = j

    wide = 2 * TILE
    at_once = 4
    groups = heads // at_once
    units = [(s, index, g) for s in range(slots) for index in range(tiles) for g in range(groups)]

    def columns_of(u):
        return prompt_len + (units[u][1] + 1) * TILE

    def rows_of(u):
        s, index, _ = units[u]
        first = (s * tiles + index) * TILE
        return slice(first, first + TILE)

    def first_head(u, side):
        return units[u][2] * at_once + 2 * side

    def chunks(u):
        return range(0, columns_of(u), TILE)

    def lanes_of(side):
        return slice(side * wide, (side + 1) * wide)

    def stacked(ref, u, side):
        first = first_head(u, side)
        return jnp.concatenate(
            [ref[rows_of(u), (first + h) * width : (first + h + 1) * width] for h in range(2)], axis=0
        )

    def fold(x, how):
        return how(how(x.reshape(x.shape[0] // 8, 8, x.shape[1]), axis=0), axis=0, keepdims=True)

    def prepare(s):
        first_block = prompt_ref[s] * OWNERS
        for o in range(OWNERS):
            start = block_position(place[first_block + o], me, n) * prow
            source = pl.ds(pl.multiple_of(start, prow), prow)
            keys[s, o * prow : (o + 1) * prow, :] = kv[source, 0:width]
            values[s, o * prow : (o + 1) * prow, :] = kv[source, width : 2 * width]
        own = slice(s * slot_rows, (s + 1) * slot_rows)
        keys[s, prompt_len:, :] = rk_all[own, :]
        values[s, prompt_len:, :] = rv_all[own, :]
        yield
        keys_t[s] = keys[s].astype(jnp.float32).T.astype(jnp.bfloat16)
        yield
        column = lax.broadcasted_iota(jnp.int32, (slot_rows, TILE), 0)
        live_bias[s] = jnp.where(column >= begin_ref[s], 0.0, MASKED)
        kt[s] = jnp.zeros_like(kt[s])
        vt[s] = jnp.zeros_like(vt[s])
        yield

    def finish(s):
        own = slice(s * slot_rows, (s + 1) * slot_rows)
        prompt_kt = kt[s, :, 0:prompt_len].T * score_scale
        prompt_vt = vt[s, :, 0:prompt_len].T
        yield
        drk_all[own, :] = kt[s, :, prompt_len:].T * score_scale
        drv_all[own, :] = vt[s, :, prompt_len:].T
        yield
        first_block = prompt_ref[s] * OWNERS
        for o in range(OWNERS):
            start = block_position(place[first_block + o], me, n) * prow
            target = pl.ds(pl.multiple_of(start, prow), prow)
            block = slice(o * prow, (o + 1) * prow)
            term_ref[target, 0:width] += prompt_kt[block]
            term_ref[target, width : 2 * width] += prompt_vt[block]
        yield

    def head(u, side, out):
        s, index, _ = units[u]
        columns, buf = columns_of(u), u % 2
        q2t, g2t = turned.at[u % 3, 0, :, lanes_of(side)], turned.at[u % 3, 1, :, lanes_of(side)]
        q2t[...] = stacked(q_all, u, side).T
        g2t[...] = stacked(g_all, u, side).T
        tops, totals, weights = [], [], []
        all_scores = jnp.dot(keys[s, 0:columns, :], q2t[...], preferred_element_type=jnp.float32)
        all_dprobs = jnp.dot(values[s, 0:columns, :], g2t[...], preferred_element_type=jnp.float32)
        for c in chunks(u):
            part = slice(c, c + TILE)
            block = all_scores[part]
            if c >= prompt_len:
                bias = live_bias[s, c - prompt_len : c - prompt_len + TILE, :]
                if c + TILE == columns:
                    bias = bias + causal_bias[...]
                block = block + jnp.concatenate([bias, bias], axis=1)
            top = fold(block, jnp.max) * EXP2_SCALE
            e = jnp.exp2(block * EXP2_SCALE - top)
            exps[buf, side, part, :] = e
            yield
            d = all_dprobs[part]
            dprobs[buf, side, part, :] = d
            tops.append(top)
            totals.append(fold(e, jnp.sum))
            weights.append(fold(e * d, jnp.sum))
            yield
        top = functools.reduce(jnp.maximum, tops)
        factors = [jnp.exp2(part - top) for part in tops]
        total = functools.reduce(jnp.add, [f * x for f, x in zip(factors, totals)])
        weighted = functools.reduce(jnp.add, [f * x for f, x in zip(factors, weights)])
        row = index * TILE + lax.broadcasted_iota(jnp.int32, (1, TILE), 1)
        live = (row >= begin_ref[s]) & (row < begin_ref[s] + length_ref[s])
        inverse = jnp.where(jnp.concatenate([live, live], axis=1), 1.0 / total, 0.0)
        out["delta"] = weighted * inverse
        out["factors"] = [f * inverse for f in factors]

    def tail(u, side, stats):
        buf, lanes = u % 2, lanes_of(side)
        delta = stats["delta"]
        for c, factor in zip(chunks(u), stats["factors"]):
            for first in range(c, c + TILE, PIECE):
                part = slice(first, first + PIECE)
                p = exps[buf, side, part, :] * factor
                prob16[buf, part, lanes] = p.astype(jnp.bfloat16)
                ds = p * (dprobs[buf, side, part, :] - delta)
                dscore16[buf, part, lanes] = ds.astype(jnp.bfloat16)
            yield

    def flush_keys(u):
        s, columns = units[u][0], columns_of(u)
        kt[s, :, 0:columns] += lax.dot_general(
            turned[u % 3, 0], dscore16[u % 2, 0:columns, :], ACROSS, preferred_element_type=jnp.float32
        )
        yield

    def flush_values(u):
        s, columns = units[u][0], columns_of(u)
        vt[s, :, 0:columns] += lax.dot_general(
            turned[u % 3, 1], prob16[u % 2, 0:columns, :], ACROSS, preferred_element_type=jnp.float32
        )
        yield

    def flush_queries(u):
        s, columns = units[u][0], columns_of(u)
        for side in range(2):
            ds = dscore16[u % 2, 0:columns, lanes_of(side)]
            dqt = jnp.dot(keys_t[s, :, 0:columns], ds, preferred_element_type=jnp.float32)
            for h in range(2):
                first = (first_head(u, side) + h) * width
                dq = dqt[:, h * TILE : (h + 1) * TILE].T * score_scale
                dq_all[rows_of(u), first : first + width] = dq
            yield

    def together(*steps):
        steps = list(steps)
        while steps:
            for step in list(steps):
                if next(step, steps) is steps:
                    steps.remove(step)

    def wait_rows(u):
        s, index, g = units[u]
        if g == 0:
            q_copy(s * tiles + index).wait()
            g_copy(s * tiles + index).wait()

    count = len(units)
    per_slot = tiles * groups
    stats = [({}, {}) for _ in units]
    together(prepare(0))
    wait_rows(0)
    together(head(0, 0, stats[0][0]))
    for u in range(count):
        s = units[u][0]
        steps = [head(u, 1, stats[u][1]), tail(u, 0, stats[u][0])]
        if u >= 1:
            steps += [flush_keys(u - 1), flush_queries(u - 1)]
        if u % per_slot == 2 and s + 1 < slots:
            steps.append(prepare(s + 1))
        if u % per_slot == 1 and s >= 1:
            steps.append(finish(s - 1))
        together(*steps)
        if u >= 1 and units[u - 1][2] == groups - 1:
            dq_copy(units[u - 1][0] * tiles + units[u - 1][1]).start()
        if u % per_slot == 1 and s >= 1:
            drk_copy(s - 1).start()
            drv_copy(s - 1).start()
        steps = []
        if u + 1 < count:
            wait_rows(u + 1)
            steps.append(head(u + 1, 0, stats[u + 1][0]))
        steps.append(tail(u, 1, stats[u][1]))
        if u >= 1:
            steps.append(flush_values(u - 1))
        together(*steps)
    together(flush_keys(count - 1), flush_values(count - 1), flush_queries(count - 1))
    dq_copy(slots * tiles - 1).start()
    together(finish(slots - 1))
    drk_copy(slots - 1).start()
    drv_copy(slots - 1).start()

    for copy in term_copies:
        copy.start()
    for copy in term_copies:
        copy.wait()
    for chunk in range(slots * tiles):
        dq_copy(chunk).wait()
    for s in range(slots):
        drk_copy(s).wait()
        drv_copy(s).wait()


def slot_grads(queries, resp_keys, resp_values, out_grad, own_kv, other_kv, prompts, lengths, begins, holders):
    slots = prompts.shape[0]
    rows, columns = queries.shape
    slot_rows, width = rows // slots, resp_keys.shape[1]
    n = holders.shape[0]
    prow = 2 * own_kv.shape[0] // n
    total = prow * OWNERS + slot_rows
    tiles = slot_rows // TILE
    hbm = pl.BlockSpec(memory_space=pltpu.HBM)
    f32, bf16 = jnp.float32, jnp.bfloat16
    return pl.pallas_call(
        grad_kernel,
        in_specs=[hbm] * 10,
        out_specs=[hbm] * 5,
        out_shape=[
            jax.ShapeDtypeStruct((rows, columns), f32),
            jax.ShapeDtypeStruct((rows, width), f32),
            jax.ShapeDtypeStruct((rows, width), f32),
            jax.ShapeDtypeStruct((n * prow // 2, 2 * width), f32),
            jax.ShapeDtypeStruct((n * prow // 2, 2 * width), f32),
        ],
        scratch_shapes=[
            pltpu.SMEM((slots,), jnp.int32),
            pltpu.SMEM((slots,), jnp.int32),
            pltpu.SMEM((slots,), jnp.int32),
            pltpu.SMEM((n,), jnp.int32),
            pltpu.SMEM((n,), jnp.int32),
            pltpu.VMEM((rows, columns), bf16),
            pltpu.VMEM((rows, columns), bf16),
            pltpu.VMEM((rows, width), bf16),
            pltpu.VMEM((rows, width), bf16),
            pltpu.VMEM((rows, columns), f32),
            pltpu.VMEM((rows, width), f32),
            pltpu.VMEM((rows, width), f32),
            pltpu.VMEM((n * prow, 2 * width), bf16),
            pltpu.VMEM((n * prow, 2 * width), f32),
            pltpu.VMEM((slots, total, width), bf16),
            pltpu.VMEM((slots, total, width), bf16),
            pltpu.VMEM((slots, width, total), bf16),
            pltpu.VMEM((slots, slot_rows, TILE), f32),
            pltpu.VMEM((TILE, TILE), f32),
            pltpu.VMEM((3, 2, width, 4 * TILE), bf16),
            pltpu.VMEM((2, 2, total, 2 * TILE), f32),
            pltpu.VMEM((2, 2, total, 2 * TILE), f32),
            pltpu.VMEM((2, total, 4 * TILE), bf16),
            pltpu.VMEM((2, total, 4 * TILE), bf16),
            pltpu.VMEM((slots, width, total), f32),
            pltpu.VMEM((slots, width, total), f32),
            pltpu.SemaphoreType.DMA((4,)),
            pltpu.SemaphoreType.DMA((2,)),
            pltpu.SemaphoreType.DMA((slots * tiles,)),
            pltpu.SemaphoreType.DMA((slots * tiles,)),
            pltpu.SemaphoreType.DMA((slots * tiles,)),
            pltpu.SemaphoreType.DMA((slots,)),
            pltpu.SemaphoreType.DMA((slots,)),
            pltpu.SemaphoreType.DMA((2,)),
            pltpu.SemaphoreType.DMA((2,)),
        ],
        compiler_params=pltpu.CompilerParams(vmem_limit_bytes=60 * 1024 * 1024),
    )(prompts, lengths, begins, holders, queries, out_grad, resp_keys, resp_values, own_kv, other_kv)


def body(
    n,
    queries,
    resp_keys,
    resp_values,
    out_grad,
    prompt_keys,
    prompt_values,
    slot_prompt,
    slot_length,
    slot_begin,
    block_prompt,
):
    width = resp_keys.shape[1]
    prow = prompt_keys.shape[0]
    own = jnp.pad(prompt_keys, ((0, 0), (0, width))) + jnp.pad(prompt_values, ((0, 0), (width, 0)))
    own = jnp.broadcast_to(own[None], (n // 2, prow, 2 * width)).reshape(-1, 2 * width)
    own_kv = exchange(own, n)
    other_kv = swap_cores(own_kv, n)
    query_grad, key_grad, value_grad, own_term, other_term = slot_grads(
        queries, resp_keys, resp_values, out_grad, own_kv, other_kv,
        slot_prompt, slot_length, slot_begin, block_prompt,
    )
    parts = exchange(own_term + swap_cores(other_term, n), n)
    owned = jnp.sum(parts.reshape(n // 2, prow, 2 * width), axis=0)
    return query_grad, key_grad, value_grad, owned[:, :width], owned[:, width:]


def solution(mesh):
    n = mesh.shape["seq"]
    rows = P(("groups", "seq"), None)
    slots = P(("groups", "seq"))
    return jax.shard_map(
        functools.partial(body, n),
        mesh=mesh,
        in_specs=(rows,) * 6 + (slots,) * 3 + (P("groups"),),
        out_specs=(rows,) * 5,
        check_vma=False,
    )
```

```python
import functools
import math

import jax
import jax.numpy as jnp
from jax import lax
from jax.experimental import pallas as pl
from jax.experimental.pallas import tpu as pltpu
from jax.sharding import PartitionSpec as P

OWNERS = 8
TILE = 128
PIECE = 16
PARTS = 3
score_scale = 0.08838834764831845
EXP2_SCALE = score_scale * math.log2(math.e)
MASKED = -1e30

ACROSS = (((1,), (1,)), ((), ()))


def same_core_groups(n):
    return [list(range(core, n, 2)) for core in range(2)]


def swap_cores(x, n):
    return lax.ppermute(x, "seq", [(i, i ^ 1) for i in range(n)])


def exchange(x, n):
    return lax.all_to_all(
        x, "seq", split_axis=0, concat_axis=0, axis_index_groups=same_core_groups(n), tiled=True
    )


def block_position(holder, me, n):
    return ((holder ^ me) & 1) * (n // 2) + (holder >> 1)


def grad_kernel(
    prompt_hbm,
    length_hbm,
    begin_hbm,
    holder_hbm,
    q_hbm,
    g_hbm,
    rk_hbm,
    rv_hbm,
    own_hbm,
    other_hbm,
    dq_hbm,
    drk_hbm,
    drv_hbm,
    own_term_hbm,
    other_term_hbm,
    prompt_ref,
    length_ref,
    begin_ref,
    holder_ref,
    place,
    q_all,
    g_all,
    rk_all,
    rv_all,
    dq_all,
    drk_all,
    drv_all,
    kv,
    term_ref,
    keys,
    scaled_keys,
    values,
    keys_t,
    values_t,
    live_bias,
    causal_bias,
    turned_q,
    turned_g,
    exps,
    prob16,
    dscore16,
    kt,
    vt,
    sem_scalar,
    sem_resp,
    sem_q,
    sem_g,
    sem_dq,
    sem_drk,
    sem_drv,
    sem_kv,
    sem_term,
):
    n = holder_ref.shape[0]
    slots = prompt_ref.shape[0]
    rows, width = rk_all.shape
    slot_rows = rows // slots
    tiles = slot_rows // TILE
    prow = term_ref.shape[0] // n
    prompt_len = prow * OWNERS
    heads = q_all.shape[1] // width
    me = lax.axis_index("seq")

    scalar_copies = [
        pltpu.make_async_copy(src, dst, sem_scalar.at[i])
        for i, (src, dst) in enumerate(
            [
                (prompt_hbm, prompt_ref),
                (length_hbm, length_ref),
                (begin_hbm, begin_ref),
                (holder_hbm, holder_ref),
            ]
        )
    ]
    resp_copies = [
        pltpu.make_async_copy(rk_hbm, rk_all, sem_resp.at[0]),
        pltpu.make_async_copy(rv_hbm, rv_all, sem_resp.at[1]),
    ]

    def tile_rows(chunk):
        return pl.ds(pl.multiple_of(chunk * TILE, TILE), TILE)

    def q_copy(chunk):
        part = tile_rows(chunk)
        return pltpu.make_async_copy(q_hbm.at[part], q_all.at[part], sem_q.at[chunk])

    def g_copy(chunk):
        part = tile_rows(chunk)
        return pltpu.make_async_copy(g_hbm.at[part], g_all.at[part], sem_g.at[chunk])

    def dq_copy(chunk):
        part = tile_rows(chunk)
        return pltpu.make_async_copy(dq_all.at[part], dq_hbm.at[part], sem_dq.at[chunk])

    def slot_part(s):
        return pl.ds(pl.multiple_of(s * slot_rows, slot_rows), slot_rows)

    def drk_copy(s):
        return pltpu.make_async_copy(
            drk_all.at[slot_part(s)], drk_hbm.at[slot_part(s)], sem_drk.at[s]
        )

    def drv_copy(s):
        return pltpu.make_async_copy(
            drv_all.at[slot_part(s)], drv_hbm.at[slot_part(s)], sem_drv.at[s]
        )

    half_rows = term_ref.shape[0] // 2
    kv_copies = [
        pltpu.make_async_copy(src, kv.at[pl.ds(i * half_rows, half_rows)], sem_kv.at[i])
        for i, src in enumerate([own_hbm, other_hbm])
    ]
    term_copies = [
        pltpu.make_async_copy(term_ref.at[pl.ds(i * half_rows, half_rows)], dst, sem_term.at[i])
        for i, dst in enumerate([own_term_hbm, other_term_hbm])
    ]
    for copy in scalar_copies + kv_copies + resp_copies:
        copy.start()
    for chunk in range(slots * tiles):
        q_copy(chunk).start()
        g_copy(chunk).start()

    term_ref[...] = jnp.zeros_like(term_ref)
    causal_bias[...] = jnp.where(
        lax.broadcasted_iota(jnp.int32, (TILE, TILE), 0)
        <= lax.broadcasted_iota(jnp.int32, (TILE, TILE), 1),
        0.0,
        MASKED,
    )
    for copy in scalar_copies + kv_copies + resp_copies:
        copy.wait()

    @pl.loop(0, n)
    def _(j):
        place[holder_ref[j]] = j

    wide = 2 * TILE
    at_once = 4
    groups = heads // at_once
    units = [(s, index, g) for s in range(slots) for index in range(tiles) for g in range(groups)]

    def columns_of(u):
        return prompt_len + (units[u][1] + 1) * TILE

    def rows_of(u):
        s, index, _ = units[u]
        first = (s * tiles + index) * TILE
        return slice(first, first + TILE)

    def first_head(u, side):
        return units[u][2] * at_once + 2 * side

    def chunks(u):
        return range(0, columns_of(u), TILE)

    def lanes_of(side):
        return slice(side * wide, (side + 1) * wide)

    def stacked(ref, u, side):
        first = first_head(u, side)
        return jnp.concatenate(
            [ref[rows_of(u), (first + h) * width : (first + h + 1) * width] for h in range(2)], axis=0
        )

    def fold(x, how):
        return how(how(x.reshape(x.shape[0] // 8, 8, x.shape[1]), axis=0), axis=0, keepdims=True)

    def prepare(s):
        first_block = prompt_ref[s] * OWNERS
        for o in range(OWNERS):
            start = block_position(place[first_block + o], me, n) * prow
            source = pl.ds(pl.multiple_of(start, prow), prow)
            keys[o * prow : (o + 1) * prow, :] = kv[source, 0:width]
            values[s, o * prow : (o + 1) * prow, 0:width] = kv[source, width : 2 * width]
        own = slice(s * slot_rows, (s + 1) * slot_rows)
        keys[prompt_len:, :] = rk_all[own, :]
        values[s, prompt_len:, 0:width] = rv_all[own, :]
        lane = lax.broadcasted_iota(jnp.int32, (keys.shape[0], width), 1)
        values[s, :, width:] = jnp.where(lane < PARTS, 1.0, 0.0).astype(jnp.bfloat16)
        yield
        wide_keys = keys[...].astype(jnp.float32)
        keys_t[s] = wide_keys.T.astype(jnp.bfloat16)
        values_t[s] = values[s, :, 0:width].astype(jnp.float32).T.astype(jnp.bfloat16)
        yield
        scaled = wide_keys * EXP2_SCALE
        high = scaled.astype(jnp.bfloat16)
        scaled_keys[s, :, 0:width] = high
        scaled_keys[s, :, width:] = (scaled - high.astype(jnp.float32)).astype(jnp.bfloat16)
        yield
        column = lax.broadcasted_iota(jnp.int32, (slot_rows, TILE), 0)
        live_bias[s] = jnp.where(column >= begin_ref[s], 0.0, MASKED)
        kt[s] = jnp.zeros_like(kt[s])
        vt[s] = jnp.zeros_like(vt[s])
        yield

    def finish(s):
        own = slice(s * slot_rows, (s + 1) * slot_rows)
        prompt_kt = kt[s, :, 0:prompt_len].T * score_scale
        prompt_vt = vt[s, :, 0:prompt_len].T
        yield
        drk_all[own, :] = kt[s, :, prompt_len:].T * score_scale
        drv_all[own, :] = vt[s, :, prompt_len:].T
        yield
        first_block = prompt_ref[s] * OWNERS
        for o in range(OWNERS):
            start = block_position(place[first_block + o], me, n) * prow
            target = pl.ds(pl.multiple_of(start, prow), prow)
            block = slice(o * prow, (o + 1) * prow)
            term_ref[target, 0:width] += prompt_kt[block]
            term_ref[target, width : 2 * width] += prompt_vt[block]
        yield

    def head(u, side, out):
        s, index, _ = units[u]
        columns, buf, lanes = columns_of(u), (2 * u + side) % 3, lanes_of(side)
        q2t = stacked(q_all, u, side).T
        turned_q[u % 3, 0:width, lanes] = q2t
        turned_q[u % 3, width:, lanes] = q2t
        turned_g[u % 3, 0:width, lanes] = stacked(g_all, u, side).T
        tops, totals = [], []
        for c in chunks(u):
            part = slice(c, c + TILE)
            block = jnp.dot(
                scaled_keys[s, part, :], turned_q[u % 3, :, lanes], preferred_element_type=jnp.float32
            )
            if c >= prompt_len:
                bias = live_bias[s, c - prompt_len : c - prompt_len + TILE, :]
                if c + TILE == columns:
                    bias = bias + causal_bias[...]
                block = block + jnp.concatenate([bias, bias], axis=1)
            top = fold(block, jnp.max)
            e = jnp.exp2(block - top)
            exps[buf, part, :] = e
            tops.append(top)
            totals.append(fold(e, jnp.sum))
            yield
        top = functools.reduce(jnp.maximum, tops)
        factors = [jnp.exp2(part - top) for part in tops]
        total = functools.reduce(jnp.add, [f * x for f, x in zip(factors, totals)])
        row = index * TILE + lax.broadcasted_iota(jnp.int32, (1, TILE), 1)
        live = (row >= begin_ref[s]) & (row < begin_ref[s] + length_ref[s])
        inverse = jnp.where(jnp.concatenate([live, live], axis=1), 1.0 / total, 0.0)
        out["factors"] = [f * inverse for f in factors]

    def middle(u, side, stats):
        s, columns, buf, lanes = units[u][0], columns_of(u), (2 * u + side) % 3, lanes_of(side)
        for c, factor in zip(chunks(u), stats["factors"]):
            for first in range(c, c + TILE, PIECE):
                part = slice(first, first + PIECE)
                p = exps[buf, part, :] * factor
                exps[buf, part, :] = p
                prob16[u % 3, part, lanes] = p.astype(jnp.bfloat16)
            yield
        attended = jnp.dot(
            values_t[s, :, 0:columns], prob16[u % 3, 0:columns, lanes], preferred_element_type=jnp.float32
        )
        grad = turned_g[u % 3, 0:width, lanes].astype(jnp.float32)
        rest = -fold(attended * grad, jnp.sum)
        row = lax.broadcasted_iota(jnp.int32, (PIECE, wide), 0)
        parts = jnp.zeros((PIECE, wide), jnp.float32)
        for i in range(PARTS):
            rounded = rest.astype(jnp.bfloat16).astype(jnp.float32)
            parts = jnp.where(row == i, rounded, parts)
            rest = rest - rounded
        turned_g[u % 3, width : width + PIECE, lanes] = parts.astype(jnp.bfloat16)
        yield

    def tail(u, side):
        s, buf, lanes = units[u][0], (2 * u + side) % 3, lanes_of(side)
        for c in chunks(u):
            part = slice(c, c + TILE)
            d = jnp.dot(
                values[s, part, :], turned_g[u % 3, :, lanes], preferred_element_type=jnp.float32
            )
            dscore16[u % 3, part, lanes] = (exps[buf, part, :] * d).astype(jnp.bfloat16)
            yield

    def flush_keys(u):
        s, columns = units[u][0], columns_of(u)
        kt[s, :, 0:columns] += lax.dot_general(
            turned_q[u % 3, 0:width, :],
            dscore16[u % 3, 0:columns, :],
            ACROSS,
            preferred_element_type=jnp.float32,
        )
        yield

    def flush_values(u):
        s, columns = units[u][0], columns_of(u)
        vt[s, :, 0:columns] += lax.dot_general(
            turned_g[u % 3, 0:width, :],
            prob16[u % 3, 0:columns, :],
            ACROSS,
            preferred_element_type=jnp.float32,
        )
        yield

    def flush_queries(u):
        s, columns = units[u][0], columns_of(u)
        for side in range(2):
            ds = dscore16[u % 3, 0:columns, lanes_of(side)]
            dqt = jnp.dot(keys_t[s, :, 0:columns], ds, preferred_element_type=jnp.float32)
            for h in range(2):
                first = (first_head(u, side) + h) * width
                dq = dqt[:, h * TILE : (h + 1) * TILE].T * score_scale
                dq_all[rows_of(u), first : first + width] = dq
            yield

    def together(*steps):
        steps = list(steps)
        while steps:
            for step in list(steps):
                if next(step, steps) is steps:
                    steps.remove(step)

    def wait_rows(u):
        s, index, g = units[u]
        if g == 0:
            q_copy(s * tiles + index).wait()
            g_copy(s * tiles + index).wait()

    count = len(units)
    per_slot = tiles * groups
    pairs = [(u, side) for u in range(count) for side in range(2)]
    stats = [{} for _ in pairs]
    turned_g[:, width:, :] = jnp.zeros_like(turned_g[:, width:, :])
    together(prepare(0))
    for t in range(len(pairs) + 4):
        steps = []
        if t < len(pairs):
            u, side = pairs[t]
            if side == 0:
                wait_rows(u)
            steps.append(head(u, side, stats[t]))
            if u % per_slot == 2 and side == 0 and units[u][0] + 1 < slots:
                steps.append(prepare(units[u][0] + 1))
        if 0 <= t - 1 < len(pairs):
            steps.append(middle(*pairs[t - 1], stats[t - 1]))
        if 0 <= t - 2 < len(pairs):
            steps.append(tail(*pairs[t - 2]))
        done = t // 2 - 2
        if 0 <= done < count and t % 2 == 0:
            steps += [flush_keys(done), flush_queries(done)]
        elif 0 <= done < count:
            steps.append(flush_values(done))
        ended = (done - 1) // per_slot
        finished = 0 <= done - 1 < count and (done - 1) % per_slot == per_slot - 1 and t % 2 == 0
        if finished:
            steps.append(finish(ended))
        together(*steps)
        if 0 <= done < count and t % 2 == 0 and units[done][2] == groups - 1:
            dq_copy(units[done][0] * tiles + units[done][1]).start()
        if finished:
            drk_copy(ended).start()
            drv_copy(ended).start()
    together(finish(slots - 1))
    drk_copy(slots - 1).start()
    drv_copy(slots - 1).start()

    for copy in term_copies:
        copy.start()
    for copy in term_copies:
        copy.wait()
    for chunk in range(slots * tiles):
        dq_copy(chunk).wait()
    for s in range(slots):
        drk_copy(s).wait()
        drv_copy(s).wait()


def slot_grads(queries, resp_keys, resp_values, out_grad, own_kv, other_kv, prompts, lengths, begins, holders):
    slots = prompts.shape[0]
    rows, columns = queries.shape
    slot_rows, width = rows // slots, resp_keys.shape[1]
    n = holders.shape[0]
    prow = 2 * own_kv.shape[0] // n
    total = prow * OWNERS + slot_rows
    tiles = slot_rows // TILE
    hbm = pl.BlockSpec(memory_space=pltpu.HBM)
    f32, bf16 = jnp.float32, jnp.bfloat16
    return pl.pallas_call(
        grad_kernel,
        in_specs=[hbm] * 10,
        out_specs=[hbm] * 5,
        out_shape=[
            jax.ShapeDtypeStruct((rows, columns), f32),
            jax.ShapeDtypeStruct((rows, width), f32),
            jax.ShapeDtypeStruct((rows, width), f32),
            jax.ShapeDtypeStruct((n * prow // 2, 2 * width), f32),
            jax.ShapeDtypeStruct((n * prow // 2, 2 * width), f32),
        ],
        scratch_shapes=[
            pltpu.SMEM((slots,), jnp.int32),
            pltpu.SMEM((slots,), jnp.int32),
            pltpu.SMEM((slots,), jnp.int32),
            pltpu.SMEM((n,), jnp.int32),
            pltpu.SMEM((n,), jnp.int32),
            pltpu.VMEM((rows, columns), bf16),
            pltpu.VMEM((rows, columns), bf16),
            pltpu.VMEM((rows, width), bf16),
            pltpu.VMEM((rows, width), bf16),
            pltpu.VMEM((rows, columns), f32),
            pltpu.VMEM((rows, width), f32),
            pltpu.VMEM((rows, width), f32),
            pltpu.VMEM((n * prow, 2 * width), bf16),
            pltpu.VMEM((n * prow, 2 * width), f32),
            pltpu.VMEM((total, width), bf16),
            pltpu.VMEM((slots, total, 2 * width), bf16),
            pltpu.VMEM((slots, total, 2 * width), bf16),
            pltpu.VMEM((slots, width, total), bf16),
            pltpu.VMEM((slots, width, total), bf16),
            pltpu.VMEM((slots, slot_rows, TILE), f32),
            pltpu.VMEM((TILE, TILE), f32),
            pltpu.VMEM((3, 2 * width, 4 * TILE), bf16),
            pltpu.VMEM((3, 2 * width, 4 * TILE), bf16),
            pltpu.VMEM((3, total, 2 * TILE), f32),
            pltpu.VMEM((3, total, 4 * TILE), bf16),
            pltpu.VMEM((3, total, 4 * TILE), bf16),
            pltpu.VMEM((slots, width, total), f32),
            pltpu.VMEM((slots, width, total), f32),
            pltpu.SemaphoreType.DMA((4,)),
            pltpu.SemaphoreType.DMA((2,)),
            pltpu.SemaphoreType.DMA((slots * tiles,)),
            pltpu.SemaphoreType.DMA((slots * tiles,)),
            pltpu.SemaphoreType.DMA((slots * tiles,)),
            pltpu.SemaphoreType.DMA((slots,)),
            pltpu.SemaphoreType.DMA((slots,)),
            pltpu.SemaphoreType.DMA((2,)),
            pltpu.SemaphoreType.DMA((2,)),
        ],
        compiler_params=pltpu.CompilerParams(vmem_limit_bytes=60 * 1024 * 1024),
    )(prompts, lengths, begins, holders, queries, out_grad, resp_keys, resp_values, own_kv, other_kv)


def body(
    n,
    queries,
    resp_keys,
    resp_values,
    out_grad,
    prompt_keys,
    prompt_values,
    slot_prompt,
    slot_length,
    slot_begin,
    block_prompt,
):
    width = resp_keys.shape[1]
    prow = prompt_keys.shape[0]
    own = jnp.pad(prompt_keys, ((0, 0), (0, width))) + jnp.pad(prompt_values, ((0, 0), (width, 0)))
    own = jnp.broadcast_to(own[None], (n // 2, prow, 2 * width)).reshape(-1, 2 * width)
    own_kv = exchange(own, n)
    other_kv = swap_cores(own_kv, n)
    query_grad, key_grad, value_grad, own_term, other_term = slot_grads(
        queries, resp_keys, resp_values, out_grad, own_kv, other_kv,
        slot_prompt, slot_length, slot_begin, block_prompt,
    )
    parts = exchange(own_term + swap_cores(other_term, n), n)
    owned = jnp.sum(parts.reshape(n // 2, prow, 2 * width), axis=0)
    return query_grad, key_grad, value_grad, owned[:, :width], owned[:, width:]


def solution(mesh):
    n = mesh.shape["seq"]
    rows = P(("groups", "seq"), None)
    slots = P(("groups", "seq"))
    return jax.shard_map(
        functools.partial(body, n),
        mesh=mesh,
        in_specs=(rows,) * 6 + (slots,) * 3 + (P("groups"),),
        out_specs=(rows,) * 5,
        check_vma=False,
    )
```

```python
import functools
import math

import jax
import jax.numpy as jnp
from jax import lax
from jax.experimental import pallas as pl
from jax.experimental.pallas import tpu as pltpu
from jax.sharding import PartitionSpec as P

OWNERS = 8
TILE = 128
PIECE = 16
score_scale = 0.08838834764831845
EXP2_SCALE = score_scale * math.log2(math.e)
MASKED = -1e30

ACROSS = (((1,), (1,)), ((), ()))


def same_core_groups(n):
    return [list(range(core, n, 2)) for core in range(2)]


def swap_cores(x, n):
    return lax.ppermute(x, "seq", [(i, i ^ 1) for i in range(n)])


def exchange(x, n):
    return lax.all_to_all(
        x, "seq", split_axis=0, concat_axis=0, axis_index_groups=same_core_groups(n), tiled=True
    )


def block_position(holder, me, n):
    return ((holder ^ me) & 1) * (n // 2) + (holder >> 1)


def grad_kernel(
    prompt_hbm,
    length_hbm,
    begin_hbm,
    holder_hbm,
    q_hbm,
    g_hbm,
    rk_hbm,
    rv_hbm,
    own_hbm,
    other_hbm,
    dq_hbm,
    drk_hbm,
    drv_hbm,
    own_term_hbm,
    other_term_hbm,
    prompt_ref,
    length_ref,
    begin_ref,
    holder_ref,
    place,
    q_all,
    g_all,
    rk_all,
    rv_all,
    dq_all,
    drk_all,
    drv_all,
    kv,
    term_ref,
    keys,
    values,
    keys_t,
    live_bias,
    causal_bias,
    turned,
    exps,
    dprobs,
    prob16,
    dscore16,
    kt,
    vt,
    sem_scalar,
    sem_resp,
    sem_q,
    sem_g,
    sem_dq,
    sem_drk,
    sem_drv,
    sem_kv,
    sem_term,
):
    n = holder_ref.shape[0]
    slots = prompt_ref.shape[0]
    rows, width = rk_all.shape
    slot_rows = rows // slots
    tiles = slot_rows // TILE
    prow = term_ref.shape[0] // n
    prompt_len = prow * OWNERS
    heads = q_all.shape[1] // width
    me = lax.axis_index("seq")

    scalar_copies = [
        pltpu.make_async_copy(src, dst, sem_scalar.at[i])
        for i, (src, dst) in enumerate(
            [
                (prompt_hbm, prompt_ref),
                (length_hbm, length_ref),
                (begin_hbm, begin_ref),
                (holder_hbm, holder_ref),
            ]
        )
    ]
    resp_copies = [
        pltpu.make_async_copy(rk_hbm, rk_all, sem_resp.at[0]),
        pltpu.make_async_copy(rv_hbm, rv_all, sem_resp.at[1]),
    ]

    def tile_rows(chunk):
        return pl.ds(pl.multiple_of(chunk * TILE, TILE), TILE)

    def q_copy(chunk):
        part = tile_rows(chunk)
        return pltpu.make_async_copy(q_hbm.at[part], q_all.at[part], sem_q.at[chunk])

    def g_copy(chunk):
        part = tile_rows(chunk)
        return pltpu.make_async_copy(g_hbm.at[part], g_all.at[part], sem_g.at[chunk])

    def dq_copy(chunk):
        part = tile_rows(chunk)
        return pltpu.make_async_copy(dq_all.at[part], dq_hbm.at[part], sem_dq.at[chunk])

    def slot_part(s):
        return pl.ds(pl.multiple_of(s * slot_rows, slot_rows), slot_rows)

    def drk_copy(s):
        return pltpu.make_async_copy(
            drk_all.at[slot_part(s)], drk_hbm.at[slot_part(s)], sem_drk.at[s]
        )

    def drv_copy(s):
        return pltpu.make_async_copy(
            drv_all.at[slot_part(s)], drv_hbm.at[slot_part(s)], sem_drv.at[s]
        )

    half_rows = term_ref.shape[0] // 2
    kv_copies = [
        pltpu.make_async_copy(src, kv.at[pl.ds(i * half_rows, half_rows)], sem_kv.at[i])
        for i, src in enumerate([own_hbm, other_hbm])
    ]
    term_copies = [
        pltpu.make_async_copy(term_ref.at[pl.ds(i * half_rows, half_rows)], dst, sem_term.at[i])
        for i, dst in enumerate([own_term_hbm, other_term_hbm])
    ]
    for copy in scalar_copies + kv_copies + resp_copies:
        copy.start()
    for chunk in range(slots * tiles):
        q_copy(chunk).start()
        g_copy(chunk).start()

    term_ref[...] = jnp.zeros_like(term_ref)
    causal_bias[...] = jnp.where(
        lax.broadcasted_iota(jnp.int32, (TILE, TILE), 0)
        <= lax.broadcasted_iota(jnp.int32, (TILE, TILE), 1),
        0.0,
        MASKED,
    )
    for copy in scalar_copies + kv_copies + resp_copies:
        copy.wait()

    @pl.loop(0, n)
    def _(j):
        place[holder_ref[j]] = j

    wide = 2 * TILE
    at_once = 4
    groups = heads // at_once
    units = [(s, index, g) for s in range(slots) for index in range(tiles) for g in range(groups)]

    def columns_of(u):
        return prompt_len + (units[u][1] + 1) * TILE

    def rows_of(u):
        s, index, _ = units[u]
        first = (s * tiles + index) * TILE
        return slice(first, first + TILE)

    def first_head(u, side):
        return units[u][2] * at_once + 2 * side

    def chunks(u):
        return range(0, columns_of(u), TILE)

    def lanes_of(side):
        return slice(side * wide, (side + 1) * wide)

    def stacked(ref, u, side):
        first = first_head(u, side)
        return jnp.concatenate(
            [ref[rows_of(u), (first + h) * width : (first + h + 1) * width] for h in range(2)], axis=0
        )

    def fold(x, how):
        return how(how(x.reshape(x.shape[0] // 8, 8, x.shape[1]), axis=0), axis=0, keepdims=True)

    def prepare(s):
        first_block = prompt_ref[s] * OWNERS
        for o in range(OWNERS):
            start = block_position(place[first_block + o], me, n) * prow
            source = pl.ds(pl.multiple_of(start, prow), prow)
            keys[s, o * prow : (o + 1) * prow, :] = kv[source, 0:width]
            values[s, o * prow : (o + 1) * prow, :] = kv[source, width : 2 * width]
        own = slice(s * slot_rows, (s + 1) * slot_rows)
        keys[s, prompt_len:, :] = rk_all[own, :]
        values[s, prompt_len:, :] = rv_all[own, :]
        yield
        keys_t[s] = keys[s].astype(jnp.float32).T.astype(jnp.bfloat16)
        yield
        column = lax.broadcasted_iota(jnp.int32, (slot_rows, TILE), 0)
        live_bias[s] = jnp.where(column >= begin_ref[s], 0.0, MASKED)
        kt[s] = jnp.zeros_like(kt[s])
        vt[s] = jnp.zeros_like(vt[s])
        yield

    def finish(s):
        own = slice(s * slot_rows, (s + 1) * slot_rows)
        prompt_kt = kt[s, :, 0:prompt_len].T * score_scale
        prompt_vt = vt[s, :, 0:prompt_len].T
        yield
        drk_all[own, :] = kt[s, :, prompt_len:].T * score_scale
        drv_all[own, :] = vt[s, :, prompt_len:].T
        yield
        first_block = prompt_ref[s] * OWNERS
        for o in range(OWNERS):
            start = block_position(place[first_block + o], me, n) * prow
            target = pl.ds(pl.multiple_of(start, prow), prow)
            block = slice(o * prow, (o + 1) * prow)
            term_ref[target, 0:width] += prompt_kt[block]
            term_ref[target, width : 2 * width] += prompt_vt[block]
        yield

    def head(u, side, out):
        s, index, _ = units[u]
        columns, buf = columns_of(u), u % 2
        q2t, g2t = turned.at[u % 3, 0, :, lanes_of(side)], turned.at[u % 3, 1, :, lanes_of(side)]
        q2t[...] = stacked(q_all, u, side).T
        g2t[...] = stacked(g_all, u, side).T
        tops, totals, weights = [], [], []
        for c in chunks(u):
            part = slice(c, c + TILE)
            block = jnp.dot(keys[s, part, :], q2t[...], preferred_element_type=jnp.float32)
            if c >= prompt_len:
                bias = live_bias[s, c - prompt_len : c - prompt_len + TILE, :]
                if c + TILE == columns:
                    bias = bias + causal_bias[...]
                block = block + jnp.concatenate([bias, bias], axis=1)
            top = fold(block, jnp.max) * EXP2_SCALE
            e = jnp.exp2(block * EXP2_SCALE - top)
            exps[buf, side, part, :] = e
            yield
            d = jnp.dot(values[s, part, :], g2t[...], preferred_element_type=jnp.float32)
            dprobs[buf, side, part, :] = d
            tops.append(top)
            totals.append(fold(e, jnp.sum))
            weights.append(fold(e * d, jnp.sum))
            yield
        top = functools.reduce(jnp.maximum, tops)
        factors = [jnp.exp2(part - top) for part in tops]
        total = functools.reduce(jnp.add, [f * x for f, x in zip(factors, totals)])
        weighted = functools.reduce(jnp.add, [f * x for f, x in zip(factors, weights)])
        row = index * TILE + lax.broadcasted_iota(jnp.int32, (1, TILE), 1)
        live = (row >= begin_ref[s]) & (row < begin_ref[s] + length_ref[s])
        inverse = jnp.where(jnp.concatenate([live, live], axis=1), 1.0 / total, 0.0)
        out["delta"] = weighted * inverse
        out["factors"] = [f * inverse for f in factors]

    def tail(u, side, stats):
        buf, lanes = u % 2, lanes_of(side)
        delta = stats["delta"]
        for c, factor in zip(chunks(u), stats["factors"]):
            for first in range(c, c + TILE, PIECE):
                part = slice(first, first + PIECE)
                p = exps[buf, side, part, :] * factor
                prob16[buf, part, lanes] = p.astype(jnp.bfloat16)
                ds = p * (dprobs[buf, side, part, :] - delta)
                dscore16[buf, part, lanes] = ds.astype(jnp.bfloat16)
                yield

    def flush_keys(u):
        s = units[u][0]
        for c in chunks(u):
            part = slice(c, c + TILE)
            kt[s, :, part] += lax.dot_general(
                turned[u % 3, 0], dscore16[u % 2, part, :], ACROSS, preferred_element_type=jnp.float32
            )
            yield

    def flush_values(u):
        s = units[u][0]
        for c in chunks(u):
            part = slice(c, c + TILE)
            vt[s, :, part] += lax.dot_general(
                turned[u % 3, 1], prob16[u % 2, part, :], ACROSS, preferred_element_type=jnp.float32
            )
            yield

    def flush_queries(u, side):
        s, columns = units[u][0], columns_of(u)
        for h in range(2):
            lanes = slice((2 * side + h) * TILE, (2 * side + h + 1) * TILE)
            dqt = jnp.dot(
                keys_t[s, :, 0:columns], dscore16[u % 2, 0:columns, lanes], preferred_element_type=jnp.float32
            )
            first = (first_head(u, side) + h) * width
            dq_all[rows_of(u), first : first + width] = dqt.T * score_scale
            yield

    def together(*steps):
        steps = [[generator, count, 0] for generator, count in steps]
        while steps:
            step = min(steps, key=lambda step: (step[2] + 0.5) / step[1])
            step[2] += 1
            if next(step[0], steps) is steps:
                steps.remove(step)

    def wait_rows(u):
        s, index, g = units[u]
        if g == 0:
            q_copy(s * tiles + index).wait()
            g_copy(s * tiles + index).wait()

    count = len(units)
    per_slot = tiles * groups
    stats = [({}, {}) for _ in units]

    def head_step(u, side):
        return (head(u, side, stats[u][side]), 2 * len(chunks(u)))

    def tail_step(u, side):
        return (tail(u, side, stats[u][side]), columns_of(u) // PIECE)

    def keys_step(u):
        return (flush_keys(u), len(chunks(u)))

    def values_step(u):
        return (flush_values(u), len(chunks(u)))

    def queries_step(u, side):
        return (flush_queries(u, side), 2)

    together((prepare(0), 3))
    wait_rows(0)
    together(head_step(0, 0))
    for u in range(count):
        s = units[u][0]
        steps = [head_step(u, 1), tail_step(u, 0)]
        if u >= 1:
            steps += [keys_step(u - 1), queries_step(u - 1, 0)]
        if u % per_slot == 2 and s + 1 < slots:
            steps.append((prepare(s + 1), 3))
        if u % per_slot == 1 and s >= 1:
            steps.append((finish(s - 1), 3))
        together(*steps)
        if u % per_slot == 1 and s >= 1:
            drk_copy(s - 1).start()
            drv_copy(s - 1).start()
        steps = []
        if u + 1 < count:
            wait_rows(u + 1)
            steps.append(head_step(u + 1, 0))
        steps.append(tail_step(u, 1))
        if u >= 1:
            steps += [values_step(u - 1), queries_step(u - 1, 1)]
        together(*steps)
        if u >= 1 and units[u - 1][2] == groups - 1:
            dq_copy(units[u - 1][0] * tiles + units[u - 1][1]).start()
    last = count - 1
    together(keys_step(last), values_step(last), queries_step(last, 0), queries_step(last, 1))
    dq_copy(slots * tiles - 1).start()
    together((finish(slots - 1), 3))
    drk_copy(slots - 1).start()
    drv_copy(slots - 1).start()

    for copy in term_copies:
        copy.start()
    for copy in term_copies:
        copy.wait()
    for chunk in range(slots * tiles):
        dq_copy(chunk).wait()
    for s in range(slots):
        drk_copy(s).wait()
        drv_copy(s).wait()


def slot_grads(queries, resp_keys, resp_values, out_grad, own_kv, other_kv, prompts, lengths, begins, holders):
    slots = prompts.shape[0]
    rows, columns = queries.shape
    slot_rows, width = rows // slots, resp_keys.shape[1]
    n = holders.shape[0]
    prow = 2 * own_kv.shape[0] // n
    total = prow * OWNERS + slot_rows
    tiles = slot_rows // TILE
    hbm = pl.BlockSpec(memory_space=pltpu.HBM)
    f32, bf16 = jnp.float32, jnp.bfloat16
    return pl.pallas_call(
        grad_kernel,
        in_specs=[hbm] * 10,
        out_specs=[hbm] * 5,
        out_shape=[
            jax.ShapeDtypeStruct((rows, columns), f32),
            jax.ShapeDtypeStruct((rows, width), f32),
            jax.ShapeDtypeStruct((rows, width), f32),
            jax.ShapeDtypeStruct((n * prow // 2, 2 * width), f32),
            jax.ShapeDtypeStruct((n * prow // 2, 2 * width), f32),
        ],
        scratch_shapes=[
            pltpu.SMEM((slots,), jnp.int32),
            pltpu.SMEM((slots,), jnp.int32),
            pltpu.SMEM((slots,), jnp.int32),
            pltpu.SMEM((n,), jnp.int32),
            pltpu.SMEM((n,), jnp.int32),
            pltpu.VMEM((rows, columns), bf16),
            pltpu.VMEM((rows, columns), bf16),
            pltpu.VMEM((rows, width), bf16),
            pltpu.VMEM((rows, width), bf16),
            pltpu.VMEM((rows, columns), f32),
            pltpu.VMEM((rows, width), f32),
            pltpu.VMEM((rows, width), f32),
            pltpu.VMEM((n * prow, 2 * width), bf16),
            pltpu.VMEM((n * prow, 2 * width), f32),
            pltpu.VMEM((slots, total, width), bf16),
            pltpu.VMEM((slots, total, width), bf16),
            pltpu.VMEM((slots, width, total), bf16),
            pltpu.VMEM((slots, slot_rows, TILE), f32),
            pltpu.VMEM((TILE, TILE), f32),
            pltpu.VMEM((3, 2, width, 4 * TILE), bf16),
            pltpu.VMEM((2, 2, total, 2 * TILE), f32),
            pltpu.VMEM((2, 2, total, 2 * TILE), f32),
            pltpu.VMEM((2, total, 4 * TILE), bf16),
            pltpu.VMEM((2, total, 4 * TILE), bf16),
            pltpu.VMEM((slots, width, total), f32),
            pltpu.VMEM((slots, width, total), f32),
            pltpu.SemaphoreType.DMA((4,)),
            pltpu.SemaphoreType.DMA((2,)),
            pltpu.SemaphoreType.DMA((slots * tiles,)),
            pltpu.SemaphoreType.DMA((slots * tiles,)),
            pltpu.SemaphoreType.DMA((slots * tiles,)),
            pltpu.SemaphoreType.DMA((slots,)),
            pltpu.SemaphoreType.DMA((slots,)),
            pltpu.SemaphoreType.DMA((2,)),
            pltpu.SemaphoreType.DMA((2,)),
        ],
        compiler_params=pltpu.CompilerParams(vmem_limit_bytes=60 * 1024 * 1024),
    )(prompts, lengths, begins, holders, queries, out_grad, resp_keys, resp_values, own_kv, other_kv)


def body(
    n,
    queries,
    resp_keys,
    resp_values,
    out_grad,
    prompt_keys,
    prompt_values,
    slot_prompt,
    slot_length,
    slot_begin,
    block_prompt,
):
    width = resp_keys.shape[1]
    prow = prompt_keys.shape[0]
    own = jnp.pad(prompt_keys, ((0, 0), (0, width))) + jnp.pad(prompt_values, ((0, 0), (width, 0)))
    own = jnp.broadcast_to(own[None], (n // 2, prow, 2 * width)).reshape(-1, 2 * width)
    own_kv = exchange(own, n)
    other_kv = swap_cores(own_kv, n)
    query_grad, key_grad, value_grad, own_term, other_term = slot_grads(
        queries, resp_keys, resp_values, out_grad, own_kv, other_kv,
        slot_prompt, slot_length, slot_begin, block_prompt,
    )
    parts = exchange(own_term + swap_cores(other_term, n), n)
    owned = jnp.sum(parts.reshape(n // 2, prow, 2 * width), axis=0)
    return query_grad, key_grad, value_grad, owned[:, :width], owned[:, width:]


def solution(mesh):
    n = mesh.shape["seq"]
    rows = P(("groups", "seq"), None)
    slots = P(("groups", "seq"))
    return jax.shard_map(
        functools.partial(body, n),
        mesh=mesh,
        in_specs=(rows,) * 6 + (slots,) * 3 + (P("groups"),),
        out_specs=(rows,) * 5,
        check_vma=False,
    )
```

```python
import functools
import math

import jax
import jax.numpy as jnp
from jax import lax
from jax.experimental import pallas as pl
from jax.experimental.pallas import tpu as pltpu
from jax.sharding import PartitionSpec as P

OWNERS = 8
TILE = 128
PIECE = 16
score_scale = 0.08838834764831845
EXP2_SCALE = score_scale * math.log2(math.e)
MASKED = -1e30

ACROSS = (((1,), (1,)), ((), ()))


def same_core_groups(n):
    return [list(range(core, n, 2)) for core in range(2)]


def swap_cores(x, n):
    return lax.ppermute(x, "seq", [(i, i ^ 1) for i in range(n)])


def exchange(x, n):
    return lax.all_to_all(
        x, "seq", split_axis=0, concat_axis=0, axis_index_groups=same_core_groups(n), tiled=True
    )


def block_position(holder, me, n):
    return ((holder ^ me) & 1) * (n // 2) + (holder >> 1)


def grad_kernel(
    prompt_hbm,
    length_hbm,
    begin_hbm,
    holder_hbm,
    q_hbm,
    g_hbm,
    rk_hbm,
    rv_hbm,
    own_hbm,
    other_hbm,
    dq_hbm,
    drk_hbm,
    drv_hbm,
    own_term_hbm,
    other_term_hbm,
    prompt_ref,
    length_ref,
    begin_ref,
    holder_ref,
    place,
    q_all,
    g_all,
    rk_all,
    rv_all,
    dq_all,
    drk_all,
    drv_all,
    kv,
    term_ref,
    keys,
    values,
    keys_t,
    live_bias,
    causal_bias,
    turned,
    exps,
    dprobs,
    prob16,
    dscore16,
    kt,
    vt,
    sem_scalar,
    sem_resp,
    sem_q,
    sem_g,
    sem_dq,
    sem_drk,
    sem_drv,
    sem_kv,
    sem_term,
):
    n = holder_ref.shape[0]
    slots = prompt_ref.shape[0]
    rows, width = rk_all.shape
    slot_rows = rows // slots
    tiles = slot_rows // TILE
    prow = term_ref.shape[0] // n
    prompt_len = prow * OWNERS
    heads = q_all.shape[1] // width
    me = lax.axis_index("seq")

    scalar_copies = [
        pltpu.make_async_copy(src, dst, sem_scalar.at[i])
        for i, (src, dst) in enumerate(
            [
                (prompt_hbm, prompt_ref),
                (length_hbm, length_ref),
                (begin_hbm, begin_ref),
                (holder_hbm, holder_ref),
            ]
        )
    ]
    resp_copies = [
        pltpu.make_async_copy(rk_hbm, rk_all, sem_resp.at[0]),
        pltpu.make_async_copy(rv_hbm, rv_all, sem_resp.at[1]),
    ]

    def tile_rows(chunk):
        return pl.ds(pl.multiple_of(chunk * TILE, TILE), TILE)

    def q_copy(chunk):
        part = tile_rows(chunk)
        return pltpu.make_async_copy(q_hbm.at[part], q_all.at[part], sem_q.at[chunk])

    def g_copy(chunk):
        part = tile_rows(chunk)
        return pltpu.make_async_copy(g_hbm.at[part], g_all.at[part], sem_g.at[chunk])

    def dq_copy(chunk):
        part = tile_rows(chunk)
        return pltpu.make_async_copy(dq_all.at[part], dq_hbm.at[part], sem_dq.at[chunk])

    def slot_part(s):
        return pl.ds(pl.multiple_of(s * slot_rows, slot_rows), slot_rows)

    def drk_copy(s):
        return pltpu.make_async_copy(
            drk_all.at[slot_part(s)], drk_hbm.at[slot_part(s)], sem_drk.at[s]
        )

    def drv_copy(s):
        return pltpu.make_async_copy(
            drv_all.at[slot_part(s)], drv_hbm.at[slot_part(s)], sem_drv.at[s]
        )

    half_rows = term_ref.shape[0] // 2
    kv_copies = [
        pltpu.make_async_copy(src, kv.at[pl.ds(i * half_rows, half_rows)], sem_kv.at[i])
        for i, src in enumerate([own_hbm, other_hbm])
    ]
    term_copies = [
        pltpu.make_async_copy(term_ref.at[pl.ds(i * half_rows, half_rows)], dst, sem_term.at[i])
        for i, dst in enumerate([own_term_hbm, other_term_hbm])
    ]
    for copy in scalar_copies + kv_copies + resp_copies:
        copy.start()
    for chunk in range(slots * tiles):
        q_copy(chunk).start()
        g_copy(chunk).start()

    term_ref[...] = jnp.zeros_like(term_ref)
    causal_bias[...] = jnp.where(
        lax.broadcasted_iota(jnp.int32, (TILE, TILE), 0)
        <= lax.broadcasted_iota(jnp.int32, (TILE, TILE), 1),
        0.0,
        MASKED,
    )
    for copy in scalar_copies + kv_copies + resp_copies:
        copy.wait()

    @pl.loop(0, n)
    def _(j):
        place[holder_ref[j]] = j

    wide = 2 * TILE
    at_once = 4
    groups = heads // at_once
    units = [(s, index, g) for s in range(slots) for index in range(tiles) for g in range(groups)]

    def columns_of(u):
        return prompt_len + (units[u][1] + 1) * TILE

    def rows_of(u):
        s, index, _ = units[u]
        first = (s * tiles + index) * TILE
        return slice(first, first + TILE)

    def first_head(u, side):
        return units[u][2] * at_once + 2 * side

    def chunks(u):
        return range(0, columns_of(u), TILE)

    def lanes_of(side):
        return slice(side * wide, (side + 1) * wide)

    def stacked(ref, u, side):
        first = first_head(u, side)
        return jnp.concatenate(
            [ref[rows_of(u), (first + h) * width : (first + h + 1) * width] for h in range(2)], axis=0
        )

    def fold(x, how):
        return how(how(x.reshape(x.shape[0] // 8, 8, x.shape[1]), axis=0), axis=0, keepdims=True)

    def prepare(s):
        first_block = prompt_ref[s] * OWNERS
        for o in range(OWNERS):
            start = block_position(place[first_block + o], me, n) * prow
            source = pl.ds(pl.multiple_of(start, prow), prow)
            keys[s, o * prow : (o + 1) * prow, :] = kv[source, 0:width]
            values[s, o * prow : (o + 1) * prow, :] = kv[source, width : 2 * width]
        own = slice(s * slot_rows, (s + 1) * slot_rows)
        keys[s, prompt_len:, :] = rk_all[own, :]
        values[s, prompt_len:, :] = rv_all[own, :]
        yield
        keys_t[s] = keys[s].astype(jnp.float32).T.astype(jnp.bfloat16)
        yield
        column = lax.broadcasted_iota(jnp.int32, (slot_rows, TILE), 0)
        live_bias[s] = jnp.where(column >= begin_ref[s], 0.0, MASKED)
        kt[s] = jnp.zeros_like(kt[s])
        vt[s] = jnp.zeros_like(vt[s])
        yield

    def finish(s):
        own = slice(s * slot_rows, (s + 1) * slot_rows)
        prompt_kt = kt[s, :, 0:prompt_len].T * score_scale
        prompt_vt = vt[s, :, 0:prompt_len].T
        yield
        drk_all[own, :] = kt[s, :, prompt_len:].T * score_scale
        drv_all[own, :] = vt[s, :, prompt_len:].T
        yield
        first_block = prompt_ref[s] * OWNERS
        for o in range(OWNERS):
            start = block_position(place[first_block + o], me, n) * prow
            target = pl.ds(pl.multiple_of(start, prow), prow)
            block = slice(o * prow, (o + 1) * prow)
            term_ref[target, 0:width] += prompt_kt[block]
            term_ref[target, width : 2 * width] += prompt_vt[block]
        yield

    def turn(u):
        for side in range(2):
            turned[u % 4, 0, :, lanes_of(side)] = stacked(q_all, u, side).T
            yield
            turned[u % 4, 1, :, lanes_of(side)] = stacked(g_all, u, side).T
            yield

    def head(u, side, out):
        s, index, _ = units[u]
        columns, buf = columns_of(u), u % 2
        q2t, g2t = turned.at[u % 4, 0, :, lanes_of(side)], turned.at[u % 4, 1, :, lanes_of(side)]
        tops, totals, weights = [], [], []
        for c in chunks(u):
            part = slice(c, c + TILE)
            block = jnp.dot(keys[s, part, :], q2t[...], preferred_element_type=jnp.float32)
            if c >= prompt_len:
                bias = live_bias[s, c - prompt_len : c - prompt_len + TILE, :]
                if c + TILE == columns:
                    bias = bias + causal_bias[...]
                block = block + jnp.concatenate([bias, bias], axis=1)
            top = fold(block, jnp.max) * EXP2_SCALE
            e = jnp.exp2(block * EXP2_SCALE - top)
            exps[buf, side, part, :] = e
            yield
            d = jnp.dot(values[s, part, :], g2t[...], preferred_element_type=jnp.float32)
            dprobs[buf, side, part, :] = d
            tops.append(top)
            totals.append(fold(e, jnp.sum))
            weights.append(fold(e * d, jnp.sum))
            yield
        top = functools.reduce(jnp.maximum, tops)
        factors = [jnp.exp2(part - top) for part in tops]
        total = functools.reduce(jnp.add, [f * x for f, x in zip(factors, totals)])
        weighted = functools.reduce(jnp.add, [f * x for f, x in zip(factors, weights)])
        row = index * TILE + lax.broadcasted_iota(jnp.int32, (1, TILE), 1)
        live = (row >= begin_ref[s]) & (row < begin_ref[s] + length_ref[s])
        inverse = jnp.where(jnp.concatenate([live, live], axis=1), 1.0 / total, 0.0)
        out["delta"] = weighted * inverse
        out["factors"] = [f * inverse for f in factors]

    def tail(u, side, stats):
        buf, lanes = u % 2, lanes_of(side)
        delta = stats["delta"]
        for c, factor in zip(chunks(u), stats["factors"]):
            for first in range(c, c + TILE, PIECE):
                part = slice(first, first + PIECE)
                p = exps[buf, side, part, :] * factor
                prob16[buf, part, lanes] = p.astype(jnp.bfloat16)
                ds = p * (dprobs[buf, side, part, :] - delta)
                dscore16[buf, part, lanes] = ds.astype(jnp.bfloat16)
                yield

    def flush_keys(u):
        s = units[u][0]
        for c in chunks(u):
            part = slice(c, c + TILE)
            kt[s, :, part] += lax.dot_general(
                turned[u % 4, 0], dscore16[u % 2, part, :], ACROSS, preferred_element_type=jnp.float32
            )
            yield

    def flush_values(u):
        s = units[u][0]
        for c in chunks(u):
            part = slice(c, c + TILE)
            vt[s, :, part] += lax.dot_general(
                turned[u % 4, 1], prob16[u % 2, part, :], ACROSS, preferred_element_type=jnp.float32
            )
            yield

    def flush_queries(u, side):
        s, columns = units[u][0], columns_of(u)
        for h in range(2):
            lanes = slice((2 * side + h) * TILE, (2 * side + h + 1) * TILE)
            dqt = jnp.dot(
                keys_t[s, :, 0:columns], dscore16[u % 2, 0:columns, lanes], preferred_element_type=jnp.float32
            )
            first = (first_head(u, side) + h) * width
            dq_all[rows_of(u), first : first + width] = dqt.T * score_scale
            yield

    def together(*steps):
        steps = [[generator, count, 0] for generator, count in steps]
        while steps:
            step = min(steps, key=lambda step: (step[2] + 0.5) / step[1])
            step[2] += 1
            if next(step[0], steps) is steps:
                steps.remove(step)

    def wait_rows(u):
        s, index, g = units[u]
        if g == 0:
            q_copy(s * tiles + index).wait()
            g_copy(s * tiles + index).wait()

    count = len(units)
    per_slot = tiles * groups
    stats = [({}, {}) for _ in units]

    def head_step(u, side):
        return (head(u, side, stats[u][side]), 2 * len(chunks(u)))

    def tail_step(u, side):
        return (tail(u, side, stats[u][side]), columns_of(u) // PIECE)

    def keys_step(u):
        return (flush_keys(u), len(chunks(u)))

    def values_step(u):
        return (flush_values(u), len(chunks(u)))

    def queries_step(u, side):
        return (flush_queries(u, side), 2)

    wait_rows(0)
    together((prepare(0), 3), (turn(0), 4))
    for u in range(-1, count + 1):
        steps = []
        if u + 1 < count:
            steps += [head_step(u + 1, side) for side in range(2)]
        if 0 <= u < count:
            steps += [tail_step(u, side) for side in range(2)]
            if u % per_slot == 1 and units[u][0] + 1 < slots:
                steps.append((prepare(units[u][0] + 1), 3))
        if u + 2 < count:
            wait_rows(u + 2)
            steps.append((turn(u + 2), 4))
        if u >= 1:
            steps += [keys_step(u - 1), values_step(u - 1)]
            steps += [queries_step(u - 1, side) for side in range(2)]
        ended = u >= 2 and (u - 1) % per_slot == 0
        if ended:
            steps.append((finish(units[u - 2][0]), 3))
        together(*steps)
        if u >= 1 and units[u - 1][2] == groups - 1:
            dq_copy(units[u - 1][0] * tiles + units[u - 1][1]).start()
        if ended:
            drk_copy(units[u - 2][0]).start()
            drv_copy(units[u - 2][0]).start()
    together((finish(slots - 1), 3))
    drk_copy(slots - 1).start()
    drv_copy(slots - 1).start()

    for copy in term_copies:
        copy.start()
    for copy in term_copies:
        copy.wait()
    for chunk in range(slots * tiles):
        dq_copy(chunk).wait()
    for s in range(slots):
        drk_copy(s).wait()
        drv_copy(s).wait()


def slot_grads(queries, resp_keys, resp_values, out_grad, own_kv, other_kv, prompts, lengths, begins, holders):
    slots = prompts.shape[0]
    rows, columns = queries.shape
    slot_rows, width = rows // slots, resp_keys.shape[1]
    n = holders.shape[0]
    prow = 2 * own_kv.shape[0] // n
    total = prow * OWNERS + slot_rows
    tiles = slot_rows // TILE
    hbm = pl.BlockSpec(memory_space=pltpu.HBM)
    f32, bf16 = jnp.float32, jnp.bfloat16
    return pl.pallas_call(
        grad_kernel,
        in_specs=[hbm] * 10,
        out_specs=[hbm] * 5,
        out_shape=[
            jax.ShapeDtypeStruct((rows, columns), f32),
            jax.ShapeDtypeStruct((rows, width), f32),
            jax.ShapeDtypeStruct((rows, width), f32),
            jax.ShapeDtypeStruct((n * prow // 2, 2 * width), f32),
            jax.ShapeDtypeStruct((n * prow // 2, 2 * width), f32),
        ],
        scratch_shapes=[
            pltpu.SMEM((slots,), jnp.int32),
            pltpu.SMEM((slots,), jnp.int32),
            pltpu.SMEM((slots,), jnp.int32),
            pltpu.SMEM((n,), jnp.int32),
            pltpu.SMEM((n,), jnp.int32),
            pltpu.VMEM((rows, columns), bf16),
            pltpu.VMEM((rows, columns), bf16),
            pltpu.VMEM((rows, width), bf16),
            pltpu.VMEM((rows, width), bf16),
            pltpu.VMEM((rows, columns), f32),
            pltpu.VMEM((rows, width), f32),
            pltpu.VMEM((rows, width), f32),
            pltpu.VMEM((n * prow, 2 * width), bf16),
            pltpu.VMEM((n * prow, 2 * width), f32),
            pltpu.VMEM((slots, total, width), bf16),
            pltpu.VMEM((slots, total, width), bf16),
            pltpu.VMEM((slots, width, total), bf16),
            pltpu.VMEM((slots, slot_rows, TILE), f32),
            pltpu.VMEM((TILE, TILE), f32),
            pltpu.VMEM((4, 2, width, 4 * TILE), bf16),
            pltpu.VMEM((2, 2, total, 2 * TILE), f32),
            pltpu.VMEM((2, 2, total, 2 * TILE), f32),
            pltpu.VMEM((2, total, 4 * TILE), bf16),
            pltpu.VMEM((2, total, 4 * TILE), bf16),
            pltpu.VMEM((slots, width, total), f32),
            pltpu.VMEM((slots, width, total), f32),
            pltpu.SemaphoreType.DMA((4,)),
            pltpu.SemaphoreType.DMA((2,)),
            pltpu.SemaphoreType.DMA((slots * tiles,)),
            pltpu.SemaphoreType.DMA((slots * tiles,)),
            pltpu.SemaphoreType.DMA((slots * tiles,)),
            pltpu.SemaphoreType.DMA((slots,)),
            pltpu.SemaphoreType.DMA((slots,)),
            pltpu.SemaphoreType.DMA((2,)),
            pltpu.SemaphoreType.DMA((2,)),
        ],
        compiler_params=pltpu.CompilerParams(vmem_limit_bytes=60 * 1024 * 1024),
    )(prompts, lengths, begins, holders, queries, out_grad, resp_keys, resp_values, own_kv, other_kv)


def body(
    n,
    queries,
    resp_keys,
    resp_values,
    out_grad,
    prompt_keys,
    prompt_values,
    slot_prompt,
    slot_length,
    slot_begin,
    block_prompt,
):
    width = resp_keys.shape[1]
    prow = prompt_keys.shape[0]
    own = jnp.pad(prompt_keys, ((0, 0), (0, width))) + jnp.pad(prompt_values, ((0, 0), (width, 0)))
    own = jnp.broadcast_to(own[None], (n // 2, prow, 2 * width)).reshape(-1, 2 * width)
    own_kv = exchange(own, n)
    other_kv = swap_cores(own_kv, n)
    query_grad, key_grad, value_grad, own_term, other_term = slot_grads(
        queries, resp_keys, resp_values, out_grad, own_kv, other_kv,
        slot_prompt, slot_length, slot_begin, block_prompt,
    )
    parts = exchange(own_term + swap_cores(other_term, n), n)
    owned = jnp.sum(parts.reshape(n // 2, prow, 2 * width), axis=0)
    return query_grad, key_grad, value_grad, owned[:, :width], owned[:, width:]


def solution(mesh):
    n = mesh.shape["seq"]
    rows = P(("groups", "seq"), None)
    slots = P(("groups", "seq"))
    return jax.shard_map(
        functools.partial(body, n),
        mesh=mesh,
        in_specs=(rows,) * 6 + (slots,) * 3 + (P("groups"),),
        out_specs=(rows,) * 5,
        check_vma=False,
    )
```

```python
import functools
import math

import jax
import jax.numpy as jnp
from jax import lax
from jax.experimental import pallas as pl
from jax.experimental.pallas import tpu as pltpu
from jax.sharding import PartitionSpec as P

OWNERS = 8
TILE = 128
PIECE = 16
EXTRA = 8
BITS = 14
score_scale = 0.08838834764831845
EXP2_SCALE = score_scale * math.log2(math.e)
MASKED = -1e30

ACROSS = (((1,), (1,)), ((), ()))


def same_core_groups(n):
    return [list(range(core, n, 2)) for core in range(2)]


def swap_cores(x, n):
    return lax.ppermute(x, "seq", [(i, i ^ 1) for i in range(n)])


def exchange(x, n):
    return lax.all_to_all(
        x, "seq", split_axis=0, concat_axis=0, axis_index_groups=same_core_groups(n), tiled=True
    )


def block_position(holder, me, n):
    return ((holder ^ me) & 1) * (n // 2) + (holder >> 1)


def encode_kernel(prow, own_ref, other_ref, out_ref):
    stride = prow + EXTRA
    pieces = []
    for start in range(0, out_ref.shape[0], stride):
        block = own_ref[start : start + stride, :] + other_ref[start : start + stride, :]
        bound = jnp.maximum(block[prow:], 1e-30)
        exponent = jnp.floor(jnp.log2(bound) + 0.001) + 1
        scale = jnp.exp2(BITS - exponent)[0:1]
        pieces += [jnp.floor(block[:prow] * scale + 0.5), exponent]
    out_ref[...] = jnp.concatenate(pieces, axis=0).astype(jnp.int32).astype(jnp.int16)


def decode_kernel(prow, in_ref, key_ref, value_ref):
    stride = prow + EXTRA
    coded = in_ref[...].astype(jnp.int32).astype(jnp.float32)
    total = jnp.zeros((prow, coded.shape[1]), jnp.float32)
    for start in range(0, coded.shape[0], stride):
        scale = jnp.exp2(coded[start + prow : start + stride] - BITS)[0:1]
        total = total + coded[start : start + prow] * scale
    width = key_ref.shape[1]
    key_ref[...] = total[:, :width]
    value_ref[...] = total[:, width:]


def owned_sum(own_term, other_term, n, prow, width):
    coded = pl.pallas_call(
        functools.partial(encode_kernel, prow),
        out_shape=jax.ShapeDtypeStruct(own_term.shape, jnp.int16),
    )(own_term, swap_cores(other_term, n))
    part = jax.ShapeDtypeStruct((prow, width), jnp.float32)
    return pl.pallas_call(functools.partial(decode_kernel, prow), out_shape=[part, part])(
        exchange(coded, n)
    )


def grad_kernel(
    prompt_hbm,
    length_hbm,
    begin_hbm,
    holder_hbm,
    q_hbm,
    g_hbm,
    rk_hbm,
    rv_hbm,
    own_hbm,
    other_hbm,
    dq_hbm,
    drk_hbm,
    drv_hbm,
    own_term_hbm,
    other_term_hbm,
    prompt_ref,
    length_ref,
    begin_ref,
    holder_ref,
    place,
    q_all,
    g_all,
    rk_all,
    rv_all,
    dq_all,
    drk_all,
    drv_all,
    kv,
    term_ref,
    keys,
    values,
    keys_t,
    live_bias,
    causal_bias,
    turned,
    exps,
    dprobs,
    prob16,
    dscore16,
    kt,
    vt,
    sem_scalar,
    sem_resp,
    sem_q,
    sem_g,
    sem_dq,
    sem_drk,
    sem_drv,
    sem_kv,
    sem_term,
):
    n = holder_ref.shape[0]
    slots = prompt_ref.shape[0]
    rows, width = rk_all.shape
    slot_rows = rows // slots
    tiles = slot_rows // TILE
    prow = kv.shape[0] // n
    stride = prow + EXTRA
    prompt_len = prow * OWNERS
    heads = q_all.shape[1] // width
    me = lax.axis_index("seq")

    scalar_copies = [
        pltpu.make_async_copy(src, dst, sem_scalar.at[i])
        for i, (src, dst) in enumerate(
            [
                (prompt_hbm, prompt_ref),
                (length_hbm, length_ref),
                (begin_hbm, begin_ref),
                (holder_hbm, holder_ref),
            ]
        )
    ]
    resp_copies = [
        pltpu.make_async_copy(rk_hbm, rk_all, sem_resp.at[0]),
        pltpu.make_async_copy(rv_hbm, rv_all, sem_resp.at[1]),
    ]

    def tile_rows(chunk):
        return pl.ds(pl.multiple_of(chunk * TILE, TILE), TILE)

    def q_copy(chunk):
        part = tile_rows(chunk)
        return pltpu.make_async_copy(q_hbm.at[part], q_all.at[part], sem_q.at[chunk])

    def g_copy(chunk):
        part = tile_rows(chunk)
        return pltpu.make_async_copy(g_hbm.at[part], g_all.at[part], sem_g.at[chunk])

    def dq_copy(chunk):
        part = tile_rows(chunk)
        return pltpu.make_async_copy(dq_all.at[part], dq_hbm.at[part], sem_dq.at[chunk])

    def slot_part(s):
        return pl.ds(pl.multiple_of(s * slot_rows, slot_rows), slot_rows)

    def drk_copy(s):
        return pltpu.make_async_copy(
            drk_all.at[slot_part(s)], drk_hbm.at[slot_part(s)], sem_drk.at[s]
        )

    def drv_copy(s):
        return pltpu.make_async_copy(
            drv_all.at[slot_part(s)], drv_hbm.at[slot_part(s)], sem_drv.at[s]
        )

    half_kv, half_rows = kv.shape[0] // 2, term_ref.shape[0] // 2
    kv_copies = [
        pltpu.make_async_copy(src, kv.at[pl.ds(i * half_kv, half_kv)], sem_kv.at[i])
        for i, src in enumerate([own_hbm, other_hbm])
    ]
    term_copies = [
        pltpu.make_async_copy(term_ref.at[pl.ds(i * half_rows, half_rows)], dst, sem_term.at[i])
        for i, dst in enumerate([own_term_hbm, other_term_hbm])
    ]
    for copy in scalar_copies + kv_copies + resp_copies:
        copy.start()
    for chunk in range(slots * tiles):
        q_copy(chunk).start()
        g_copy(chunk).start()

    term_ref[...] = jnp.zeros_like(term_ref)
    causal_bias[...] = jnp.where(
        lax.broadcasted_iota(jnp.int32, (TILE, TILE), 0)
        <= lax.broadcasted_iota(jnp.int32, (TILE, TILE), 1),
        0.0,
        MASKED,
    )
    for copy in scalar_copies + kv_copies + resp_copies:
        copy.wait()

    @pl.loop(0, n)
    def _(j):
        place[holder_ref[j]] = j

    wide = 2 * TILE
    at_once = 4
    groups = heads // at_once
    units = [(s, index, g) for s in range(slots) for index in range(tiles) for g in range(groups)]

    def columns_of(u):
        return prompt_len + (units[u][1] + 1) * TILE

    def rows_of(u):
        s, index, _ = units[u]
        first = (s * tiles + index) * TILE
        return slice(first, first + TILE)

    def first_head(u, side):
        return units[u][2] * at_once + 2 * side

    def chunks(u):
        return range(0, columns_of(u), TILE)

    def lanes_of(side):
        return slice(side * wide, (side + 1) * wide)

    def stacked(ref, u, side):
        first = first_head(u, side)
        return jnp.concatenate(
            [ref[rows_of(u), (first + h) * width : (first + h + 1) * width] for h in range(2)], axis=0
        )

    def fold(x, how):
        return how(how(x.reshape(x.shape[0] // 8, 8, x.shape[1]), axis=0), axis=0, keepdims=True)

    def prepare(s):
        first_block = prompt_ref[s] * OWNERS
        for o in range(OWNERS):
            start = block_position(place[first_block + o], me, n) * prow
            source = pl.ds(pl.multiple_of(start, prow), prow)
            keys[s, o * prow : (o + 1) * prow, :] = kv[source, 0:width]
            values[s, o * prow : (o + 1) * prow, :] = kv[source, width : 2 * width]
        own = slice(s * slot_rows, (s + 1) * slot_rows)
        keys[s, prompt_len:, :] = rk_all[own, :]
        values[s, prompt_len:, :] = rv_all[own, :]
        yield
        keys_t[s] = keys[s].astype(jnp.float32).T.astype(jnp.bfloat16)
        yield
        column = lax.broadcasted_iota(jnp.int32, (slot_rows, TILE), 0)
        live_bias[s] = jnp.where(column >= begin_ref[s], 0.0, MASKED)
        kt[s] = jnp.zeros_like(kt[s])
        vt[s] = jnp.zeros_like(vt[s])
        yield

    def finish(s):
        own = slice(s * slot_rows, (s + 1) * slot_rows)
        prompt_kt = kt[s, :, 0:prompt_len].T * score_scale
        prompt_vt = vt[s, :, 0:prompt_len].T
        yield
        drk_all[own, :] = kt[s, :, prompt_len:].T * score_scale
        drv_all[own, :] = vt[s, :, prompt_len:].T
        yield
        first_block = prompt_ref[s] * OWNERS
        for o in range(OWNERS):
            start = block_position(place[first_block + o], me, n) * stride
            target = pl.ds(pl.multiple_of(start, 8), prow)
            block = slice(o * prow, (o + 1) * prow)
            term_ref[target, 0:width] += prompt_kt[block]
            term_ref[target, width : 2 * width] += prompt_vt[block]
        yield

    def head(u, side, out):
        s, index, _ = units[u]
        columns, buf = columns_of(u), u % 2
        q2t, g2t = turned.at[u % 3, 0, :, lanes_of(side)], turned.at[u % 3, 1, :, lanes_of(side)]
        q2t[...] = stacked(q_all, u, side).T
        g2t[...] = stacked(g_all, u, side).T
        tops, totals, weights = [], [], []
        for c in chunks(u):
            part = slice(c, c + TILE)
            block = jnp.dot(keys[s, part, :], q2t[...], preferred_element_type=jnp.float32)
            if c >= prompt_len:
                bias = live_bias[s, c - prompt_len : c - prompt_len + TILE, :]
                if c + TILE == columns:
                    bias = bias + causal_bias[...]
                block = block + jnp.concatenate([bias, bias], axis=1)
            top = fold(block, jnp.max) * EXP2_SCALE
            e = jnp.exp2(block * EXP2_SCALE - top)
            exps[buf, side, part, :] = e
            yield
            d = jnp.dot(values[s, part, :], g2t[...], preferred_element_type=jnp.float32)
            dprobs[buf, side, part, :] = d
            tops.append(top)
            totals.append(fold(e, jnp.sum))
            weights.append(fold(e * d, jnp.sum))
            yield
        top = functools.reduce(jnp.maximum, tops)
        factors = [jnp.exp2(part - top) for part in tops]
        total = functools.reduce(jnp.add, [f * x for f, x in zip(factors, totals)])
        weighted = functools.reduce(jnp.add, [f * x for f, x in zip(factors, weights)])
        row = index * TILE + lax.broadcasted_iota(jnp.int32, (1, TILE), 1)
        live = (row >= begin_ref[s]) & (row < begin_ref[s] + length_ref[s])
        inverse = jnp.where(jnp.concatenate([live, live], axis=1), 1.0 / total, 0.0)
        out["delta"] = weighted * inverse
        out["factors"] = [f * inverse for f in factors]

    def tail(u, side, stats):
        buf, lanes = u % 2, lanes_of(side)
        delta = stats["delta"]
        for c, factor in zip(chunks(u), stats["factors"]):
            for first in range(c, c + TILE, PIECE):
                part = slice(first, first + PIECE)
                p = exps[buf, side, part, :] * factor
                prob16[buf, part, lanes] = p.astype(jnp.bfloat16)
                ds = p * (dprobs[buf, side, part, :] - delta)
                dscore16[buf, part, lanes] = ds.astype(jnp.bfloat16)
            yield

    def flush_keys(u):
        s, columns = units[u][0], columns_of(u)
        kt[s, :, 0:columns] += lax.dot_general(
            turned[u % 3, 0], dscore16[u % 2, 0:columns, :], ACROSS, preferred_element_type=jnp.float32
        )
        yield

    def flush_values(u):
        s, columns = units[u][0], columns_of(u)
        vt[s, :, 0:columns] += lax.dot_general(
            turned[u % 3, 1], prob16[u % 2, 0:columns, :], ACROSS, preferred_element_type=jnp.float32
        )
        yield

    def flush_queries(u):
        s, columns = units[u][0], columns_of(u)
        for side in range(2):
            ds = dscore16[u % 2, 0:columns, lanes_of(side)]
            dqt = jnp.dot(keys_t[s, :, 0:columns], ds, preferred_element_type=jnp.float32)
            for h in range(2):
                first = (first_head(u, side) + h) * width
                dq = dqt[:, h * TILE : (h + 1) * TILE].T * score_scale
                dq_all[rows_of(u), first : first + width] = dq
            yield

    def together(*steps):
        steps = list(steps)
        while steps:
            for step in list(steps):
                if next(step, steps) is steps:
                    steps.remove(step)

    def wait_rows(u):
        s, index, g = units[u]
        if g == 0:
            q_copy(s * tiles + index).wait()
            g_copy(s * tiles + index).wait()

    count = len(units)
    per_slot = tiles * groups
    stats = [({}, {}) for _ in units]
    together(prepare(0))
    wait_rows(0)
    together(head(0, 0, stats[0][0]))
    for u in range(count):
        s = units[u][0]
        steps = [head(u, 1, stats[u][1]), tail(u, 0, stats[u][0])]
        if u >= 1:
            steps += [flush_keys(u - 1), flush_queries(u - 1)]
        if u % per_slot == 2 and s + 1 < slots:
            steps.append(prepare(s + 1))
        if u % per_slot == 1 and s >= 1:
            steps.append(finish(s - 1))
        together(*steps)
        if u >= 1 and units[u - 1][2] == groups - 1:
            dq_copy(units[u - 1][0] * tiles + units[u - 1][1]).start()
        if u % per_slot == 1 and s >= 1:
            drk_copy(s - 1).start()
            drv_copy(s - 1).start()
        steps = []
        if u + 1 < count:
            wait_rows(u + 1)
            steps.append(head(u + 1, 0, stats[u + 1][0]))
        steps.append(tail(u, 1, stats[u][1]))
        if u >= 1:
            steps.append(flush_values(u - 1))
        together(*steps)
    together(flush_keys(count - 1), flush_values(count - 1), flush_queries(count - 1))
    dq_copy(slots * tiles - 1).start()
    together(finish(slots - 1))
    drk_copy(slots - 1).start()
    drv_copy(slots - 1).start()

    for block in range(n):
        largest = jnp.max(jnp.abs(term_ref[block * stride : block * stride + prow, :]), axis=0, keepdims=True)
        term_ref[block * stride + prow : (block + 1) * stride, :] = jnp.broadcast_to(
            largest, (EXTRA, largest.shape[1])
        )
    for copy in term_copies:
        copy.start()
    for copy in term_copies:
        copy.wait()
    for chunk in range(slots * tiles):
        dq_copy(chunk).wait()
    for s in range(slots):
        drk_copy(s).wait()
        drv_copy(s).wait()


def slot_grads(queries, resp_keys, resp_values, out_grad, own_kv, other_kv, prompts, lengths, begins, holders):
    slots = prompts.shape[0]
    rows, columns = queries.shape
    slot_rows, width = rows // slots, resp_keys.shape[1]
    n = holders.shape[0]
    prow = 2 * own_kv.shape[0] // n
    total = prow * OWNERS + slot_rows
    tiles = slot_rows // TILE
    hbm = pl.BlockSpec(memory_space=pltpu.HBM)
    f32, bf16 = jnp.float32, jnp.bfloat16
    return pl.pallas_call(
        grad_kernel,
        in_specs=[hbm] * 10,
        out_specs=[hbm] * 5,
        out_shape=[
            jax.ShapeDtypeStruct((rows, columns), f32),
            jax.ShapeDtypeStruct((rows, width), f32),
            jax.ShapeDtypeStruct((rows, width), f32),
            jax.ShapeDtypeStruct((n * (prow + EXTRA) // 2, 2 * width), f32),
            jax.ShapeDtypeStruct((n * (prow + EXTRA) // 2, 2 * width), f32),
        ],
        scratch_shapes=[
            pltpu.SMEM((slots,), jnp.int32),
            pltpu.SMEM((slots,), jnp.int32),
            pltpu.SMEM((slots,), jnp.int32),
            pltpu.SMEM((n,), jnp.int32),
            pltpu.SMEM((n,), jnp.int32),
            pltpu.VMEM((rows, columns), bf16),
            pltpu.VMEM((rows, columns), bf16),
            pltpu.VMEM((rows, width), bf16),
            pltpu.VMEM((rows, width), bf16),
            pltpu.VMEM((rows, columns), f32),
            pltpu.VMEM((rows, width), f32),
            pltpu.VMEM((rows, width), f32),
            pltpu.VMEM((n * prow, 2 * width), bf16),
            pltpu.VMEM((n * (prow + EXTRA), 2 * width), f32),
            pltpu.VMEM((slots, total, width), bf16),
            pltpu.VMEM((slots, total, width), bf16),
            pltpu.VMEM((slots, width, total), bf16),
            pltpu.VMEM((slots, slot_rows, TILE), f32),
            pltpu.VMEM((TILE, TILE), f32),
            pltpu.VMEM((3, 2, width, 4 * TILE), bf16),
            pltpu.VMEM((2, 2, total, 2 * TILE), f32),
            pltpu.VMEM((2, 2, total, 2 * TILE), f32),
            pltpu.VMEM((2, total, 4 * TILE), bf16),
            pltpu.VMEM((2, total, 4 * TILE), bf16),
            pltpu.VMEM((slots, width, total), f32),
            pltpu.VMEM((slots, width, total), f32),
            pltpu.SemaphoreType.DMA((4,)),
            pltpu.SemaphoreType.DMA((2,)),
            pltpu.SemaphoreType.DMA((slots * tiles,)),
            pltpu.SemaphoreType.DMA((slots * tiles,)),
            pltpu.SemaphoreType.DMA((slots * tiles,)),
            pltpu.SemaphoreType.DMA((slots,)),
            pltpu.SemaphoreType.DMA((slots,)),
            pltpu.SemaphoreType.DMA((2,)),
            pltpu.SemaphoreType.DMA((2,)),
        ],
        compiler_params=pltpu.CompilerParams(vmem_limit_bytes=60 * 1024 * 1024),
    )(prompts, lengths, begins, holders, queries, out_grad, resp_keys, resp_values, own_kv, other_kv)


def body(
    n,
    queries,
    resp_keys,
    resp_values,
    out_grad,
    prompt_keys,
    prompt_values,
    slot_prompt,
    slot_length,
    slot_begin,
    block_prompt,
):
    width = resp_keys.shape[1]
    prow = prompt_keys.shape[0]
    own = jnp.pad(prompt_keys, ((0, 0), (0, width))) + jnp.pad(prompt_values, ((0, 0), (width, 0)))
    own = jnp.broadcast_to(own[None], (n // 2, prow, 2 * width)).reshape(-1, 2 * width)
    own_kv = exchange(own, n)
    other_kv = swap_cores(own_kv, n)
    query_grad, key_grad, value_grad, own_term, other_term = slot_grads(
        queries, resp_keys, resp_values, out_grad, own_kv, other_kv,
        slot_prompt, slot_length, slot_begin, block_prompt,
    )
    prompt_grads = owned_sum(own_term, other_term, n, prow, width)
    return query_grad, key_grad, value_grad, *prompt_grads


def solution(mesh):
    n = mesh.shape["seq"]
    rows = P(("groups", "seq"), None)
    slots = P(("groups", "seq"))
    return jax.shard_map(
        functools.partial(body, n),
        mesh=mesh,
        in_specs=(rows,) * 6 + (slots,) * 3 + (P("groups"),),
        out_specs=(rows,) * 5,
        check_vma=False,
    )
```

```python
import functools
import math

import jax
import jax.numpy as jnp
from jax import lax
from jax.experimental import pallas as pl
from jax.experimental.pallas import tpu as pltpu
from jax.sharding import PartitionSpec as P

OWNERS = 8
TILE = 128
ROWS = 64
PIECE = 16
score_scale = 0.08838834764831845
EXP2_SCALE = score_scale * math.log2(math.e)
MASKED = -1e30

ACROSS = (((1,), (1,)), ((), ()))


def same_core_groups(n):
    return [list(range(core, n, 2)) for core in range(2)]


def swap_cores(x, n):
    return lax.ppermute(x, "seq", [(i, i ^ 1) for i in range(n)])


def exchange(x, n):
    return lax.all_to_all(
        x, "seq", split_axis=0, concat_axis=0, axis_index_groups=same_core_groups(n), tiled=True
    )


def block_position(holder, me, n):
    return ((holder ^ me) & 1) * (n // 2) + (holder >> 1)


def grad_kernel(
    prompt_hbm,
    length_hbm,
    begin_hbm,
    holder_hbm,
    q_hbm,
    g_hbm,
    rk_hbm,
    rv_hbm,
    own_hbm,
    other_hbm,
    dq_hbm,
    drk_hbm,
    drv_hbm,
    own_term_hbm,
    other_term_hbm,
    prompt_ref,
    length_ref,
    begin_ref,
    holder_ref,
    place,
    q_all,
    g_all,
    rk_all,
    rv_all,
    dq_all,
    drk_all,
    drv_all,
    kv,
    term_ref,
    keys,
    values,
    keys_t,
    live_bias,
    causal_bias,
    turned,
    exps,
    dprobs,
    prob16,
    dscore16,
    kt,
    vt,
    sem_scalar,
    sem_resp,
    sem_q,
    sem_g,
    sem_dq,
    sem_drk,
    sem_drv,
    sem_kv,
    sem_term,
):
    n = holder_ref.shape[0]
    slots = prompt_ref.shape[0]
    rows, width = rk_all.shape
    slot_rows = rows // slots
    tiles = slot_rows // TILE
    prow = term_ref.shape[0] // n
    prompt_len = prow * OWNERS
    heads = q_all.shape[1] // width
    me = lax.axis_index("seq")

    scalar_copies = [
        pltpu.make_async_copy(src, dst, sem_scalar.at[i])
        for i, (src, dst) in enumerate(
            [
                (prompt_hbm, prompt_ref),
                (length_hbm, length_ref),
                (begin_hbm, begin_ref),
                (holder_hbm, holder_ref),
            ]
        )
    ]
    resp_copies = [
        pltpu.make_async_copy(rk_hbm, rk_all, sem_resp.at[0]),
        pltpu.make_async_copy(rv_hbm, rv_all, sem_resp.at[1]),
    ]

    def tile_rows(chunk):
        return pl.ds(pl.multiple_of(chunk * TILE, TILE), TILE)

    def q_copy(chunk):
        part = tile_rows(chunk)
        return pltpu.make_async_copy(q_hbm.at[part], q_all.at[part], sem_q.at[chunk])

    def g_copy(chunk):
        part = tile_rows(chunk)
        return pltpu.make_async_copy(g_hbm.at[part], g_all.at[part], sem_g.at[chunk])

    def dq_copy(chunk):
        part = tile_rows(chunk)
        return pltpu.make_async_copy(dq_all.at[part], dq_hbm.at[part], sem_dq.at[chunk])

    def slot_part(s):
        return pl.ds(pl.multiple_of(s * slot_rows, slot_rows), slot_rows)

    def drk_copy(s):
        return pltpu.make_async_copy(
            drk_all.at[slot_part(s)], drk_hbm.at[slot_part(s)], sem_drk.at[s]
        )

    def drv_copy(s):
        return pltpu.make_async_copy(
            drv_all.at[slot_part(s)], drv_hbm.at[slot_part(s)], sem_drv.at[s]
        )

    half_rows = term_ref.shape[0] // 2
    kv_copies = [
        pltpu.make_async_copy(src, kv.at[pl.ds(i * half_rows, half_rows)], sem_kv.at[i])
        for i, src in enumerate([own_hbm, other_hbm])
    ]
    term_copies = [
        pltpu.make_async_copy(term_ref.at[pl.ds(i * half_rows, half_rows)], dst, sem_term.at[i])
        for i, dst in enumerate([own_term_hbm, other_term_hbm])
    ]
    for copy in scalar_copies + kv_copies + resp_copies:
        copy.start()
    q_copy(0).start()
    g_copy(0).start()

    term_ref[...] = jnp.zeros_like(term_ref)
    causal_bias[...] = jnp.where(
        lax.broadcasted_iota(jnp.int32, causal_bias.shape, 0)
        <= (lax.broadcasted_iota(jnp.int32, causal_bias.shape, 1) & (ROWS - 1)),
        0.0,
        MASKED,
    )
    for copy in scalar_copies + kv_copies + resp_copies:
        copy.wait()

    for chunk in range(1, slots * tiles):
        q_copy(chunk).start()
        g_copy(chunk).start()

    @pl.loop(0, n)
    def _(j):
        place[holder_ref[j]] = j

    wide = 2 * TILE
    at_once = wide // ROWS
    steps_of = slot_rows // ROWS
    units = []
    for s in range(slots):
        order = range(steps_of) if s + 1 < slots else range(steps_of - 1, -1, -1)
        units += [(s, index) for index in order]

    def columns_of(u):
        return prompt_len + (units[u][1] + 1) * ROWS

    def padded_columns(u):
        return -(-columns_of(u) // TILE) * TILE

    def rows_of(u):
        s, index = units[u]
        first = s * slot_rows + index * ROWS
        return slice(first, first + ROWS)

    def chunk_of(u):
        return rows_of(u).start // TILE

    def chunks(u):
        columns = columns_of(u)
        return [(c, min(TILE, columns - c)) for c in range(0, columns, TILE)]

    def lanes_of(side):
        return slice(side * wide, (side + 1) * wide)

    def stacked(ref, u, side):
        first = side * at_once
        return jnp.concatenate(
            [ref[rows_of(u), (first + h) * width : (first + h + 1) * width] for h in range(at_once)],
            axis=0,
        )

    def fold(x, how):
        return how(how(x.reshape(x.shape[0] // 8, 8, x.shape[1]), axis=0), axis=0, keepdims=True)

    def prepare(s):
        first_block = prompt_ref[s] * OWNERS
        for o in range(OWNERS):
            start = block_position(place[first_block + o], me, n) * prow
            source = pl.ds(pl.multiple_of(start, prow), prow)
            keys[s, o * prow : (o + 1) * prow, :] = kv[source, 0:width]
            values[s, o * prow : (o + 1) * prow, :] = kv[source, width : 2 * width]
        own = slice(s * slot_rows, (s + 1) * slot_rows)
        keys[s, prompt_len:, :] = rk_all[own, :]
        values[s, prompt_len:, :] = rv_all[own, :]
        yield
        keys_t[s] = keys[s].astype(jnp.float32).T.astype(jnp.bfloat16)
        yield
        column = lax.broadcasted_iota(jnp.int32, (slot_rows, TILE), 0)
        live_bias[s] = jnp.where(column >= begin_ref[s], 0.0, MASKED)
        kt[s] = jnp.zeros_like(kt[s])
        vt[s] = jnp.zeros_like(vt[s])
        yield

    def finish(s):
        own = slice(s * slot_rows, (s + 1) * slot_rows)
        prompt_kt = kt[s, :, 0:prompt_len].T * score_scale
        prompt_vt = vt[s, :, 0:prompt_len].T
        yield
        drk_all[own, :] = kt[s, :, prompt_len:].T * score_scale
        drv_all[own, :] = vt[s, :, prompt_len:].T
        yield
        first_block = prompt_ref[s] * OWNERS
        for o in range(OWNERS):
            start = block_position(place[first_block + o], me, n) * prow
            target = pl.ds(pl.multiple_of(start, prow), prow)
            block = slice(o * prow, (o + 1) * prow)
            term_ref[target, 0:width] += prompt_kt[block]
            term_ref[target, width : 2 * width] += prompt_vt[block]
        yield

    def head(u, side, out):
        s, index = units[u]
        columns, buf = columns_of(u), u % 2
        q2t, g2t = turned.at[u % 3, 0, :, lanes_of(side)], turned.at[u % 3, 1, :, lanes_of(side)]
        q2t[...] = stacked(q_all, u, side).T
        g2t[...] = stacked(g_all, u, side).T
        tops, totals, weights = [], [], []
        all_scores = jnp.dot(keys[s, 0:columns, :], q2t[...], preferred_element_type=jnp.float32)
        all_dprobs = jnp.dot(values[s, 0:columns, :], g2t[...], preferred_element_type=jnp.float32)
        for c, size in chunks(u):
            part = slice(c, c + size)
            block = all_scores[part]
            if c >= prompt_len:
                bias = live_bias[s, c - prompt_len : c - prompt_len + size, :]
                if c + size == columns:
                    last = bias[size - ROWS :] + causal_bias[...]
                    bias = last if size == ROWS else jnp.concatenate([bias[: size - ROWS], last], axis=0)
                block = block + jnp.concatenate([bias, bias], axis=1)
            top = fold(block, jnp.max) * EXP2_SCALE
            e = jnp.exp2(block * EXP2_SCALE - top)
            exps[buf, side, part, :] = e
            yield
            d = all_dprobs[part]
            dprobs[buf, side, part, :] = d
            tops.append(top)
            totals.append(fold(e, jnp.sum))
            weights.append(fold(e * d, jnp.sum))
            yield
        top = functools.reduce(jnp.maximum, tops)
        factors = [jnp.exp2(part - top) for part in tops]
        total = functools.reduce(jnp.add, [f * x for f, x in zip(factors, totals)])
        weighted = functools.reduce(jnp.add, [f * x for f, x in zip(factors, weights)])
        row = index * ROWS + (lax.broadcasted_iota(jnp.int32, (1, wide), 1) & (ROWS - 1))
        live = (row >= begin_ref[s]) & (row < begin_ref[s] + length_ref[s])
        inverse = jnp.where(live, 1.0 / total, 0.0)
        out["delta"] = weighted * inverse
        out["factors"] = [f * inverse for f in factors]

    def tail(u, side, stats):
        buf, lanes = u % 2, lanes_of(side)
        delta = stats["delta"]
        for (c, size), factor in zip(chunks(u), stats["factors"]):
            for first in range(c, c + size, PIECE):
                part = slice(first, first + PIECE)
                p = exps[buf, side, part, :] * factor
                prob16[buf, part, lanes] = p.astype(jnp.bfloat16)
                ds = p * (dprobs[buf, side, part, :] - delta)
                dscore16[buf, part, lanes] = ds.astype(jnp.bfloat16)
            yield
        pad = slice(columns_of(u), padded_columns(u))
        if pad.start < pad.stop:
            zero = jnp.zeros((pad.stop - pad.start, wide), jnp.bfloat16)
            prob16[buf, pad, lanes] = zero
            dscore16[buf, pad, lanes] = zero
            yield

    def flush_keys(u):
        s, columns = units[u][0], padded_columns(u)
        kt[s, :, 0:columns] += lax.dot_general(
            turned[u % 3, 0], dscore16[u % 2, 0:columns, :], ACROSS, preferred_element_type=jnp.float32
        )
        yield

    def flush_values(u):
        s, columns = units[u][0], padded_columns(u)
        vt[s, :, 0:columns] += lax.dot_general(
            turned[u % 3, 1], prob16[u % 2, 0:columns, :], ACROSS, preferred_element_type=jnp.float32
        )
        yield

    def flush_queries(u):
        s, columns = units[u][0], padded_columns(u)
        for side in range(2):
            ds = dscore16[u % 2, 0:columns, lanes_of(side)]
            dqt = jnp.dot(keys_t[s, :, 0:columns], ds, preferred_element_type=jnp.float32)
            dq = dqt.T * score_scale
            for h in range(at_once):
                first = (side * at_once + h) * width
                dq_all[rows_of(u), first : first + width] = dq[h * ROWS : (h + 1) * ROWS]
            yield

    def together(*steps):
        steps = list(steps)
        while steps:
            for step in list(steps):
                if next(step, steps) is steps:
                    steps.remove(step)

    def wait_rows(u):
        if all(chunk_of(other) != chunk_of(u) for other in range(u)):
            q_copy(chunk_of(u)).wait()
            g_copy(chunk_of(u)).wait()

    def send_rows(u):
        if all(chunk_of(other) != chunk_of(u) for other in range(u + 1, len(units))):
            dq_copy(chunk_of(u)).start()

    count = len(units)
    per_slot = steps_of
    stats = [({}, {}) for _ in units]
    together(prepare(0))
    wait_rows(0)
    together(head(0, 0, stats[0][0]))
    for u in range(count):
        s = units[u][0]
        steps = [head(u, 1, stats[u][1]), tail(u, 0, stats[u][0])]
        if u >= 1:
            steps += [flush_keys(u - 1), flush_queries(u - 1)]
        if u % per_slot == 2 and s + 1 < slots:
            steps.append(prepare(s + 1))
        if u % per_slot == 1 and s >= 1:
            steps.append(finish(s - 1))
        together(*steps)
        if u >= 1:
            send_rows(u - 1)
        if u % per_slot == 1 and s >= 1:
            drk_copy(s - 1).start()
            drv_copy(s - 1).start()
        steps = []
        if u + 1 < count:
            wait_rows(u + 1)
            steps.append(head(u + 1, 0, stats[u + 1][0]))
        steps.append(tail(u, 1, stats[u][1]))
        if u >= 1:
            steps.append(flush_values(u - 1))
        together(*steps)
    together(flush_keys(count - 1), flush_values(count - 1), flush_queries(count - 1))
    send_rows(count - 1)
    together(finish(slots - 1))
    drk_copy(slots - 1).start()
    drv_copy(slots - 1).start()

    for copy in term_copies:
        copy.start()
    for copy in term_copies:
        copy.wait()
    for chunk in range(slots * tiles):
        dq_copy(chunk).wait()
    for s in range(slots):
        drk_copy(s).wait()
        drv_copy(s).wait()


def slot_grads(queries, resp_keys, resp_values, out_grad, own_kv, other_kv, prompts, lengths, begins, holders):
    slots = prompts.shape[0]
    rows, columns = queries.shape
    slot_rows, width = rows // slots, resp_keys.shape[1]
    n = holders.shape[0]
    prow = 2 * own_kv.shape[0] // n
    total = prow * OWNERS + slot_rows
    tiles = slot_rows // TILE
    hbm = pl.BlockSpec(memory_space=pltpu.HBM)
    f32, bf16 = jnp.float32, jnp.bfloat16
    return pl.pallas_call(
        grad_kernel,
        in_specs=[hbm] * 10,
        out_specs=[hbm] * 5,
        out_shape=[
            jax.ShapeDtypeStruct((rows, columns), f32),
            jax.ShapeDtypeStruct((rows, width), f32),
            jax.ShapeDtypeStruct((rows, width), f32),
            jax.ShapeDtypeStruct((n * prow // 2, 2 * width), f32),
            jax.ShapeDtypeStruct((n * prow // 2, 2 * width), f32),
        ],
        scratch_shapes=[
            pltpu.SMEM((slots,), jnp.int32),
            pltpu.SMEM((slots,), jnp.int32),
            pltpu.SMEM((slots,), jnp.int32),
            pltpu.SMEM((n,), jnp.int32),
            pltpu.SMEM((n,), jnp.int32),
            pltpu.VMEM((rows, columns), bf16),
            pltpu.VMEM((rows, columns), bf16),
            pltpu.VMEM((rows, width), bf16),
            pltpu.VMEM((rows, width), bf16),
            pltpu.VMEM((rows, columns), f32),
            pltpu.VMEM((rows, width), f32),
            pltpu.VMEM((rows, width), f32),
            pltpu.VMEM((n * prow, 2 * width), bf16),
            pltpu.VMEM((n * prow, 2 * width), f32),
            pltpu.VMEM((slots, total, width), bf16),
            pltpu.VMEM((slots, total, width), bf16),
            pltpu.VMEM((slots, width, total), bf16),
            pltpu.VMEM((slots, slot_rows, TILE), f32),
            pltpu.VMEM((ROWS, TILE), f32),
            pltpu.VMEM((3, 2, width, 4 * TILE), bf16),
            pltpu.VMEM((2, 2, total, 2 * TILE), f32),
            pltpu.VMEM((2, 2, total, 2 * TILE), f32),
            pltpu.VMEM((2, total, 4 * TILE), bf16),
            pltpu.VMEM((2, total, 4 * TILE), bf16),
            pltpu.VMEM((slots, width, total), f32),
            pltpu.VMEM((slots, width, total), f32),
            pltpu.SemaphoreType.DMA((4,)),
            pltpu.SemaphoreType.DMA((2,)),
            pltpu.SemaphoreType.DMA((slots * tiles,)),
            pltpu.SemaphoreType.DMA((slots * tiles,)),
            pltpu.SemaphoreType.DMA((slots * tiles,)),
            pltpu.SemaphoreType.DMA((slots,)),
            pltpu.SemaphoreType.DMA((slots,)),
            pltpu.SemaphoreType.DMA((2,)),
            pltpu.SemaphoreType.DMA((2,)),
        ],
        compiler_params=pltpu.CompilerParams(vmem_limit_bytes=60 * 1024 * 1024),
    )(prompts, lengths, begins, holders, queries, out_grad, resp_keys, resp_values, own_kv, other_kv)


def body(
    n,
    queries,
    resp_keys,
    resp_values,
    out_grad,
    prompt_keys,
    prompt_values,
    slot_prompt,
    slot_length,
    slot_begin,
    block_prompt,
):
    width = resp_keys.shape[1]
    prow = prompt_keys.shape[0]
    own = jnp.pad(prompt_keys, ((0, 0), (0, width))) + jnp.pad(prompt_values, ((0, 0), (width, 0)))
    own = jnp.broadcast_to(own[None], (n // 2, prow, 2 * width)).reshape(-1, 2 * width)
    own_kv = exchange(own, n)
    other_kv = swap_cores(own_kv, n)
    query_grad, key_grad, value_grad, own_term, other_term = slot_grads(
        queries, resp_keys, resp_values, out_grad, own_kv, other_kv,
        slot_prompt, slot_length, slot_begin, block_prompt,
    )
    parts = exchange(own_term + swap_cores(other_term, n), n)
    owned = jnp.sum(parts.reshape(n // 2, prow, 2 * width), axis=0)
    return query_grad, key_grad, value_grad, owned[:, :width], owned[:, width:]


def solution(mesh):
    n = mesh.shape["seq"]
    rows = P(("groups", "seq"), None)
    slots = P(("groups", "seq"))
    return jax.shard_map(
        functools.partial(body, n),
        mesh=mesh,
        in_specs=(rows,) * 6 + (slots,) * 3 + (P("groups"),),
        out_specs=(rows,) * 5,
        check_vma=False,
    )
```

```python
import functools
import math

import jax
import jax.numpy as jnp
from jax import lax
from jax.experimental import pallas as pl
from jax.experimental.pallas import tpu as pltpu
from jax.sharding import PartitionSpec as P

OWNERS = 8
TILE = 128
ROWS = 64
SPAN = 64
PIECE = 16
score_scale = 0.08838834764831845
EXP2_SCALE = score_scale * math.log2(math.e)
MASKED = -1e30

ACROSS = (((1,), (1,)), ((), ()))


def same_core_groups(n):
    return [list(range(core, n, 2)) for core in range(2)]


def swap_cores(x, n):
    return lax.ppermute(x, "seq", [(i, i ^ 1) for i in range(n)])


def exchange(x, n):
    return lax.all_to_all(
        x, "seq", split_axis=0, concat_axis=0, axis_index_groups=same_core_groups(n), tiled=True
    )


def block_position(holder, me, n):
    return ((holder ^ me) & 1) * (n // 2) + (holder >> 1)


def grad_kernel(
    prompt_hbm,
    length_hbm,
    begin_hbm,
    holder_hbm,
    q_hbm,
    g_hbm,
    rk_hbm,
    rv_hbm,
    own_hbm,
    other_hbm,
    dq_hbm,
    drk_hbm,
    drv_hbm,
    own_term_hbm,
    other_term_hbm,
    prompt_ref,
    length_ref,
    begin_ref,
    holder_ref,
    place,
    q_all,
    g_all,
    rk_all,
    rv_all,
    dq_all,
    drk_all,
    drv_all,
    kv,
    term_ref,
    keys,
    values,
    keys_t,
    live_bias,
    causal_bias,
    turned,
    exps,
    dprobs,
    prob16,
    dscore16,
    kt,
    vt,
    sem_scalar,
    sem_resp,
    sem_q,
    sem_g,
    sem_dq,
    sem_drk,
    sem_drv,
    sem_kv,
    sem_term,
):
    n = holder_ref.shape[0]
    slots = prompt_ref.shape[0]
    rows, width = rk_all.shape
    slot_rows = rows // slots
    tiles = slot_rows // TILE
    prow = term_ref.shape[0] // n
    prompt_len = prow * OWNERS
    heads = q_all.shape[1] // width
    me = lax.axis_index("seq")

    scalar_copies = [
        pltpu.make_async_copy(src, dst, sem_scalar.at[i])
        for i, (src, dst) in enumerate(
            [
                (prompt_hbm, prompt_ref),
                (length_hbm, length_ref),
                (begin_hbm, begin_ref),
                (holder_hbm, holder_ref),
            ]
        )
    ]
    resp_copies = [
        pltpu.make_async_copy(rk_hbm, rk_all, sem_resp.at[0]),
        pltpu.make_async_copy(rv_hbm, rv_all, sem_resp.at[1]),
    ]

    def tile_rows(chunk):
        return pl.ds(pl.multiple_of(chunk * TILE, TILE), TILE)

    def q_copy(chunk):
        part = tile_rows(chunk)
        return pltpu.make_async_copy(q_hbm.at[part], q_all.at[part], sem_q.at[chunk])

    def g_copy(chunk):
        part = tile_rows(chunk)
        return pltpu.make_async_copy(g_hbm.at[part], g_all.at[part], sem_g.at[chunk])

    def dq_copy(chunk):
        part = tile_rows(chunk)
        return pltpu.make_async_copy(dq_all.at[part], dq_hbm.at[part], sem_dq.at[chunk])

    def slot_part(s):
        return pl.ds(pl.multiple_of(s * slot_rows, slot_rows), slot_rows)

    def drk_copy(s):
        return pltpu.make_async_copy(
            drk_all.at[slot_part(s)], drk_hbm.at[slot_part(s)], sem_drk.at[s]
        )

    def drv_copy(s):
        return pltpu.make_async_copy(
            drv_all.at[slot_part(s)], drv_hbm.at[slot_part(s)], sem_drv.at[s]
        )

    half_rows = term_ref.shape[0] // 2
    kv_copies = [
        pltpu.make_async_copy(src, kv.at[pl.ds(i * half_rows, half_rows)], sem_kv.at[i])
        for i, src in enumerate([own_hbm, other_hbm])
    ]
    term_copies = [
        pltpu.make_async_copy(term_ref.at[pl.ds(i * half_rows, half_rows)], dst, sem_term.at[i])
        for i, dst in enumerate([own_term_hbm, other_term_hbm])
    ]
    for copy in scalar_copies + kv_copies + resp_copies:
        copy.start()
    q_copy(0).start()
    g_copy(0).start()

    term_ref[...] = jnp.zeros_like(term_ref)
    causal_bias[...] = jnp.where(
        lax.broadcasted_iota(jnp.int32, causal_bias.shape, 0)
        <= (lax.broadcasted_iota(jnp.int32, causal_bias.shape, 1) & (ROWS - 1)),
        0.0,
        MASKED,
    )
    for copy in scalar_copies + kv_copies + resp_copies:
        copy.wait()

    for chunk in range(1, slots * tiles):
        q_copy(chunk).start()
        g_copy(chunk).start()

    @pl.loop(0, n)
    def _(j):
        place[holder_ref[j]] = j

    wide = 2 * TILE
    at_once = wide // ROWS
    steps_of = slot_rows // ROWS
    units = []
    for s in range(slots):
        order = range(steps_of) if s + 1 < slots else range(steps_of - 1, -1, -1)
        units += [(s, index) for index in order]

    def columns_of(u):
        return prompt_len + (units[u][1] + 1) * ROWS

    def padded_columns(u):
        return -(-columns_of(u) // TILE) * TILE

    def rows_of(u):
        s, index = units[u]
        first = s * slot_rows + index * ROWS
        return slice(first, first + ROWS)

    def chunk_of(u):
        return rows_of(u).start // TILE

    def chunks(u):
        columns = columns_of(u)
        return [(c, min(SPAN, columns - c)) for c in range(0, columns, SPAN)]

    def lanes_of(side):
        return slice(side * wide, (side + 1) * wide)

    def stacked(ref, u, side):
        first = side * at_once
        return jnp.concatenate(
            [ref[rows_of(u), (first + h) * width : (first + h + 1) * width] for h in range(at_once)],
            axis=0,
        )

    def classes(x):
        return x.reshape(x.shape[0] // 8, 8, x.shape[1])

    def prepare(s):
        first_block = prompt_ref[s] * OWNERS
        for o in range(OWNERS):
            start = block_position(place[first_block + o], me, n) * prow
            source = pl.ds(pl.multiple_of(start, prow), prow)
            keys[s, o * prow : (o + 1) * prow, :] = kv[source, 0:width]
            values[s, o * prow : (o + 1) * prow, :] = kv[source, width : 2 * width]
        own = slice(s * slot_rows, (s + 1) * slot_rows)
        keys[s, prompt_len:, :] = rk_all[own, :]
        values[s, prompt_len:, :] = rv_all[own, :]
        yield
        keys_t[s] = keys[s].astype(jnp.float32).T.astype(jnp.bfloat16)
        yield
        column = lax.broadcasted_iota(jnp.int32, (slot_rows, TILE), 0)
        live_bias[s] = jnp.where(column >= begin_ref[s], 0.0, MASKED)
        kt[s] = jnp.zeros_like(kt[s])
        vt[s] = jnp.zeros_like(vt[s])
        yield

    def finish(s):
        own = slice(s * slot_rows, (s + 1) * slot_rows)
        prompt_kt = kt[s, :, 0:prompt_len].T * score_scale
        prompt_vt = vt[s, :, 0:prompt_len].T
        yield
        drk_all[own, :] = kt[s, :, prompt_len:].T * score_scale
        drv_all[own, :] = vt[s, :, prompt_len:].T
        yield
        first_block = prompt_ref[s] * OWNERS
        for o in range(OWNERS):
            start = block_position(place[first_block + o], me, n) * prow
            target = pl.ds(pl.multiple_of(start, prow), prow)
            block = slice(o * prow, (o + 1) * prow)
            term_ref[target, 0:width] += prompt_kt[block]
            term_ref[target, width : 2 * width] += prompt_vt[block]
        yield

    def head(u, side, out):
        s, index = units[u]
        columns, buf = columns_of(u), u % 2
        q2t, g2t = turned.at[u % 3, 0, :, lanes_of(side)], turned.at[u % 3, 1, :, lanes_of(side)]
        q2t[...] = stacked(q_all, u, side).T
        g2t[...] = stacked(g_all, u, side).T
        tops, totals, weights = [], [], []
        all_scores = jnp.dot(keys[s, 0:columns, :], q2t[...], preferred_element_type=jnp.float32)
        all_dprobs = jnp.dot(values[s, 0:columns, :], g2t[...], preferred_element_type=jnp.float32)
        for c, size in chunks(u):
            part = slice(c, c + size)
            block = all_scores[part]
            if c >= prompt_len:
                bias = live_bias[s, c - prompt_len : c - prompt_len + size, :]
                if c + size == columns:
                    last = bias[size - ROWS :] + causal_bias[...]
                    bias = last if size == ROWS else jnp.concatenate([bias[: size - ROWS], last], axis=0)
                block = block + jnp.concatenate([bias, bias], axis=1)
            block = classes(block)
            top = jnp.max(block, axis=0) * EXP2_SCALE
            e = jnp.exp2(block * EXP2_SCALE - top[None])
            exps[buf, side, part, :] = e.reshape(size, wide)
            yield
            d = all_dprobs[part]
            dprobs[buf, side, part, :] = d
            tops.append(top)
            totals.append(jnp.sum(e, axis=0))
            weights.append(jnp.sum(e * classes(d), axis=0))
            yield
        top = jnp.max(functools.reduce(jnp.maximum, tops), axis=0, keepdims=True)
        factors = [jnp.exp2(part - top) for part in tops]
        total = functools.reduce(jnp.add, [f * x for f, x in zip(factors, totals)])
        weighted = functools.reduce(jnp.add, [f * x for f, x in zip(factors, weights)])
        total = jnp.sum(total, axis=0, keepdims=True)
        weighted = jnp.sum(weighted, axis=0, keepdims=True)
        row = index * ROWS + (lax.broadcasted_iota(jnp.int32, (1, wide), 1) & (ROWS - 1))
        live = (row >= begin_ref[s]) & (row < begin_ref[s] + length_ref[s])
        inverse = jnp.where(live, 1.0 / total, 0.0)
        out["delta"] = weighted * inverse
        out["factors"] = [f * inverse for f in factors]

    def tail(u, side, stats):
        buf, lanes = u % 2, lanes_of(side)
        delta = stats["delta"]
        for (c, size), factor in zip(chunks(u), stats["factors"]):
            for first in range(c, c + size, PIECE):
                part = slice(first, first + PIECE)
                p = (classes(exps[buf, side, part, :]) * factor[None]).reshape(PIECE, wide)
                prob16[buf, part, lanes] = p.astype(jnp.bfloat16)
                ds = p * (dprobs[buf, side, part, :] - delta)
                dscore16[buf, part, lanes] = ds.astype(jnp.bfloat16)
            yield
        pad = slice(columns_of(u), padded_columns(u))
        if pad.start < pad.stop:
            zero = jnp.zeros((pad.stop - pad.start, wide), jnp.bfloat16)
            prob16[buf, pad, lanes] = zero
            dscore16[buf, pad, lanes] = zero
            yield

    def flush_keys(u):
        s, columns = units[u][0], padded_columns(u)
        kt[s, :, 0:columns] += lax.dot_general(
            turned[u % 3, 0], dscore16[u % 2, 0:columns, :], ACROSS, preferred_element_type=jnp.float32
        )
        yield

    def flush_values(u):
        s, columns = units[u][0], padded_columns(u)
        vt[s, :, 0:columns] += lax.dot_general(
            turned[u % 3, 1], prob16[u % 2, 0:columns, :], ACROSS, preferred_element_type=jnp.float32
        )
        yield

    def flush_queries(u):
        s, columns = units[u][0], padded_columns(u)
        for side in range(2):
            ds = dscore16[u % 2, 0:columns, lanes_of(side)]
            dqt = jnp.dot(keys_t[s, :, 0:columns], ds, preferred_element_type=jnp.float32)
            dq = dqt.T * score_scale
            for h in range(at_once):
                first = (side * at_once + h) * width
                dq_all[rows_of(u), first : first + width] = dq[h * ROWS : (h + 1) * ROWS]
            yield

    def together(*steps):
        steps = list(steps)
        while steps:
            for step in list(steps):
                if next(step, steps) is steps:
                    steps.remove(step)

    def wait_rows(u):
        if all(chunk_of(other) != chunk_of(u) for other in range(u)):
            q_copy(chunk_of(u)).wait()
            g_copy(chunk_of(u)).wait()

    def send_rows(u):
        if all(chunk_of(other) != chunk_of(u) for other in range(u + 1, len(units))):
            dq_copy(chunk_of(u)).start()

    count = len(units)
    per_slot = steps_of
    stats = [({}, {}) for _ in units]
    together(prepare(0))
    wait_rows(0)
    together(head(0, 0, stats[0][0]))
    for u in range(count):
        s = units[u][0]
        steps = [head(u, 1, stats[u][1]), tail(u, 0, stats[u][0])]
        if u >= 1:
            steps += [flush_keys(u - 1), flush_queries(u - 1)]
        if u % per_slot == 2 and s + 1 < slots:
            steps.append(prepare(s + 1))
        if u % per_slot == 1 and s >= 1:
            steps.append(finish(s - 1))
        together(*steps)
        if u >= 1:
            send_rows(u - 1)
        if u % per_slot == 1 and s >= 1:
            drk_copy(s - 1).start()
            drv_copy(s - 1).start()
        steps = []
        if u + 1 < count:
            wait_rows(u + 1)
            steps.append(head(u + 1, 0, stats[u + 1][0]))
        steps.append(tail(u, 1, stats[u][1]))
        if u >= 1:
            steps.append(flush_values(u - 1))
        together(*steps)
    together(flush_keys(count - 1), flush_values(count - 1), flush_queries(count - 1))
    send_rows(count - 1)
    together(finish(slots - 1))
    drk_copy(slots - 1).start()
    drv_copy(slots - 1).start()

    for copy in term_copies:
        copy.start()
    for copy in term_copies:
        copy.wait()
    for chunk in range(slots * tiles):
        dq_copy(chunk).wait()
    for s in range(slots):
        drk_copy(s).wait()
        drv_copy(s).wait()


def slot_grads(queries, resp_keys, resp_values, out_grad, own_kv, other_kv, prompts, lengths, begins, holders):
    slots = prompts.shape[0]
    rows, columns = queries.shape
    slot_rows, width = rows // slots, resp_keys.shape[1]
    n = holders.shape[0]
    prow = 2 * own_kv.shape[0] // n
    total = prow * OWNERS + slot_rows
    tiles = slot_rows // TILE
    hbm = pl.BlockSpec(memory_space=pltpu.HBM)
    f32, bf16 = jnp.float32, jnp.bfloat16
    return pl.pallas_call(
        grad_kernel,
        in_specs=[hbm] * 10,
        out_specs=[hbm] * 5,
        out_shape=[
            jax.ShapeDtypeStruct((rows, columns), f32),
            jax.ShapeDtypeStruct((rows, width), f32),
            jax.ShapeDtypeStruct((rows, width), f32),
            jax.ShapeDtypeStruct((n * prow // 2, 2 * width), f32),
            jax.ShapeDtypeStruct((n * prow // 2, 2 * width), f32),
        ],
        scratch_shapes=[
            pltpu.SMEM((slots,), jnp.int32),
            pltpu.SMEM((slots,), jnp.int32),
            pltpu.SMEM((slots,), jnp.int32),
            pltpu.SMEM((n,), jnp.int32),
            pltpu.SMEM((n,), jnp.int32),
            pltpu.VMEM((rows, columns), bf16),
            pltpu.VMEM((rows, columns), bf16),
            pltpu.VMEM((rows, width), bf16),
            pltpu.VMEM((rows, width), bf16),
            pltpu.VMEM((rows, columns), f32),
            pltpu.VMEM((rows, width), f32),
            pltpu.VMEM((rows, width), f32),
            pltpu.VMEM((n * prow, 2 * width), bf16),
            pltpu.VMEM((n * prow, 2 * width), f32),
            pltpu.VMEM((slots, total, width), bf16),
            pltpu.VMEM((slots, total, width), bf16),
            pltpu.VMEM((slots, width, total), bf16),
            pltpu.VMEM((slots, slot_rows, TILE), f32),
            pltpu.VMEM((ROWS, TILE), f32),
            pltpu.VMEM((3, 2, width, 4 * TILE), bf16),
            pltpu.VMEM((2, 2, total, 2 * TILE), f32),
            pltpu.VMEM((2, 2, total, 2 * TILE), f32),
            pltpu.VMEM((2, total, 4 * TILE), bf16),
            pltpu.VMEM((2, total, 4 * TILE), bf16),
            pltpu.VMEM((slots, width, total), f32),
            pltpu.VMEM((slots, width, total), f32),
            pltpu.SemaphoreType.DMA((4,)),
            pltpu.SemaphoreType.DMA((2,)),
            pltpu.SemaphoreType.DMA((slots * tiles,)),
            pltpu.SemaphoreType.DMA((slots * tiles,)),
            pltpu.SemaphoreType.DMA((slots * tiles,)),
            pltpu.SemaphoreType.DMA((slots,)),
            pltpu.SemaphoreType.DMA((slots,)),
            pltpu.SemaphoreType.DMA((2,)),
            pltpu.SemaphoreType.DMA((2,)),
        ],
        compiler_params=pltpu.CompilerParams(vmem_limit_bytes=60 * 1024 * 1024),
    )(prompts, lengths, begins, holders, queries, out_grad, resp_keys, resp_values, own_kv, other_kv)


def body(
    n,
    queries,
    resp_keys,
    resp_values,
    out_grad,
    prompt_keys,
    prompt_values,
    slot_prompt,
    slot_length,
    slot_begin,
    block_prompt,
):
    width = resp_keys.shape[1]
    prow = prompt_keys.shape[0]
    own = jnp.pad(prompt_keys, ((0, 0), (0, width))) + jnp.pad(prompt_values, ((0, 0), (width, 0)))
    own = jnp.broadcast_to(own[None], (n // 2, prow, 2 * width)).reshape(-1, 2 * width)
    own_kv = exchange(own, n)
    other_kv = swap_cores(own_kv, n)
    query_grad, key_grad, value_grad, own_term, other_term = slot_grads(
        queries, resp_keys, resp_values, out_grad, own_kv, other_kv,
        slot_prompt, slot_length, slot_begin, block_prompt,
    )
    parts = exchange(own_term + swap_cores(other_term, n), n)
    owned = jnp.sum(parts.reshape(n // 2, prow, 2 * width), axis=0)
    return query_grad, key_grad, value_grad, owned[:, :width], owned[:, width:]


def solution(mesh):
    n = mesh.shape["seq"]
    rows = P(("groups", "seq"), None)
    slots = P(("groups", "seq"))
    return jax.shard_map(
        functools.partial(body, n),
        mesh=mesh,
        in_specs=(rows,) * 6 + (slots,) * 3 + (P("groups"),),
        out_specs=(rows,) * 5,
        check_vma=False,
    )
```

```python
import functools
import math

import jax
import jax.numpy as jnp
from jax import lax
from jax.experimental import pallas as pl
from jax.experimental.pallas import tpu as pltpu
from jax.sharding import PartitionSpec as P

OWNERS = 8
TILE = 128
ROWS = 64
SIDE = 32
SPAN = 64
PIECE = 16
score_scale = 0.08838834764831845
EXP2_SCALE = score_scale * math.log2(math.e)
MASKED = -1e30

ACROSS = (((1,), (1,)), ((), ()))


def same_core_groups(n):
    return [list(range(core, n, 2)) for core in range(2)]


def swap_cores(x, n):
    return lax.ppermute(x, "seq", [(i, i ^ 1) for i in range(n)])


def exchange(x, n):
    return lax.all_to_all(
        x, "seq", split_axis=0, concat_axis=0, axis_index_groups=same_core_groups(n), tiled=True
    )


def block_position(holder, me, n):
    return ((holder ^ me) & 1) * (n // 2) + (holder >> 1)


def grad_kernel(
    prompt_hbm,
    length_hbm,
    begin_hbm,
    holder_hbm,
    q_hbm,
    g_hbm,
    rk_hbm,
    rv_hbm,
    own_hbm,
    other_hbm,
    dq_hbm,
    drk_hbm,
    drv_hbm,
    own_term_hbm,
    other_term_hbm,
    prompt_ref,
    length_ref,
    begin_ref,
    holder_ref,
    place,
    q_all,
    g_all,
    rk_all,
    rv_all,
    dq_all,
    drk_all,
    drv_all,
    kv,
    term_ref,
    keys,
    values,
    keys_t,
    live_bias,
    causal_bias,
    turned,
    exps,
    dprobs,
    prob16,
    dscore16,
    kt,
    vt,
    sem_scalar,
    sem_resp,
    sem_q,
    sem_g,
    sem_dq,
    sem_drk,
    sem_drv,
    sem_kv,
    sem_term,
):
    n = holder_ref.shape[0]
    slots = prompt_ref.shape[0]
    rows, width = rk_all.shape
    slot_rows = rows // slots
    tiles = slot_rows // TILE
    prow = term_ref.shape[0] // n
    prompt_len = prow * OWNERS
    heads = q_all.shape[1] // width
    me = lax.axis_index("seq")

    scalar_copies = [
        pltpu.make_async_copy(src, dst, sem_scalar.at[i])
        for i, (src, dst) in enumerate(
            [
                (prompt_hbm, prompt_ref),
                (length_hbm, length_ref),
                (begin_hbm, begin_ref),
                (holder_hbm, holder_ref),
            ]
        )
    ]
    resp_copies = [
        pltpu.make_async_copy(rk_hbm, rk_all, sem_resp.at[0]),
        pltpu.make_async_copy(rv_hbm, rv_all, sem_resp.at[1]),
    ]

    def tile_rows(chunk):
        return pl.ds(pl.multiple_of(chunk * TILE, TILE), TILE)

    def q_copy(chunk):
        part = tile_rows(chunk)
        return pltpu.make_async_copy(q_hbm.at[part], q_all.at[part], sem_q.at[chunk])

    def g_copy(chunk):
        part = tile_rows(chunk)
        return pltpu.make_async_copy(g_hbm.at[part], g_all.at[part], sem_g.at[chunk])

    def dq_copy(chunk):
        part = tile_rows(chunk)
        return pltpu.make_async_copy(dq_all.at[part], dq_hbm.at[part], sem_dq.at[chunk])

    def slot_part(s):
        return pl.ds(pl.multiple_of(s * slot_rows, slot_rows), slot_rows)

    def drk_copy(s):
        return pltpu.make_async_copy(
            drk_all.at[slot_part(s)], drk_hbm.at[slot_part(s)], sem_drk.at[s]
        )

    def drv_copy(s):
        return pltpu.make_async_copy(
            drv_all.at[slot_part(s)], drv_hbm.at[slot_part(s)], sem_drv.at[s]
        )

    half_rows = term_ref.shape[0] // 2
    kv_copies = [
        pltpu.make_async_copy(src, kv.at[pl.ds(i * half_rows, half_rows)], sem_kv.at[i])
        for i, src in enumerate([own_hbm, other_hbm])
    ]
    term_copies = [
        pltpu.make_async_copy(term_ref.at[pl.ds(i * half_rows, half_rows)], dst, sem_term.at[i])
        for i, dst in enumerate([own_term_hbm, other_term_hbm])
    ]
    for copy in scalar_copies + kv_copies + resp_copies:
        copy.start()
    q_copy(0).start()
    g_copy(0).start()

    term_ref[...] = jnp.zeros_like(term_ref)
    causal_bias[...] = jnp.where(
        lax.broadcasted_iota(jnp.int32, causal_bias.shape, 0)
        <= (lax.broadcasted_iota(jnp.int32, causal_bias.shape, 1) & (SIDE - 1)),
        0.0,
        MASKED,
    )
    for copy in scalar_copies + kv_copies + resp_copies:
        copy.wait()

    for chunk in range(1, slots * tiles):
        q_copy(chunk).start()
        g_copy(chunk).start()

    @pl.loop(0, n)
    def _(j):
        place[holder_ref[j]] = j

    wide = 2 * TILE
    at_once = wide // SIDE
    steps_of = slot_rows // ROWS
    units = []
    for s in range(slots):
        order = range(steps_of) if s + 1 < slots else range(steps_of - 1, -1, -1)
        units += [(s, index) for index in order]

    def columns_of(u, side):
        return prompt_len + units[u][1] * ROWS + (side + 1) * SIDE

    def padded_columns(u):
        return -(-columns_of(u, 1) // TILE) * TILE

    def rows_of(u):
        s, index = units[u]
        first = s * slot_rows + index * ROWS
        return slice(first, first + ROWS)

    def chunk_of(u):
        return rows_of(u).start // TILE

    def chunks(u, side):
        columns = columns_of(u, side)
        return [(c, min(SPAN, columns - c)) for c in range(0, columns, SPAN)]

    def lanes_of(side):
        return slice(side * wide, (side + 1) * wide)

    def side_rows(u, side):
        first = rows_of(u).start + side * SIDE
        return slice(first, first + SIDE)

    def stacked(ref, u, side):
        part = side_rows(u, side)
        return jnp.concatenate([ref[part, h * width : (h + 1) * width] for h in range(at_once)], axis=0)

    def classes(x):
        return x.reshape(x.shape[0] // 8, 8, x.shape[1])

    def prepare(s):
        first_block = prompt_ref[s] * OWNERS
        for o in range(OWNERS):
            start = block_position(place[first_block + o], me, n) * prow
            source = pl.ds(pl.multiple_of(start, prow), prow)
            keys[s, o * prow : (o + 1) * prow, :] = kv[source, 0:width]
            values[s, o * prow : (o + 1) * prow, :] = kv[source, width : 2 * width]
        own = slice(s * slot_rows, (s + 1) * slot_rows)
        keys[s, prompt_len:, :] = rk_all[own, :]
        values[s, prompt_len:, :] = rv_all[own, :]
        yield
        keys_t[s] = keys[s].astype(jnp.float32).T.astype(jnp.bfloat16)
        yield
        column = lax.broadcasted_iota(jnp.int32, (slot_rows, TILE), 0)
        live_bias[s] = jnp.where(column >= begin_ref[s], 0.0, MASKED)
        kt[s] = jnp.zeros_like(kt[s])
        vt[s] = jnp.zeros_like(vt[s])
        yield

    def finish(s):
        own = slice(s * slot_rows, (s + 1) * slot_rows)
        prompt_kt = kt[s, :, 0:prompt_len].T * score_scale
        prompt_vt = vt[s, :, 0:prompt_len].T
        yield
        drk_all[own, :] = kt[s, :, prompt_len:].T * score_scale
        drv_all[own, :] = vt[s, :, prompt_len:].T
        yield
        first_block = prompt_ref[s] * OWNERS
        for o in range(OWNERS):
            start = block_position(place[first_block + o], me, n) * prow
            target = pl.ds(pl.multiple_of(start, prow), prow)
            block = slice(o * prow, (o + 1) * prow)
            term_ref[target, 0:width] += prompt_kt[block]
            term_ref[target, width : 2 * width] += prompt_vt[block]
        yield

    def head(u, side, out):
        s, index = units[u]
        columns, buf = columns_of(u, side), u % 2
        q2t, g2t = turned.at[u % 3, 0, :, lanes_of(side)], turned.at[u % 3, 1, :, lanes_of(side)]
        q2t[...] = stacked(q_all, u, side).T
        g2t[...] = stacked(g_all, u, side).T
        tops, totals, weights = [], [], []
        all_scores = jnp.dot(keys[s, 0:columns, :], q2t[...], preferred_element_type=jnp.float32)
        all_dprobs = jnp.dot(values[s, 0:columns, :], g2t[...], preferred_element_type=jnp.float32)
        for c, size in chunks(u, side):
            part = slice(c, c + size)
            block = all_scores[part]
            if c >= prompt_len:
                bias = live_bias[s, c - prompt_len : c - prompt_len + size, :]
                if c + size == columns:
                    last = bias[size - SIDE :] + causal_bias[...]
                    bias = last if size == SIDE else jnp.concatenate([bias[: size - SIDE], last], axis=0)
                block = block + jnp.concatenate([bias, bias], axis=1)
            block = classes(block)
            top = jnp.max(block, axis=0) * EXP2_SCALE
            e = jnp.exp2(block * EXP2_SCALE - top[None])
            exps[buf, side, part, :] = e.reshape(size, wide)
            yield
            d = all_dprobs[part]
            dprobs[buf, side, part, :] = d
            tops.append(top)
            totals.append(jnp.sum(e, axis=0))
            weights.append(jnp.sum(e * classes(d), axis=0))
            yield
        top = jnp.max(functools.reduce(jnp.maximum, tops), axis=0, keepdims=True)
        factors = [jnp.exp2(part - top) for part in tops]
        total = functools.reduce(jnp.add, [f * x for f, x in zip(factors, totals)])
        weighted = functools.reduce(jnp.add, [f * x for f, x in zip(factors, weights)])
        total = jnp.sum(total, axis=0, keepdims=True)
        weighted = jnp.sum(weighted, axis=0, keepdims=True)
        row = index * ROWS + side * SIDE + (lax.broadcasted_iota(jnp.int32, (1, wide), 1) & (SIDE - 1))
        live = (row >= begin_ref[s]) & (row < begin_ref[s] + length_ref[s])
        inverse = jnp.where(live, 1.0 / total, 0.0)
        out["delta"] = weighted * inverse
        out["factors"] = [f * inverse for f in factors]

    def tail(u, side, stats):
        buf, lanes = u % 2, lanes_of(side)
        delta = stats["delta"]
        for (c, size), factor in zip(chunks(u, side), stats["factors"]):
            for first in range(c, c + size, PIECE):
                part = slice(first, first + PIECE)
                p = (classes(exps[buf, side, part, :]) * factor[None]).reshape(PIECE, wide)
                prob16[buf, part, lanes] = p.astype(jnp.bfloat16)
                ds = p * (dprobs[buf, side, part, :] - delta)
                dscore16[buf, part, lanes] = ds.astype(jnp.bfloat16)
            yield
        pad = slice(columns_of(u, side), padded_columns(u))
        if pad.start < pad.stop:
            zero = jnp.zeros((pad.stop - pad.start, wide), jnp.bfloat16)
            prob16[buf, pad, lanes] = zero
            dscore16[buf, pad, lanes] = zero
            yield

    def flush_keys(u):
        s, columns = units[u][0], padded_columns(u)
        kt[s, :, 0:columns] += lax.dot_general(
            turned[u % 3, 0], dscore16[u % 2, 0:columns, :], ACROSS, preferred_element_type=jnp.float32
        )
        yield

    def flush_values(u):
        s, columns = units[u][0], padded_columns(u)
        vt[s, :, 0:columns] += lax.dot_general(
            turned[u % 3, 1], prob16[u % 2, 0:columns, :], ACROSS, preferred_element_type=jnp.float32
        )
        yield

    def flush_queries(u):
        s, columns = units[u][0], padded_columns(u)
        for side in range(2):
            ds = dscore16[u % 2, 0:columns, lanes_of(side)]
            dqt = jnp.dot(keys_t[s, :, 0:columns], ds, preferred_element_type=jnp.float32)
            dq = dqt.T * score_scale
            for h in range(at_once):
                lanes = slice(h * width, (h + 1) * width)
                dq_all[side_rows(u, side), lanes] = dq[h * SIDE : (h + 1) * SIDE]
            yield

    def together(*steps):
        steps = list(steps)
        while steps:
            for step in list(steps):
                if next(step, steps) is steps:
                    steps.remove(step)

    def wait_rows(u):
        if all(chunk_of(other) != chunk_of(u) for other in range(u)):
            q_copy(chunk_of(u)).wait()
            g_copy(chunk_of(u)).wait()

    def send_rows(u):
        if all(chunk_of(other) != chunk_of(u) for other in range(u + 1, len(units))):
            dq_copy(chunk_of(u)).start()

    count = len(units)
    per_slot = steps_of
    stats = [({}, {}) for _ in units]
    together(prepare(0))
    wait_rows(0)
    together(head(0, 0, stats[0][0]))
    for u in range(count):
        s = units[u][0]
        steps = [head(u, 1, stats[u][1]), tail(u, 0, stats[u][0])]
        if u >= 1:
            steps += [flush_keys(u - 1), flush_queries(u - 1)]
        if u % per_slot == 2 and s + 1 < slots:
            steps.append(prepare(s + 1))
        if u % per_slot == 1 and s >= 1:
            steps.append(finish(s - 1))
        together(*steps)
        if u >= 1:
            send_rows(u - 1)
        if u % per_slot == 1 and s >= 1:
            drk_copy(s - 1).start()
            drv_copy(s - 1).start()
        steps = []
        if u + 1 < count:
            wait_rows(u + 1)
            steps.append(head(u + 1, 0, stats[u + 1][0]))
        steps.append(tail(u, 1, stats[u][1]))
        if u >= 1:
            steps.append(flush_values(u - 1))
        together(*steps)
    together(flush_keys(count - 1), flush_values(count - 1), flush_queries(count - 1))
    send_rows(count - 1)
    together(finish(slots - 1))
    drk_copy(slots - 1).start()
    drv_copy(slots - 1).start()

    for copy in term_copies:
        copy.start()
    for copy in term_copies:
        copy.wait()
    for chunk in range(slots * tiles):
        dq_copy(chunk).wait()
    for s in range(slots):
        drk_copy(s).wait()
        drv_copy(s).wait()


def slot_grads(queries, resp_keys, resp_values, out_grad, own_kv, other_kv, prompts, lengths, begins, holders):
    slots = prompts.shape[0]
    rows, columns = queries.shape
    slot_rows, width = rows // slots, resp_keys.shape[1]
    n = holders.shape[0]
    prow = 2 * own_kv.shape[0] // n
    total = prow * OWNERS + slot_rows
    tiles = slot_rows // TILE
    hbm = pl.BlockSpec(memory_space=pltpu.HBM)
    f32, bf16 = jnp.float32, jnp.bfloat16
    return pl.pallas_call(
        grad_kernel,
        in_specs=[hbm] * 10,
        out_specs=[hbm] * 5,
        out_shape=[
            jax.ShapeDtypeStruct((rows, columns), f32),
            jax.ShapeDtypeStruct((rows, width), f32),
            jax.ShapeDtypeStruct((rows, width), f32),
            jax.ShapeDtypeStruct((n * prow // 2, 2 * width), f32),
            jax.ShapeDtypeStruct((n * prow // 2, 2 * width), f32),
        ],
        scratch_shapes=[
            pltpu.SMEM((slots,), jnp.int32),
            pltpu.SMEM((slots,), jnp.int32),
            pltpu.SMEM((slots,), jnp.int32),
            pltpu.SMEM((n,), jnp.int32),
            pltpu.SMEM((n,), jnp.int32),
            pltpu.VMEM((rows, columns), bf16),
            pltpu.VMEM((rows, columns), bf16),
            pltpu.VMEM((rows, width), bf16),
            pltpu.VMEM((rows, width), bf16),
            pltpu.VMEM((rows, columns), f32),
            pltpu.VMEM((rows, width), f32),
            pltpu.VMEM((rows, width), f32),
            pltpu.VMEM((n * prow, 2 * width), bf16),
            pltpu.VMEM((n * prow, 2 * width), f32),
            pltpu.VMEM((slots, total, width), bf16),
            pltpu.VMEM((slots, total, width), bf16),
            pltpu.VMEM((slots, width, total), bf16),
            pltpu.VMEM((slots, slot_rows, TILE), f32),
            pltpu.VMEM((SIDE, TILE), f32),
            pltpu.VMEM((3, 2, width, 4 * TILE), bf16),
            pltpu.VMEM((2, 2, total, 2 * TILE), f32),
            pltpu.VMEM((2, 2, total, 2 * TILE), f32),
            pltpu.VMEM((2, total, 4 * TILE), bf16),
            pltpu.VMEM((2, total, 4 * TILE), bf16),
            pltpu.VMEM((slots, width, total), f32),
            pltpu.VMEM((slots, width, total), f32),
            pltpu.SemaphoreType.DMA((4,)),
            pltpu.SemaphoreType.DMA((2,)),
            pltpu.SemaphoreType.DMA((slots * tiles,)),
            pltpu.SemaphoreType.DMA((slots * tiles,)),
            pltpu.SemaphoreType.DMA((slots * tiles,)),
            pltpu.SemaphoreType.DMA((slots,)),
            pltpu.SemaphoreType.DMA((slots,)),
            pltpu.SemaphoreType.DMA((2,)),
            pltpu.SemaphoreType.DMA((2,)),
        ],
        compiler_params=pltpu.CompilerParams(vmem_limit_bytes=60 * 1024 * 1024),
    )(prompts, lengths, begins, holders, queries, out_grad, resp_keys, resp_values, own_kv, other_kv)


def body(
    n,
    queries,
    resp_keys,
    resp_values,
    out_grad,
    prompt_keys,
    prompt_values,
    slot_prompt,
    slot_length,
    slot_begin,
    block_prompt,
):
    width = resp_keys.shape[1]
    prow = prompt_keys.shape[0]
    own = jnp.pad(prompt_keys, ((0, 0), (0, width))) + jnp.pad(prompt_values, ((0, 0), (width, 0)))
    own = jnp.broadcast_to(own[None], (n // 2, prow, 2 * width)).reshape(-1, 2 * width)
    own_kv = exchange(own, n)
    other_kv = swap_cores(own_kv, n)
    query_grad, key_grad, value_grad, own_term, other_term = slot_grads(
        queries, resp_keys, resp_values, out_grad, own_kv, other_kv,
        slot_prompt, slot_length, slot_begin, block_prompt,
    )
    parts = exchange(own_term + swap_cores(other_term, n), n)
    owned = jnp.sum(parts.reshape(n // 2, prow, 2 * width), axis=0)
    return query_grad, key_grad, value_grad, owned[:, :width], owned[:, width:]


def solution(mesh):
    n = mesh.shape["seq"]
    rows = P(("groups", "seq"), None)
    slots = P(("groups", "seq"))
    return jax.shard_map(
        functools.partial(body, n),
        mesh=mesh,
        in_specs=(rows,) * 6 + (slots,) * 3 + (P("groups"),),
        out_specs=(rows,) * 5,
        check_vma=False,
    )
```

```python
import functools
import math

import jax
import jax.numpy as jnp
from jax import lax
from jax.experimental import pallas as pl
from jax.experimental.pallas import tpu as pltpu
from jax.sharding import PartitionSpec as P

OWNERS = 8
TILE = 128
ROWS = 64
SIDE = 32
SPAN = 64
PIECE = 16
score_scale = 0.08838834764831845
EXP2_SCALE = score_scale * math.log2(math.e)
MASKED = -1e30

ACROSS = (((1,), (1,)), ((), ()))


def same_core_groups(n):
    return [list(range(core, n, 2)) for core in range(2)]


def swap_cores(x, n):
    return lax.ppermute(x, "seq", [(i, i ^ 1) for i in range(n)])


def exchange(x, n):
    return lax.all_to_all(
        x, "seq", split_axis=0, concat_axis=0, axis_index_groups=same_core_groups(n), tiled=True
    )


def block_position(holder, me, n):
    return ((holder ^ me) & 1) * (n // 2) + (holder >> 1)


def grad_kernel(
    prompt_hbm,
    length_hbm,
    begin_hbm,
    holder_hbm,
    q_hbm,
    g_hbm,
    rk_hbm,
    rv_hbm,
    own_hbm,
    other_hbm,
    dq_hbm,
    drk_hbm,
    drv_hbm,
    own_term_hbm,
    other_term_hbm,
    prompt_ref,
    length_ref,
    begin_ref,
    holder_ref,
    place,
    q_all,
    g_all,
    rk_all,
    rv_all,
    dq_all,
    drk_all,
    drv_all,
    kv,
    term_ref,
    keys,
    values,
    keys_t,
    live_bias,
    causal_bias,
    turned,
    exps,
    dprobs,
    prob16,
    dscore16,
    kt,
    vt,
    sem_scalar,
    sem_resp,
    sem_q,
    sem_g,
    sem_dq,
    sem_drk,
    sem_drv,
    sem_kv,
    sem_term,
):
    n = holder_ref.shape[0]
    slots = prompt_ref.shape[0]
    rows, width = rk_all.shape
    slot_rows = rows // slots
    tiles = slot_rows // TILE
    prow = term_ref.shape[0] // n
    prompt_len = prow * OWNERS
    heads = q_all.shape[1] // width
    me = lax.axis_index("seq")

    scalar_copies = [
        pltpu.make_async_copy(src, dst, sem_scalar.at[i])
        for i, (src, dst) in enumerate(
            [
                (prompt_hbm, prompt_ref),
                (length_hbm, length_ref),
                (begin_hbm, begin_ref),
                (holder_hbm, holder_ref),
            ]
        )
    ]
    resp_copies = [
        pltpu.make_async_copy(rk_hbm, rk_all, sem_resp.at[0]),
        pltpu.make_async_copy(rv_hbm, rv_all, sem_resp.at[1]),
    ]

    def tile_rows(chunk):
        return pl.ds(pl.multiple_of(chunk * TILE, TILE), TILE)

    def q_copy(chunk):
        part = tile_rows(chunk)
        return pltpu.make_async_copy(q_hbm.at[part], q_all.at[part], sem_q.at[chunk])

    def g_copy(chunk):
        part = tile_rows(chunk)
        return pltpu.make_async_copy(g_hbm.at[part], g_all.at[part], sem_g.at[chunk])

    def dq_copy(chunk):
        part = tile_rows(chunk)
        return pltpu.make_async_copy(dq_all.at[part], dq_hbm.at[part], sem_dq.at[chunk])

    def slot_part(s):
        return pl.ds(pl.multiple_of(s * slot_rows, slot_rows), slot_rows)

    def drk_copy(s):
        return pltpu.make_async_copy(
            drk_all.at[slot_part(s)], drk_hbm.at[slot_part(s)], sem_drk.at[s]
        )

    def drv_copy(s):
        return pltpu.make_async_copy(
            drv_all.at[slot_part(s)], drv_hbm.at[slot_part(s)], sem_drv.at[s]
        )

    half_rows = term_ref.shape[0] // 2
    kv_copies = [
        pltpu.make_async_copy(src, kv.at[pl.ds(i * half_rows, half_rows)], sem_kv.at[i])
        for i, src in enumerate([own_hbm, other_hbm])
    ]
    term_copies = [
        pltpu.make_async_copy(term_ref.at[pl.ds(i * half_rows, half_rows)], dst, sem_term.at[i])
        for i, dst in enumerate([own_term_hbm, other_term_hbm])
    ]
    for copy in scalar_copies + kv_copies + resp_copies:
        copy.start()
    q_copy(0).start()
    g_copy(0).start()

    term_ref[...] = jnp.zeros_like(term_ref)
    causal_bias[...] = jnp.where(
        lax.broadcasted_iota(jnp.int32, causal_bias.shape, 0)
        <= (lax.broadcasted_iota(jnp.int32, causal_bias.shape, 1) & (SIDE - 1)),
        0.0,
        MASKED,
    )
    for copy in scalar_copies + kv_copies + resp_copies:
        copy.wait()

    for chunk in range(1, slots * tiles):
        q_copy(chunk).start()
        g_copy(chunk).start()

    @pl.loop(0, n)
    def _(j):
        place[holder_ref[j]] = j

    wide = 2 * TILE
    at_once = wide // SIDE
    steps_of = slot_rows // ROWS
    units = []
    for s in range(slots):
        order = range(steps_of) if s + 1 < slots else range(steps_of - 1, -1, -1)
        units += [(s, index) for index in order]

    def columns_of(u, side):
        return prompt_len + units[u][1] * ROWS + (side + 1) * SIDE

    def padded_columns(u):
        return -(-columns_of(u, 1) // TILE) * TILE

    def rows_of(u):
        s, index = units[u]
        first = s * slot_rows + index * ROWS
        return slice(first, first + ROWS)

    def chunk_of(u):
        return rows_of(u).start // TILE

    def chunks(u, side):
        columns = columns_of(u, side)
        return [(c, min(SPAN, columns - c)) for c in range(0, columns, SPAN)]

    def lanes_of(side):
        return slice(side * wide, (side + 1) * wide)

    def side_rows(u, side):
        first = rows_of(u).start + side * SIDE
        return slice(first, first + SIDE)

    def stacked(ref, u, side):
        part = side_rows(u, side)
        return jnp.concatenate([ref[part, h * width : (h + 1) * width] for h in range(at_once)], axis=0)

    def classes(x):
        return x.reshape(x.shape[0] // 8, 8, x.shape[1])

    def prepare(s):
        first_block = prompt_ref[s] * OWNERS
        for o in range(OWNERS):
            start = block_position(place[first_block + o], me, n) * prow
            source = pl.ds(pl.multiple_of(start, prow), prow)
            keys[s, o * prow : (o + 1) * prow, :] = kv[source, 0:width]
            values[s, o * prow : (o + 1) * prow, :] = kv[source, width : 2 * width]
        own = slice(s * slot_rows, (s + 1) * slot_rows)
        keys[s, prompt_len:, :] = rk_all[own, :]
        values[s, prompt_len:, :] = rv_all[own, :]
        yield
        keys_t[s] = keys[s].astype(jnp.float32).T.astype(jnp.bfloat16)
        yield
        column = lax.broadcasted_iota(jnp.int32, (slot_rows, TILE), 0)
        live_bias[s] = jnp.where(column >= begin_ref[s], 0.0, MASKED)
        kt[s] = jnp.zeros_like(kt[s])
        vt[s] = jnp.zeros_like(vt[s])
        yield

    def finish(s):
        own = slice(s * slot_rows, (s + 1) * slot_rows)
        prompt_kt = kt[s, :, 0:prompt_len].T * score_scale
        prompt_vt = vt[s, :, 0:prompt_len].T
        yield
        drk_all[own, :] = kt[s, :, prompt_len:].T * score_scale
        drv_all[own, :] = vt[s, :, prompt_len:].T
        yield
        first_block = prompt_ref[s] * OWNERS
        for o in range(OWNERS):
            start = block_position(place[first_block + o], me, n) * prow
            target = pl.ds(pl.multiple_of(start, prow), prow)
            block = slice(o * prow, (o + 1) * prow)
            term_ref[target, 0:width] += prompt_kt[block]
            term_ref[target, width : 2 * width] += prompt_vt[block]
        yield

    def head(u, side, out):
        s, index = units[u]
        columns, buf = columns_of(u, side), u % 2
        q2t, g2t = turned.at[u % 3, 0, :, lanes_of(side)], turned.at[u % 3, 1, :, lanes_of(side)]
        q2t[...] = stacked(q_all, u, side).T
        g2t[...] = stacked(g_all, u, side).T
        tops, totals, weights = [], [], []
        all_scores = jnp.dot(keys[s, 0:columns, :], q2t[...], preferred_element_type=jnp.float32)
        all_dprobs = jnp.dot(values[s, 0:columns, :], g2t[...], preferred_element_type=jnp.float32)
        for c, size in chunks(u, side):
            part = slice(c, c + size)
            block = all_scores[part]
            if c >= prompt_len:
                bias = live_bias[s, c - prompt_len : c - prompt_len + size, :]
                if c + size == columns:
                    last = bias[size - SIDE :] + causal_bias[...]
                    bias = last if size == SIDE else jnp.concatenate([bias[: size - SIDE], last], axis=0)
                block = block + jnp.concatenate([bias, bias], axis=1)
            block = classes(block)
            top = jnp.max(block, axis=0) * EXP2_SCALE
            e = jnp.exp2(block * EXP2_SCALE - top[None])
            exps[buf, side, part, :] = e.reshape(size, wide)
            yield
            d = all_dprobs[part]
            dprobs[buf, side, part, :] = d
            tops.append(top)
            totals.append(jnp.sum(e, axis=0))
            weights.append(jnp.sum(e * classes(d), axis=0))
            yield
        top = jnp.max(functools.reduce(jnp.maximum, tops), axis=0, keepdims=True)
        factors = [jnp.exp2(part - top) for part in tops]
        total = functools.reduce(jnp.add, [f * x for f, x in zip(factors, totals)])
        weighted = functools.reduce(jnp.add, [f * x for f, x in zip(factors, weights)])
        total = jnp.sum(total, axis=0, keepdims=True)
        weighted = jnp.sum(weighted, axis=0, keepdims=True)
        row = index * ROWS + side * SIDE + (lax.broadcasted_iota(jnp.int32, (1, wide), 1) & (SIDE - 1))
        live = (row >= begin_ref[s]) & (row < begin_ref[s] + length_ref[s])
        inverse = jnp.where(live, 1.0 / total, 0.0)
        out["delta"] = weighted * inverse
        out["factors"] = [f * inverse for f in factors]

    def tail(u, side, stats):
        buf, lanes = u % 2, lanes_of(side)
        delta = stats["delta"]
        for (c, size), factor in zip(chunks(u, side), stats["factors"]):
            for first in range(c, c + size, PIECE):
                part = slice(first, first + PIECE)
                p = (classes(exps[buf, side, part, :]) * factor[None]).reshape(PIECE, wide)
                prob16[buf, part, lanes] = p.astype(jnp.bfloat16)
                ds = p * (dprobs[buf, side, part, :] - delta)
                dscore16[buf, part, lanes] = ds.astype(jnp.bfloat16)
            yield
        pad = slice(columns_of(u, side), padded_columns(u))
        if pad.start < pad.stop:
            zero = jnp.zeros((pad.stop - pad.start, wide), jnp.bfloat16)
            prob16[buf, pad, lanes] = zero
            dscore16[buf, pad, lanes] = zero
            yield

    def flush_keys(u):
        s, columns = units[u][0], padded_columns(u)
        kt[s, :, 0:columns] += lax.dot_general(
            turned[u % 3, 0], dscore16[u % 2, 0:columns, :], ACROSS, preferred_element_type=jnp.float32
        )
        yield

    def flush_values(u):
        s, columns = units[u][0], padded_columns(u)
        vt[s, :, 0:columns] += lax.dot_general(
            turned[u % 3, 1], prob16[u % 2, 0:columns, :], ACROSS, preferred_element_type=jnp.float32
        )
        yield

    def flush_queries(u, side):
        s, columns = units[u][0], padded_columns(u)
        ds = dscore16[u % 2, 0:columns, lanes_of(side)]
        dqt = jnp.dot(keys_t[s, :, 0:columns], ds, preferred_element_type=jnp.float32)
        dq = dqt.T * score_scale
        for h in range(at_once):
            lanes = slice(h * width, (h + 1) * width)
            dq_all[side_rows(u, side), lanes] = dq[h * SIDE : (h + 1) * SIDE]
        yield

    def together(*steps):
        steps = list(steps)
        while steps:
            for step in list(steps):
                if next(step, steps) is steps:
                    steps.remove(step)

    def wait_rows(u):
        if all(chunk_of(other) != chunk_of(u) for other in range(u)):
            q_copy(chunk_of(u)).wait()
            g_copy(chunk_of(u)).wait()

    def send_rows(u):
        if all(chunk_of(other) != chunk_of(u) for other in range(u + 1, len(units))):
            dq_copy(chunk_of(u)).start()

    count = len(units)
    per_slot = steps_of
    stats = [({}, {}) for _ in units]
    wait_rows(0)
    together(prepare(0))
    together(head(0, 0, stats[0][0]))
    for u in range(count):
        s = units[u][0]
        steps = [head(u, 1, stats[u][1]), tail(u, 0, stats[u][0])]
        if u >= 1:
            steps += [flush_keys(u - 1), flush_queries(u - 1, 0)]
        if u % per_slot == 2 and s + 1 < slots:
            steps.append(prepare(s + 1))
        if u % per_slot == 1 and s >= 1:
            steps.append(finish(s - 1))
        together(*steps)
        if u % per_slot == 1 and s >= 1:
            drk_copy(s - 1).start()
            drv_copy(s - 1).start()
        steps = []
        if u + 1 < count:
            wait_rows(u + 1)
            steps.append(head(u + 1, 0, stats[u + 1][0]))
        steps.append(tail(u, 1, stats[u][1]))
        if u >= 1:
            steps += [flush_values(u - 1), flush_queries(u - 1, 1)]
        together(*steps)
        if u >= 1:
            send_rows(u - 1)
    together(flush_keys(count - 1), flush_values(count - 1))
    together(finish(slots - 1), flush_queries(count - 1, 0), flush_queries(count - 1, 1))
    send_rows(count - 1)
    drk_copy(slots - 1).start()
    drv_copy(slots - 1).start()

    for copy in term_copies:
        copy.start()
    for copy in term_copies:
        copy.wait()
    for chunk in range(slots * tiles):
        dq_copy(chunk).wait()
    for s in range(slots):
        drk_copy(s).wait()
        drv_copy(s).wait()


def slot_grads(queries, resp_keys, resp_values, out_grad, own_kv, other_kv, prompts, lengths, begins, holders):
    slots = prompts.shape[0]
    rows, columns = queries.shape
    slot_rows, width = rows // slots, resp_keys.shape[1]
    n = holders.shape[0]
    prow = 2 * own_kv.shape[0] // n
    total = prow * OWNERS + slot_rows
    tiles = slot_rows // TILE
    hbm = pl.BlockSpec(memory_space=pltpu.HBM)
    f32, bf16 = jnp.float32, jnp.bfloat16
    return pl.pallas_call(
        grad_kernel,
        in_specs=[hbm] * 10,
        out_specs=[hbm] * 5,
        out_shape=[
            jax.ShapeDtypeStruct((rows, columns), f32),
            jax.ShapeDtypeStruct((rows, width), f32),
            jax.ShapeDtypeStruct((rows, width), f32),
            jax.ShapeDtypeStruct((n * prow // 2, 2 * width), f32),
            jax.ShapeDtypeStruct((n * prow // 2, 2 * width), f32),
        ],
        scratch_shapes=[
            pltpu.SMEM((slots,), jnp.int32),
            pltpu.SMEM((slots,), jnp.int32),
            pltpu.SMEM((slots,), jnp.int32),
            pltpu.SMEM((n,), jnp.int32),
            pltpu.SMEM((n,), jnp.int32),
            pltpu.VMEM((rows, columns), bf16),
            pltpu.VMEM((rows, columns), bf16),
            pltpu.VMEM((rows, width), bf16),
            pltpu.VMEM((rows, width), bf16),
            pltpu.VMEM((rows, columns), f32),
            pltpu.VMEM((rows, width), f32),
            pltpu.VMEM((rows, width), f32),
            pltpu.VMEM((n * prow, 2 * width), bf16),
            pltpu.VMEM((n * prow, 2 * width), f32),
            pltpu.VMEM((slots, total, width), bf16),
            pltpu.VMEM((slots, total, width), bf16),
            pltpu.VMEM((slots, width, total), bf16),
            pltpu.VMEM((slots, slot_rows, TILE), f32),
            pltpu.VMEM((SIDE, TILE), f32),
            pltpu.VMEM((3, 2, width, 4 * TILE), bf16),
            pltpu.VMEM((2, 2, total, 2 * TILE), f32),
            pltpu.VMEM((2, 2, total, 2 * TILE), f32),
            pltpu.VMEM((2, total, 4 * TILE), bf16),
            pltpu.VMEM((2, total, 4 * TILE), bf16),
            pltpu.VMEM((slots, width, total), f32),
            pltpu.VMEM((slots, width, total), f32),
            pltpu.SemaphoreType.DMA((4,)),
            pltpu.SemaphoreType.DMA((2,)),
            pltpu.SemaphoreType.DMA((slots * tiles,)),
            pltpu.SemaphoreType.DMA((slots * tiles,)),
            pltpu.SemaphoreType.DMA((slots * tiles,)),
            pltpu.SemaphoreType.DMA((slots,)),
            pltpu.SemaphoreType.DMA((slots,)),
            pltpu.SemaphoreType.DMA((2,)),
            pltpu.SemaphoreType.DMA((2,)),
        ],
        compiler_params=pltpu.CompilerParams(vmem_limit_bytes=60 * 1024 * 1024),
    )(prompts, lengths, begins, holders, queries, out_grad, resp_keys, resp_values, own_kv, other_kv)


def body(
    n,
    queries,
    resp_keys,
    resp_values,
    out_grad,
    prompt_keys,
    prompt_values,
    slot_prompt,
    slot_length,
    slot_begin,
    block_prompt,
):
    width = resp_keys.shape[1]
    prow = prompt_keys.shape[0]
    own = jnp.pad(prompt_keys, ((0, 0), (0, width))) + jnp.pad(prompt_values, ((0, 0), (width, 0)))
    own = jnp.broadcast_to(own[None], (n // 2, prow, 2 * width)).reshape(-1, 2 * width)
    own_kv = exchange(own, n)
    other_kv = swap_cores(own_kv, n)
    query_grad, key_grad, value_grad, own_term, other_term = slot_grads(
        queries, resp_keys, resp_values, out_grad, own_kv, other_kv,
        slot_prompt, slot_length, slot_begin, block_prompt,
    )
    parts = exchange(own_term + swap_cores(other_term, n), n)
    owned = jnp.sum(parts.reshape(n // 2, prow, 2 * width), axis=0)
    return query_grad, key_grad, value_grad, owned[:, :width], owned[:, width:]


def solution(mesh):
    n = mesh.shape["seq"]
    rows = P(("groups", "seq"), None)
    slots = P(("groups", "seq"))
    return jax.shard_map(
        functools.partial(body, n),
        mesh=mesh,
        in_specs=(rows,) * 6 + (slots,) * 3 + (P("groups"),),
        out_specs=(rows,) * 5,
        check_vma=False,
    )
```
